128 devices in a mesh: ctx: 16 (over y, x_hi, core), tp: 8 (over x_lo, z).
Axes of the slice: x: 4 (x_hi: 2, x_lo: 2; x = x_hi * 2 + x_lo), y: 4, z: 4, core: 2. Of those that a mesh axis runs over, the one named last changes fastest.
Arguments:
- tokens: bfloat16 [8192, 4096], P('ctx'), may hold values from -6 to 6
- in_weight: bfloat16 [4096, 3, 4096], P('ctx', None, 'tp'), may hold values from -0.09375 to 0.09375
- short_taps: float32 [3, 3, 4096], P(None, None, 'tp'), may hold values from -3 to 3
- long_filter: float32 [4096, 8192], P(('tp', 'ctx'))
- skip_bias: float32 [4096], P(('tp', 'ctx')), may hold values from -4 to 4
- out_grad: bfloat16 [4096, 8192], P('tp', 'ctx'), may hold values from -1.5 to 1.5
Outputs:
- input_grad: bfloat16 [8192, 4096], P(('ctx', 'tp'))
- weight_grad: bfloat16 [4096, 3, 4096], P('ctx', None, 'tp')
- filter_grad: float32 [4096, 8192], P(('tp', 'ctx'))
The draws below stay inside these ranges and needn't reach their ends.
All inputs are finite; a program needn't handle non-finite values.
Results may differ from the reference program's by a relative error of at most 0.019.
Values may be sent and summed in bfloat16 or wider, within the bound.
A program may use at most 128 MiB of HBM per device.

```python
import jax
import jax.numpy as jnp
from jax import lax

D = 4096
SEQ = 8192
N_CTX = 16


def draw_long_filter(key, part):
    key = jax.random.fold_in(key, 11)
    key_rough = jax.random.fold_in(key, 1)
    key_rate = jax.random.fold_in(key, 2)
    rate = jax.random.uniform(key_rate, (D, 1), jnp.float32, 0.0, 3.0)
    position = jnp.arange(SEQ, dtype=jnp.float32)[None, :] / SEQ
    envelope = jnp.exp(-rate * position) * (2.0 / SEQ) ** 0.5
    rough = jax.random.truncated_normal(key_rough, -4.0, 4.0, (D, SEQ), jnp.float32)
    return rough * envelope


def block_scale(stream_key, extent, cuts, low, top_value):
    def one(dim, parts):
        draws = jax.random.uniform(jax.random.fold_in(jax.random.fold_in(stream_key, 6), dim), (parts,), jnp.float32, low / len(cuts), top_value / len(cuts))
        return jnp.repeat(jnp.exp(draws), extent[dim] // parts).reshape((-1,) + (1,) * (len(extent) - dim - 1))

    gain = one(*cuts[0])
    for cut in cuts[1:]:
        gain = gain * one(*cut)
    return gain


def scatter_about(own_key, extent, scale, bound, cuts=(), kind=jnp.bfloat16):
    loudness = block_scale(own_key, extent, cuts, -0.22, 0.18) if cuts else 1.0
    result = jax.random.normal(own_key, extent, jnp.float32) * scale * loudness
    return jnp.minimum(jnp.maximum(result, -bound), bound).astype(kind)


def setup_inputs(seed: int = 0) -> dict:
    key_list = jax.random.split(jax.random.key(seed), 7)
    tokens = scatter_about(key_list[0], (SEQ, D), 1.0, 6.0, ((0, 16),))
    in_weight = scatter_about(key_list[1], (D, 3, D), D ** -0.5, 0.09375, ((0, 16), (2, 8)))
    short_taps = scatter_about(key_list[2], (3, 3, D), 0.5, 3.0, ((2, 8),), jnp.float32)
    long_filter = draw_long_filter(jax.random.fold_in(key_list[6], 71), 0)
    skip_bias = scatter_about(key_list[4], (D,), 1.0, 4.0, ((0, 128),), jnp.float32)
    out_grad = scatter_about(key_list[5], (D, SEQ), 0.25, 1.5, ((0, 8), (1, 16)))
    return dict(tokens=tokens, in_weight=in_weight, short_taps=short_taps, long_filter=long_filter, skip_bias=skip_bias, out_grad=out_grad)


def causal_taps(values, taps):
    one = jnp.pad(values, ((1, 0), (0, 0), (0, 0)))[:-1]
    two = jnp.pad(values, ((2, 0), (0, 0), (0, 0)))[:-2]
    return taps[0] * values + taps[1] * one + taps[2] * two


def ahead_taps(values, taps):
    one = jnp.pad(values, ((0, 1), (0, 0), (0, 0)))[1:]
    two = jnp.pad(values, ((0, 2), (0, 0), (0, 0)))[2:]
    return taps[0] * values + taps[1] * one + taps[2] * two


def reference(tokens, in_weight, short_taps, long_filter, skip_bias, out_grad):
    length = tokens.shape[0]
    projected = jnp.dot(tokens, in_weight.reshape(D, 3 * D), preferred_element_type=jnp.float32)
    projected = projected.reshape(length, 3, D).astype(jnp.bfloat16)
    filtered = causal_taps(projected.astype(jnp.float32), short_taps).astype(jnp.bfloat16)
    streams = filtered.astype(jnp.float32)
    query = streams[:, 0, :].T
    key_part = streams[:, 1, :].T
    value_part = streams[:, 2, :].T
    cotangent = out_grad.astype(jnp.float32)
    products = key_part * value_part
    weighted = cotangent * query
    size = 2 * length
    spec_prod = jnp.fft.rfft(products, n=size, axis=-1)
    spec_filter = jnp.fft.rfft(long_filter, n=size, axis=-1)
    spec_weighted = jnp.fft.rfft(weighted, n=size, axis=-1)
    conv = jnp.fft.irfft(spec_prod * spec_filter, n=size, axis=-1)[:, :length]
    back_conv = jnp.fft.irfft(jnp.conj(spec_filter) * spec_weighted, n=size, axis=-1)[:, :length]
    filter_grad = jnp.fft.irfft(jnp.conj(spec_prod) * spec_weighted, n=size, axis=-1)[:, :length]
    bias = skip_bias[:, None]
    query_grad = cotangent * (conv + bias * products)
    prod_grad = back_conv + bias * weighted
    conv_grad = jnp.stack([query_grad, prod_grad * value_part, prod_grad * key_part], axis=0)
    conv_grad = jnp.transpose(conv_grad, (2, 0, 1)).astype(jnp.bfloat16)
    proj_grad = ahead_taps(conv_grad.astype(jnp.float32), short_taps).astype(jnp.bfloat16)
    input_grad = jnp.dot(proj_grad.reshape(length, 3 * D), in_weight.reshape(D, 3 * D).T,
                         preferred_element_type=jnp.float32).astype(jnp.bfloat16)
    block_tokens = tokens.reshape(N_CTX, length // N_CTX, D)
    block_grads = proj_grad.reshape(N_CTX, length // N_CTX, 3 * D)

    def add_block(total, pair):
        partial_sum = jnp.dot(pair[0].T, pair[1], preferred_element_type=jnp.float32)
        rounded = lax.optimization_barrier(partial_sum.astype(jnp.bfloat16))
        return total + rounded.astype(jnp.float32), None

    total, unused = lax.scan(add_block, jnp.zeros((D, 3 * D), jnp.float32), (block_tokens, block_grads))
    weight_grad = total.reshape(D, 3, D).astype(jnp.bfloat16)
    return input_grad, weight_grad, filter_grad
```

```python
import functools
import math

import jax
import jax.numpy as jnp
import numpy as np
from jax import lax
from jax.experimental import pallas as pl
from jax.experimental.pallas import tpu as pltpu
from jax.sharding import PartitionSpec as P

MESH = pl.DeviceIdType.MESH
ANY = pl.BlockSpec(memory_space=pl.ANY)
IN_VMEM = pl.BlockSpec(memory_space=pltpu.VMEM)
N_CTX = 16
LANES = 128
BLOCKS = 64
GROUP = 4


def shifted(value, axis, steps):
    count = lax.axis_size(axis)
    first, last = (max(0, -steps), min(count, count - steps))
    return lax.ppermute(value, axis, [(source, source + steps) for source in range(first, last)])


def exchange_kernel(pick, place, src, out, send_sem, recv_sem, local_sem):
    me = lax.axis_index("ctx")
    barrier = pltpu.get_barrier_semaphore()
    for step in range(1, N_CTX):
        pl.semaphore_signal(
            barrier, inc=1, device_id={"ctx": lax.rem(me + step, N_CTX)}, device_id_type=MESH
        )
    pl.semaphore_wait(barrier, N_CTX - 1)
    copies = []
    for step in range(1, N_CTX):
        peer = lax.rem(me + step, N_CTX)
        copy = pltpu.make_async_remote_copy(
            src_ref=pick(src, peer),
            dst_ref=place(out, me),
            send_sem=send_sem.at[step - 1],
            recv_sem=recv_sem.at[step - 1],
            device_id={"ctx": peer},
            device_id_type=MESH,
        )
        copy.start()
        copies.append(copy)
    own = pltpu.make_async_copy(pick(src, me), place(out, me), local_sem)
    own.start()
    own.wait()
    for copy in copies:
        copy.wait()


def rows_of(ref, index):
    return ref.at[:, pl.ds(pl.multiple_of(index * 32, 32), 32), :]


def positions_of(ref, index):
    return ref.at[:, :, pl.ds(pl.multiple_of(index * 512, 512), 512)]


def exchange(value, shape, pick, place, collective_id):
    return pl.pallas_call(
        functools.partial(exchange_kernel, pick, place),
        out_shape=jax.ShapeDtypeStruct(shape, value.dtype),
        in_specs=[ANY],
        out_specs=ANY,
        scratch_shapes=[
            pltpu.SemaphoreType.DMA((N_CTX - 1,)),
            pltpu.SemaphoreType.DMA((N_CTX - 1,)),
            pltpu.SemaphoreType.DMA,
        ],
        compiler_params=pltpu.CompilerParams(collective_id=collective_id, has_side_effects=True),
    )(value)


def tables():
    size = 2 * BLOCKS * LANES
    half = np.arange(BLOCKS) + 0.5
    n = np.arange(BLOCKS)
    m = np.arange(LANES)
    theta = 2 * np.pi * half[:, None] * n[None, :] / LANES
    phi = 2 * np.pi * half[:, None] * m[None, :] / size
    psi = 2 * np.pi * (m[:, None] * m[None, :] % LANES) / LANES
    first = np.concatenate([np.cos(theta), -np.sin(theta)], axis=0)
    second = np.block([[np.cos(psi), -np.sin(psi)], [np.sin(psi), np.cos(psi)]])
    second_back = np.block([[np.cos(psi), np.sin(psi)], [-np.sin(psi), np.cos(psi)]])
    first_back = np.concatenate([np.cos(theta).T, -np.sin(theta).T], axis=1)
    low = lambda value: jnp.asarray(value, jnp.bfloat16)
    turn = jnp.asarray(np.stack([np.cos(phi), np.sin(phi)]), jnp.float32)
    return low(first), low(second), low(second_back), low(first_back), turn


def convolve_kernel(
    arrived, filters, bias, first, second, second_back, first_back, turn, grad, result, held
):
    f32, bf16 = jnp.float32, jnp.bfloat16
    size = 2 * BLOCKS * LANES
    for n in range(BLOCKS):
        at = slice(n * LANES, (n + 1) * LANES)
        rows = slice(n * 32, (n + 1) * 32)
        held[0, rows, :] = arrived[0, :, at].astype(f32)
        held[1, rows, :] = arrived[1, :, at].astype(f32)
        held[2, rows, :] = filters[:, at]

    def dot(a, b):
        return jnp.dot(a, b, preferred_element_type=f32)

    def some(step, carry):
        cos, sin = turn[0], turn[1]
        pairs = [(j, s) for j in range(GROUP) for s in range(3)]
        signals = [
            held[s, pl.ds(step * GROUP + j, BLOCKS, stride=32), :].astype(bf16) for j, s in pairs
        ]
        mixed = dot(first[...], jnp.concatenate(signals, axis=1))
        turned = []
        for index in range(len(pairs)):
            at = slice(index * LANES, (index + 1) * LANES)
            re, im = mixed[:BLOCKS, at], mixed[BLOCKS:, at]
            turned.append(
                jnp.concatenate([re * cos + im * sin, im * cos - re * sin], axis=1).astype(bf16)
            )
        spectra = dot(jnp.concatenate(turned, axis=0), second[...])
        joined = []
        for j in range(GROUP):
            parts = []
            for s in range(3):
                rows = slice((3 * j + s) * BLOCKS, (3 * j + s + 1) * BLOCKS)
                parts.append((spectra[rows, :LANES], spectra[rows, LANES:]))
            (pr, pi), (wr, wi), (hr, hi) = parts
            joined.append(jnp.concatenate([pr * hr - pi * hi, pr * hi + pi * hr], axis=1))
            joined.append(jnp.concatenate([hr * wr + hi * wi, hr * wi - hi * wr], axis=1))
            joined.append(jnp.concatenate([pr * wr + pi * wi, pr * wi - pi * wr], axis=1))
        back = dot(jnp.concatenate(joined, axis=0).astype(bf16), second_back[...])
        cos, sin = cos * (2.0 / size), sin * (2.0 / size)
        unturned = []
        for index in range(len(pairs)):
            rows = slice(index * BLOCKS, (index + 1) * BLOCKS)
            re, im = back[rows, :LANES], back[rows, LANES:]
            unturned.append(
                jnp.concatenate([re * cos - im * sin, im * cos + re * sin], axis=0).astype(bf16)
            )
        final = dot(first_back[...], jnp.concatenate(unturned, axis=1))
        for index, (j, s) in enumerate(pairs):
            held[s, pl.ds(step * GROUP + j, BLOCKS, stride=32), :] = final[
                :, index * LANES : (index + 1) * LANES
            ]
        return carry

    lax.fori_loop(0, 32 // GROUP, some, 0)
    gain = bias[...]
    for n in range(BLOCKS):
        at = slice(n * LANES, (n + 1) * LANES)
        rows = slice(n * 32, (n + 1) * 32)
        for s in range(2):
            result[s, :, at] = (held[s, rows, :] + gain * arrived[s, :, at].astype(f32)).astype(bf16)
        grad[:, at] = held[2, rows, :]


def convolve(arrived, long_filter, skip_bias):
    bias = jnp.broadcast_to(skip_bias[:, None], (32, LANES))
    return pl.pallas_call(
        convolve_kernel,
        out_shape=(
            jax.ShapeDtypeStruct((32, BLOCKS * LANES), jnp.float32),
            jax.ShapeDtypeStruct((2, 32, BLOCKS * LANES), jnp.bfloat16),
        ),
        in_specs=[IN_VMEM] * 8,
        out_specs=(IN_VMEM, IN_VMEM),
        scratch_shapes=[pltpu.VMEM((3, 32 * BLOCKS, LANES), jnp.float32)],
        compiler_params=pltpu.CompilerParams(vmem_limit_bytes=48 * 1024 * 1024),
    )(arrived, long_filter, bias, *tables())


def short_forward(values, before, taps):
    extended = jnp.concatenate([before, values], axis=2).astype(jnp.float32)
    return (
        taps[0][:, :, None] * extended[:, :, 2:]
        + taps[1][:, :, None] * extended[:, :, 1:-1]
        + taps[2][:, :, None] * extended[:, :, :-2]
    ).astype(jnp.bfloat16)


def short_backward(values, after, taps):
    extended = jnp.concatenate([values, after], axis=2).astype(jnp.float32)
    return (
        taps[0][:, :, None] * extended[:, :, :-2]
        + taps[1][:, :, None] * extended[:, :, 1:-1]
        + taps[2][:, :, None] * extended[:, :, 2:]
    ).astype(jnp.bfloat16)


def on_device(tokens, in_weight, short_taps, long_filter, skip_bias, out_grad):
    f32, bf16 = jnp.float32, jnp.bfloat16
    whole_weight = lax.all_gather(in_weight, "ctx", axis=0, tiled=True)
    projected = jnp.einsum("tr,rpc->pct", tokens, whole_weight, preferred_element_type=f32)
    projected = projected.astype(bf16)
    before = shifted(projected[:, :, -2:], "ctx", 1)
    streams = short_forward(projected, before, short_taps).astype(f32)
    cotangent = out_grad.astype(f32)
    outgoing = jnp.stack([streams[1] * streams[2], cotangent * streams[0]]).astype(bf16)
    arrived = exchange(outgoing, (2, 32, 8192), rows_of, positions_of, 1)
    filter_grad, result = convolve(arrived, long_filter, skip_bias)
    returned = exchange(result, (2, 512, 512), positions_of, rows_of, 2).astype(f32)
    conv_grad = jnp.stack(
        [cotangent * returned[0], returned[1] * streams[2], returned[1] * streams[1]], axis=0
    ).astype(bf16)
    after = shifted(conv_grad[:, :, :2], "ctx", -1)
    proj_grad = short_backward(conv_grad, after, short_taps)
    weight_grad = lax.psum_scatter(
        jnp.einsum("tr,pct->rpc", tokens, proj_grad, preferred_element_type=f32).astype(bf16),
        "ctx",
        scatter_dimension=0,
        tiled=True,
    )
    input_grad = lax.psum_scatter(
        jnp.einsum("pct,rpc->tr", proj_grad, whole_weight, preferred_element_type=f32).astype(
            bf16
        ),
        "tp",
        scatter_dimension=0,
        tiled=True,
    )
    return (input_grad, weight_grad, filter_grad)


def solution(mesh):
    in_specs = (
        P("ctx", None),
        P("ctx", None, "tp"),
        P(None, None, "tp"),
        P(("tp", "ctx"), None),
        P(("tp", "ctx")),
        P("tp", "ctx"),
    )
    out_specs = (P(("ctx", "tp"), None), P("ctx", None, "tp"), P(("tp", "ctx"), None))
    return jax.shard_map(
        on_device, mesh=mesh, in_specs=in_specs, out_specs=out_specs, check_vma=False
    )
```

```python
import functools
import math

import jax
import jax.numpy as jnp
import numpy as np
from jax import lax
from jax.experimental import pallas as pl
from jax.experimental.pallas import tpu as pltpu
from jax.sharding import PartitionSpec as P

MESH = pl.DeviceIdType.MESH
ANY = pl.BlockSpec(memory_space=pl.ANY)
IN_VMEM = pl.BlockSpec(memory_space=pltpu.VMEM)
N_CTX = 16
LANES = 128
BLOCKS = 64
GROUP = 4


def shifted(value, axis, steps):
    count = lax.axis_size(axis)
    first, last = (max(0, -steps), min(count, count - steps))
    return lax.ppermute(value, axis, [(source, source + steps) for source in range(first, last)])


def exchange_kernel(pick, place, src, out, send_sem, recv_sem, local_sem):
    me = lax.axis_index("ctx")
    barrier = pltpu.get_barrier_semaphore()
    for step in range(1, N_CTX):
        pl.semaphore_signal(
            barrier, inc=1, device_id={"ctx": lax.rem(me + step, N_CTX)}, device_id_type=MESH
        )
    pl.semaphore_wait(barrier, N_CTX - 1)
    copies = []
    for step in range(1, N_CTX):
        peer = lax.rem(me + step, N_CTX)
        copy = pltpu.make_async_remote_copy(
            src_ref=pick(src, peer),
            dst_ref=place(out, me),
            send_sem=send_sem.at[step - 1],
            recv_sem=recv_sem.at[step - 1],
            device_id={"ctx": peer},
            device_id_type=MESH,
        )
        copy.start()
        copies.append(copy)
    own = pltpu.make_async_copy(pick(src, me), place(out, me), local_sem)
    own.start()
    own.wait()
    for copy in copies:
        copy.wait()


def rows_of(ref, index):
    return ref.at[:, pl.ds(pl.multiple_of(index * 32, 32), 32), :]


def positions_of(ref, index):
    return ref.at[:, :, pl.ds(pl.multiple_of(index * 512, 512), 512)]


def exchange(value, shape, pick, place, collective_id):
    return pl.pallas_call(
        functools.partial(exchange_kernel, pick, place),
        out_shape=jax.ShapeDtypeStruct(shape, value.dtype),
        in_specs=[ANY],
        out_specs=ANY,
        scratch_shapes=[
            pltpu.SemaphoreType.DMA((N_CTX - 1,)),
            pltpu.SemaphoreType.DMA((N_CTX - 1,)),
            pltpu.SemaphoreType.DMA,
        ],
        compiler_params=pltpu.CompilerParams(collective_id=collective_id, has_side_effects=True),
    )(value)


def tables():
    size = 2 * BLOCKS * LANES
    half = np.arange(BLOCKS) + 0.5
    n = np.arange(BLOCKS)
    m = np.arange(LANES)
    theta = 2 * np.pi * half[:, None] * n[None, :] / LANES
    phi = 2 * np.pi * half[:, None] * m[None, :] / size
    psi = 2 * np.pi * (m[:, None] * m[None, :] % LANES) / LANES
    first = np.concatenate([np.cos(theta), -np.sin(theta)], axis=0)
    second = np.block([[np.cos(psi), -np.sin(psi)], [np.sin(psi), np.cos(psi)]])
    second_back = np.block([[np.cos(psi), np.sin(psi)], [-np.sin(psi), np.cos(psi)]])
    first_back = np.concatenate([np.cos(theta).T, -np.sin(theta).T], axis=1)
    low = lambda value: jnp.asarray(value, jnp.bfloat16)
    turn = jnp.asarray(np.stack([np.cos(phi), np.sin(phi)]), jnp.float32)
    return low(first), low(second), low(second_back), low(first_back), turn


def convolve_kernel(
    arrived, filters, bias, first, second, second_back, first_back, turn, grad, result, held
):
    f32, bf16 = jnp.float32, jnp.bfloat16
    size = 2 * BLOCKS * LANES
    for n in range(BLOCKS):
        at = slice(n * LANES, (n + 1) * LANES)
        rows = slice(n * 32, (n + 1) * 32)
        held[0, rows, :] = arrived[0, :, at].astype(f32)
        held[1, rows, :] = arrived[1, :, at].astype(f32)
        held[2, rows, :] = filters[:, at]

    def dot(a, b):
        return jnp.dot(a, b, preferred_element_type=f32)

    def some(step, carry):
        cos, sin = turn[0], turn[1]
        pairs = [(j, s) for j in range(GROUP) for s in range(3)]
        signals = [
            held[s, pl.ds(step * GROUP + j, BLOCKS, stride=32), :].astype(bf16) for j, s in pairs
        ]
        mixed = dot(first[...], jnp.concatenate(signals, axis=1))
        turned = []
        for index in range(len(pairs)):
            at = slice(index * LANES, (index + 1) * LANES)
            re, im = mixed[:BLOCKS, at], mixed[BLOCKS:, at]
            turned.append(
                jnp.concatenate([re * cos + im * sin, im * cos - re * sin], axis=1).astype(bf16)
            )
        spectra = dot(jnp.concatenate(turned, axis=0), second[...])
        joined = []
        for j in range(GROUP):
            parts = []
            for s in range(3):
                rows = slice((3 * j + s) * BLOCKS, (3 * j + s + 1) * BLOCKS)
                parts.append((spectra[rows, :LANES], spectra[rows, LANES:]))
            (pr, pi), (wr, wi), (hr, hi) = parts
            joined.append(jnp.concatenate([pr * hr - pi * hi, pr * hi + pi * hr], axis=1))
            joined.append(jnp.concatenate([hr * wr + hi * wi, hr * wi - hi * wr], axis=1))
            joined.append(jnp.concatenate([pr * wr + pi * wi, pr * wi - pi * wr], axis=1))
        back = dot(jnp.concatenate(joined, axis=0).astype(bf16), second_back[...])
        cos, sin = cos * (2.0 / size), sin * (2.0 / size)
        unturned = []
        for index in range(len(pairs)):
            rows = slice(index * BLOCKS, (index + 1) * BLOCKS)
            re, im = back[rows, :LANES], back[rows, LANES:]
            unturned.append(
                jnp.concatenate([re * cos - im * sin, im * cos + re * sin], axis=0).astype(bf16)
            )
        final = dot(first_back[...], jnp.concatenate(unturned, axis=1))
        for index, (j, s) in enumerate(pairs):
            held[s, pl.ds(step * GROUP + j, BLOCKS, stride=32), :] = final[
                :, index * LANES : (index + 1) * LANES
            ]
        return carry

    lax.fori_loop(0, 32 // GROUP, some, 0)
    gain = bias[...]
    for n in range(BLOCKS):
        at = slice(n * LANES, (n + 1) * LANES)
        rows = slice(n * 32, (n + 1) * 32)
        for s in range(2):
            result[s, :, at] = (held[s, rows, :] + gain * arrived[s, :, at].astype(f32)).astype(bf16)
        grad[:, at] = held[2, rows, :]


def convolve(arrived, long_filter, skip_bias):
    bias = jnp.broadcast_to(skip_bias[:, None], (32, LANES))
    return pl.pallas_call(
        convolve_kernel,
        out_shape=(
            jax.ShapeDtypeStruct((32, BLOCKS * LANES), jnp.float32),
            jax.ShapeDtypeStruct((2, 32, BLOCKS * LANES), jnp.bfloat16),
        ),
        in_specs=[IN_VMEM] * 8,
        out_specs=(IN_VMEM, IN_VMEM),
        scratch_shapes=[pltpu.VMEM((3, 32 * BLOCKS, LANES), jnp.float32)],
        compiler_params=pltpu.CompilerParams(vmem_limit_bytes=48 * 1024 * 1024),
    )(arrived, long_filter, bias, *tables())


def places():
    me, b = lax.axis_index("ctx"), lax.axis_index("tp")
    core, xh, y = lax.rem(me, 2), lax.rem(me // 2, 2), me // 4
    z, xl = lax.rem(b, 4), b // 4
    ctx_of = lambda y, xh: (y * 2 + xh) * 2 + core
    return dict(
        core=core,
        xh=xh,
        y=y,
        z=z,
        xl=xl,
        twin={"ctx": me + 1 - 2 * core},
        up={"ctx": ctx_of(lax.rem(y + 1, 4), xh)},
        down={"ctx": ctx_of(lax.rem(y + 3, 4), xh)},
        near={"ctx": me, "tp": (1 - xl) * 4 + z},
        far={"ctx": ctx_of(y, 1 - xh), "tp": (1 - xl) * 4 + z},
        above={"tp": xl * 4 + lax.rem(z + 1, 4)},
        below={"tp": xl * 4 + lax.rem(z + 3, 4)},
    )


def greet(peers):
    barrier = pltpu.get_barrier_semaphore()
    for peer in peers:
        pl.semaphore_signal(barrier, inc=1, device_id=peer, device_id_type=MESH)
    pl.semaphore_wait(barrier, len(peers))


def reduce_kernel(
    pgc, pgt, tokens, others, weight, ig_out, wg_out,
    tok, oth, wei, pgo, ig, acc, part, r2, rf, relay, xr, z2, zf, xz, send, recv, load,
):
    f32, bf16 = jnp.float32, jnp.bfloat16
    at = places()
    core, xh, y, z, xl = at["core"], at["xh"], at["y"], at["z"], at["xl"]
    loads = [
        pltpu.make_async_copy(weight.at[pl.ds(0, 2048)], wei.at[pl.ds(0, 2048)], load.at[0]),
        pltpu.make_async_copy(tokens, tok, load.at[1]),
        pltpu.make_async_copy(others, oth, load.at[2]),
        pltpu.make_async_copy(weight.at[pl.ds(2048, 2048)], wei.at[pl.ds(2048, 2048)], load.at[3]),
    ]
    for one in loads:
        one.start()
    greet([at[name] for name in ("twin", "up", "down", "near", "far", "above", "below")])
    sent = {}

    def start(name, src, dst, peer):
        index = len(sent)
        copy = pltpu.make_async_remote_copy(
            src_ref=src,
            dst_ref=dst,
            send_sem=send.at[index],
            recv_sem=recv.at[index],
            device_id=at[peer],
            device_id_type=MESH,
        )
        copy.start()
        sent[name] = copy

    def arrived(name):
        sent[name].wait_recv()

    def input_tiles(first):
        def tile(step, carry):
            rows = pl.ds(pl.multiple_of((first + step) * 256, 256), 256)
            ig[:, rows] = lax.dot_general(
                pgt[...], wei[rows, :], (((1,), (1,)), ((), ())), preferred_element_type=f32
            ).astype(bf16)
            return carry

        lax.fori_loop(0, 8, tile, 0)

    def weight_part(block):
        mine = pl.ds(pl.multiple_of((2 * block + core) * 256, 256), 256)
        theirs = pl.ds(pl.multiple_of(block * 256, 256), 256)

        def half(step, carry):
            rows = pl.ds(pl.multiple_of(step * 768, 256), 768)
            acc[rows, :] = jnp.dot(pgc[rows, :], tok[:, mine], preferred_element_type=f32) + jnp.dot(
                pgo[rows, :], oth[:, theirs], preferred_element_type=f32
            )
            return carry

        lax.fori_loop(0, 2, half, 0)

    def fold(dst, first, last, *terms):
        def chunk(step, carry):
            rows = pl.ds(pl.multiple_of(step * 128, 128), 128)
            total = acc[rows, :]
            for term, offset in terms:
                part_rows = pl.ds(pl.multiple_of(step * 128 - offset, 128), 128)
                total = total + term[part_rows, :].astype(f32)
            dst[rows, :] = total.astype(bf16)
            return carry

        lax.fori_loop(first // 128, last // 128, chunk, 0)

    def block_of(y, xh):
        return y * 2 + xh

    y2, yp, ym = lax.rem(y + 2, 4), lax.rem(y + 1, 4), lax.rem(y + 3, 4)
    z2i, zp, zm = lax.rem(z + 2, 4), lax.rem(z + 1, 4), lax.rem(z + 3, 4)
    columns = (1 - xh, xh)
    sides = (1 - xl, xl)
    low, high = pl.ds(0, 768), pl.ds(768, 768)

    start("twin", pgc, pgo, "twin")
    loads[0].wait()
    input_tiles(0)
    loads[1].wait()
    loads[2].wait()
    arrived("twin")
    for k in range(2):
        weight_part(block_of(y2, columns[k]))
        fold(part.at[k], 0, 1536)
        start(("2p", k), part.at[k, low], r2.at[k, 0], "up")
        start(("2m", k), part.at[k, high], r2.at[k, 1], "down")
    loads[3].wait()
    input_tiles(8)

    def ig_rows(side, z, first, count):
        return pl.ds(pl.multiple_of((side * 4 + z) * 64 + first, 32), count)

    for k in range(2):
        start(("z2p", k), ig.at[ig_rows(sides[k], z2i, 0, 32)], z2.at[k, 0], "above")
        start(("z2m", k), ig.at[ig_rows(sides[k], z2i, 32, 32)], z2.at[k, 1], "below")

    def ig_add(rows, *terms):
        total = ig[rows, :].astype(f32)
        for term in terms:
            total = total + term[...].astype(f32)
        return total

    for k in range(2):
        weight_part(block_of(yp, columns[k]))
        arrived(("2p", k))
        fold(part.at[2 + 2 * k], 0, 768, (r2.at[k, 0], 0))
        fold(part.at[2 + 2 * k], 768, 1536)
        start(("fp", k), part.at[2 + 2 * k], rf.at[k, 0], "up")
        weight_part(block_of(ym, columns[k]))
        arrived(("2m", k))
        fold(part.at[3 + 2 * k], 0, 768)
        fold(part.at[3 + 2 * k], 768, 1536, (r2.at[k, 1], 768))
        start(("fm", k), part.at[3 + 2 * k], rf.at[k, 1], "down")
        arrived(("z2p", k))
        rows = ig_rows(sides[k], zp, 0, 32)
        ig[rows, :] = ig_add(rows, z2.at[k, 0]).astype(bf16)
        start(("zfp", k), ig.at[ig_rows(sides[k], zp, 0, 64)], zf.at[k, 0], "above")
        arrived(("z2m", k))
        rows = ig_rows(sides[k], zm, 32, 32)
        ig[rows, :] = ig_add(rows, z2.at[k, 1]).astype(bf16)
        start(("zfm", k), ig.at[ig_rows(sides[k], zm, 0, 64)], zf.at[k, 1], "below")

    weight_part(block_of(y, columns[0]))
    arrived(("fp", 0))
    arrived(("fm", 0))
    fold(part.at[6], 0, 1536, (rf.at[0, 0], 0), (rf.at[0, 1], 0))
    start("xa", part.at[6, low], relay.at[0], "near")
    start("xb", part.at[6, high], relay.at[1], "far")
    arrived(("zfp", 0))
    arrived(("zfm", 0))
    rows = ig_rows(sides[0], z, 0, 64)
    ig[rows, :] = ig_add(rows, zf.at[0, 0], zf.at[0, 1]).astype(bf16)
    start("xz", ig.at[rows], xz, "near")
    arrived("xa")
    start("ya", relay.at[0], xr.at[low], "far")
    arrived("xb")
    start("yb", relay.at[1], xr.at[high], "near")
    weight_part(block_of(y, columns[1]))
    arrived(("zfp", 1))
    arrived(("zfm", 1))
    arrived("xz")
    ig_out[...] = ig_add(ig_rows(sides[1], z, 0, 64), zf.at[1, 0], zf.at[1, 1], xz).astype(bf16)
    arrived(("fp", 1))
    arrived(("fm", 1))
    arrived("ya")
    arrived("yb")
    fold(wg_out, 0, 1536, (rf.at[1, 0], 0), (rf.at[1, 1], 0), (xr, 0))
    for copy in sent.values():
        copy.wait_send()


def gradients(pgc, pgt, tokens, others, weight):
    bf16 = jnp.bfloat16
    vmem = lambda *shape: pltpu.VMEM(shape, bf16)
    return pl.pallas_call(
        reduce_kernel,
        out_shape=(
            jax.ShapeDtypeStruct((64, 4096), bf16),
            jax.ShapeDtypeStruct((1536, 256), bf16),
        ),
        in_specs=[IN_VMEM, IN_VMEM, ANY, ANY, ANY],
        out_specs=(IN_VMEM, IN_VMEM),
        scratch_shapes=[
            vmem(512, 4096),
            vmem(512, 2048),
            vmem(4096, 1536),
            vmem(1536, 512),
            vmem(512, 4096),
            pltpu.VMEM((1536, 256), jnp.float32),
            vmem(7, 1536, 256),
            vmem(2, 2, 768, 256),
            vmem(2, 2, 1536, 256),
            vmem(2, 768, 256),
            vmem(1536, 256),
            vmem(2, 2, 32, 4096),
            vmem(2, 2, 64, 4096),
            vmem(64, 4096),
            pltpu.SemaphoreType.DMA((22,)),
            pltpu.SemaphoreType.DMA((22,)),
            pltpu.SemaphoreType.DMA((4,)),
        ],
        compiler_params=pltpu.CompilerParams(
            collective_id=3, has_side_effects=True, vmem_limit_bytes=56 * 1024 * 1024
        ),
        cost_estimate=pl.CostEstimate(
            flops=4 * 512 * 4096 * 1536, bytes_accessed=24 * 1024 * 1024, transcendentals=0
        ),
    )(pgc, pgt, tokens, others, weight)


def short_forward(values, before, taps):
    extended = jnp.concatenate([before, values], axis=2).astype(jnp.float32)
    return (
        taps[0][:, :, None] * extended[:, :, 2:]
        + taps[1][:, :, None] * extended[:, :, 1:-1]
        + taps[2][:, :, None] * extended[:, :, :-2]
    ).astype(jnp.bfloat16)


def short_backward(values, after, taps):
    extended = jnp.concatenate([values, after], axis=2).astype(jnp.float32)
    return (
        taps[0][:, :, None] * extended[:, :, :-2]
        + taps[1][:, :, None] * extended[:, :, 1:-1]
        + taps[2][:, :, None] * extended[:, :, 2:]
    ).astype(jnp.bfloat16)


def on_device(tokens, in_weight, short_taps, long_filter, skip_bias, out_grad):
    f32, bf16 = jnp.float32, jnp.bfloat16
    me = lax.axis_index("ctx")
    cut = tokens.reshape(512, 8, 2, 256)
    theirs = lax.dynamic_index_in_dim(cut, 1 - lax.rem(me, 2), 2, keepdims=False).reshape(512, 2048)
    others = lax.ppermute(theirs, "ctx", [(index, index ^ 1) for index in range(N_CTX)])
    whole_weight = lax.all_gather(in_weight.reshape(256, 1536), "ctx", axis=0, tiled=True)
    projected = lax.dot_general(
        whole_weight, tokens, (((0,), (1,)), ((), ())), preferred_element_type=f32
    )
    projected = projected.astype(bf16).reshape(3, 512, 512)
    before = shifted(projected[:, :, -2:], "ctx", 1)
    streams = short_forward(projected, before, short_taps).astype(f32)
    cotangent = out_grad.astype(f32)
    outgoing = jnp.stack([streams[1] * streams[2], cotangent * streams[0]]).astype(bf16)
    arrived = exchange(outgoing, (2, 32, 8192), rows_of, positions_of, 1)
    filter_grad, result = convolve(arrived, long_filter, skip_bias)
    returned = exchange(result, (2, 512, 512), positions_of, rows_of, 2).astype(f32)
    conv_grad = jnp.stack(
        [cotangent * returned[0], returned[1] * streams[2], returned[1] * streams[1]], axis=0
    ).astype(bf16)
    after = shifted(conv_grad[:, :, :2], "ctx", -1)
    proj_grad = short_backward(conv_grad, after, short_taps).reshape(1536, 512)
    input_grad, weight_grad = gradients(proj_grad, proj_grad.T, tokens, others, whole_weight)
    return (input_grad, weight_grad.T.reshape(256, 3, 512), filter_grad)


def solution(mesh):
    in_specs = (
        P("ctx", None),
        P("ctx", None, "tp"),
        P(None, None, "tp"),
        P(("tp", "ctx"), None),
        P(("tp", "ctx")),
        P("tp", "ctx"),
    )
    out_specs = (P(("ctx", "tp"), None), P("ctx", None, "tp"), P(("tp", "ctx"), None))
    return jax.shard_map(
        on_device, mesh=mesh, in_specs=in_specs, out_specs=out_specs, check_vma=False
    )
```

```python
import functools
import math

import jax
import jax.numpy as jnp
import numpy as np
from jax import lax
from jax.experimental import pallas as pl
from jax.experimental.pallas import tpu as pltpu
from jax.sharding import PartitionSpec as P

MESH = pl.DeviceIdType.MESH
ANY = pl.BlockSpec(memory_space=pl.ANY)
IN_VMEM = pl.BlockSpec(memory_space=pltpu.VMEM)
N_CTX = 16
LANES = 128
BLOCKS = 64
GROUP = 4


def shifted(value, axis, steps):
    count = lax.axis_size(axis)
    first, last = (max(0, -steps), min(count, count - steps))
    return lax.ppermute(value, axis, [(source, source + steps) for source in range(first, last)])


def exchange_kernel(pick, place, src, out, send_sem, recv_sem, local_sem):
    me = lax.axis_index("ctx")
    barrier = pltpu.get_barrier_semaphore()
    for step in range(1, N_CTX):
        pl.semaphore_signal(
            barrier, inc=1, device_id={"ctx": lax.rem(me + step, N_CTX)}, device_id_type=MESH
        )
    pl.semaphore_wait(barrier, N_CTX - 1)
    copies = []
    for step in range(1, N_CTX):
        peer = lax.rem(me + step, N_CTX)
        copy = pltpu.make_async_remote_copy(
            src_ref=pick(src, peer),
            dst_ref=place(out, me),
            send_sem=send_sem.at[step - 1],
            recv_sem=recv_sem.at[step - 1],
            device_id={"ctx": peer},
            device_id_type=MESH,
        )
        copy.start()
        copies.append(copy)
    own = pltpu.make_async_copy(pick(src, me), place(out, me), local_sem)
    own.start()
    own.wait()
    for copy in copies:
        copy.wait()


def rows_of(ref, index):
    return ref.at[:, pl.ds(pl.multiple_of(index * 32, 32), 32), :]


def positions_of(ref, index):
    return ref.at[:, :, pl.ds(pl.multiple_of(index * 512, 512), 512)]


def exchange(value, shape, pick, place, collective_id):
    return pl.pallas_call(
        functools.partial(exchange_kernel, pick, place),
        out_shape=jax.ShapeDtypeStruct(shape, value.dtype),
        in_specs=[ANY],
        out_specs=ANY,
        scratch_shapes=[
            pltpu.SemaphoreType.DMA((N_CTX - 1,)),
            pltpu.SemaphoreType.DMA((N_CTX - 1,)),
            pltpu.SemaphoreType.DMA,
        ],
        compiler_params=pltpu.CompilerParams(collective_id=collective_id, has_side_effects=True),
    )(value)


def tables():
    size = 2 * BLOCKS * LANES
    half = np.arange(BLOCKS) + 0.5
    n = np.arange(BLOCKS)
    m = np.arange(LANES)
    theta = 2 * np.pi * half[:, None] * n[None, :] / LANES
    phi = 2 * np.pi * half[:, None] * m[None, :] / size
    psi = 2 * np.pi * (m[:, None] * m[None, :] % LANES) / LANES
    first = np.concatenate([np.cos(theta), -np.sin(theta)], axis=0)
    second = np.block([[np.cos(psi), -np.sin(psi)], [np.sin(psi), np.cos(psi)]])
    second_back = np.block([[np.cos(psi), np.sin(psi)], [-np.sin(psi), np.cos(psi)]])
    first_back = np.concatenate([np.cos(theta).T, -np.sin(theta).T], axis=1)
    low = lambda value: jnp.asarray(value, jnp.bfloat16)
    turn = jnp.asarray(np.stack([np.cos(phi), np.sin(phi)]), jnp.float32)
    return low(first), low(second), low(second_back), low(first_back), turn


def convolve_kernel(
    arrived, filters, bias, first, second, second_back, first_back, turn, grad, result, held
):
    f32, bf16 = jnp.float32, jnp.bfloat16
    size = 2 * BLOCKS * LANES
    for n in range(BLOCKS):
        at = slice(n * LANES, (n + 1) * LANES)
        rows = slice(n * 32, (n + 1) * 32)
        held[0, rows, :] = arrived[0, :, at].astype(f32)
        held[1, rows, :] = arrived[1, :, at].astype(f32)
        held[2, rows, :] = filters[:, at]

    def dot(a, b):
        return jnp.dot(a, b, preferred_element_type=f32)

    def some(step, carry):
        cos, sin = turn[0], turn[1]
        pairs = [(j, s) for j in range(GROUP) for s in range(3)]
        signals = [
            held[s, pl.ds(step * GROUP + j, BLOCKS, stride=32), :].astype(bf16) for j, s in pairs
        ]
        mixed = dot(first[...], jnp.concatenate(signals, axis=1))
        turned = []
        for index in range(len(pairs)):
            at = slice(index * LANES, (index + 1) * LANES)
            re, im = mixed[:BLOCKS, at], mixed[BLOCKS:, at]
            turned.append(
                jnp.concatenate([re * cos + im * sin, im * cos - re * sin], axis=1).astype(bf16)
            )
        spectra = dot(jnp.concatenate(turned, axis=0), second[...])
        joined = []
        for j in range(GROUP):
            parts = []
            for s in range(3):
                rows = slice((3 * j + s) * BLOCKS, (3 * j + s + 1) * BLOCKS)
                parts.append((spectra[rows, :LANES], spectra[rows, LANES:]))
            (pr, pi), (wr, wi), (hr, hi) = parts
            joined.append(jnp.concatenate([pr * hr - pi * hi, pr * hi + pi * hr], axis=1))
            joined.append(jnp.concatenate([hr * wr + hi * wi, hr * wi - hi * wr], axis=1))
            joined.append(jnp.concatenate([pr * wr + pi * wi, pr * wi - pi * wr], axis=1))
        back = dot(jnp.concatenate(joined, axis=0).astype(bf16), second_back[...])
        cos, sin = cos * (2.0 / size), sin * (2.0 / size)
        unturned = []
        for index in range(len(pairs)):
            rows = slice(index * BLOCKS, (index + 1) * BLOCKS)
            re, im = back[rows, :LANES], back[rows, LANES:]
            unturned.append(
                jnp.concatenate([re * cos - im * sin, im * cos + re * sin], axis=0).astype(bf16)
            )
        final = dot(first_back[...], jnp.concatenate(unturned, axis=1))
        for index, (j, s) in enumerate(pairs):
            held[s, pl.ds(step * GROUP + j, BLOCKS, stride=32), :] = final[
                :, index * LANES : (index + 1) * LANES
            ]
        return carry

    lax.fori_loop(0, 32 // GROUP, some, 0)
    gain = bias[...]
    for n in range(BLOCKS):
        at = slice(n * LANES, (n + 1) * LANES)
        rows = slice(n * 32, (n + 1) * 32)
        for s in range(2):
            result[s, :, at] = (held[s, rows, :] + gain * arrived[s, :, at].astype(f32)).astype(bf16)
        grad[:, at] = held[2, rows, :]


def convolve(arrived, long_filter, skip_bias):
    bias = jnp.broadcast_to(skip_bias[:, None], (32, LANES))
    return pl.pallas_call(
        convolve_kernel,
        out_shape=(
            jax.ShapeDtypeStruct((32, BLOCKS * LANES), jnp.float32),
            jax.ShapeDtypeStruct((2, 32, BLOCKS * LANES), jnp.bfloat16),
        ),
        in_specs=[IN_VMEM] * 8,
        out_specs=(IN_VMEM, IN_VMEM),
        scratch_shapes=[pltpu.VMEM((3, 32 * BLOCKS, LANES), jnp.float32)],
        compiler_params=pltpu.CompilerParams(vmem_limit_bytes=48 * 1024 * 1024),
    )(arrived, long_filter, bias, *tables())


def places():
    me, b = lax.axis_index("ctx"), lax.axis_index("tp")
    core, xh, y = lax.rem(me, 2), lax.rem(me // 2, 2), me // 4
    z, xl = lax.rem(b, 4), b // 4
    ctx_of = lambda y, xh: (y * 2 + xh) * 2 + core
    return dict(
        core=core,
        xh=xh,
        y=y,
        z=z,
        xl=xl,
        twin={"ctx": me + 1 - 2 * core},
        up={"ctx": ctx_of(lax.rem(y + 1, 4), xh)},
        down={"ctx": ctx_of(lax.rem(y + 3, 4), xh)},
        near={"ctx": me, "tp": (1 - xl) * 4 + z},
        far={"ctx": ctx_of(y, 1 - xh), "tp": (1 - xl) * 4 + z},
        above={"tp": xl * 4 + lax.rem(z + 1, 4)},
        below={"tp": xl * 4 + lax.rem(z + 3, 4)},
    )


def greet(peers):
    barrier = pltpu.get_barrier_semaphore()
    for peer in peers:
        pl.semaphore_signal(barrier, inc=1, device_id=peer, device_id_type=MESH)
    pl.semaphore_wait(barrier, len(peers))


def reduce_kernel(
    pgc, pgt, tokens, others, weight, ig_out, wg_out,
    tok, oth, wei, pgo, ig, acc, part, r2, rf, relay, xr, z2, zf, xz, send, recv, load,
):
    f32, bf16 = jnp.float32, jnp.bfloat16
    at = places()
    core, xh, y, z, xl = at["core"], at["xh"], at["y"], at["z"], at["xl"]
    loads = [
        pltpu.make_async_copy(weight.at[pl.ds(0, 2048)], wei.at[pl.ds(0, 2048)], load.at[0]),
        pltpu.make_async_copy(tokens, tok, load.at[1]),
        pltpu.make_async_copy(others, oth, load.at[2]),
        pltpu.make_async_copy(weight.at[pl.ds(2048, 2048)], wei.at[pl.ds(2048, 2048)], load.at[3]),
    ]
    for one in loads:
        one.start()
    greet([at[name] for name in ("twin", "up", "down", "near", "far", "above", "below")])
    sent = {}

    def start(name, src, dst, peer):
        index = len(sent)
        copy = pltpu.make_async_remote_copy(
            src_ref=src,
            dst_ref=dst,
            send_sem=send.at[index],
            recv_sem=recv.at[index],
            device_id=at[peer],
            device_id_type=MESH,
        )
        copy.start()
        sent[name] = copy

    def arrived(name):
        sent[name].wait_recv()

    def input_tiles(first):
        def tile(step, carry):
            rows = pl.ds(pl.multiple_of((first + step) * 256, 256), 256)
            ig[:, rows] = lax.dot_general(
                pgt[...], wei[rows, :], (((1,), (1,)), ((), ())), preferred_element_type=f32
            ).astype(bf16)
            return carry

        lax.fori_loop(0, 8, tile, 0)

    def weight_part(block):
        mine = pl.ds(pl.multiple_of((2 * block + core) * 256, 256), 256)
        theirs = pl.ds(pl.multiple_of(block * 256, 256), 256)

        def half(step, carry):
            rows = pl.ds(pl.multiple_of(step * 768, 256), 768)
            acc[rows, :] = jnp.dot(pgc[rows, :], tok[:, mine], preferred_element_type=f32) + jnp.dot(
                pgo[rows, :], oth[:, theirs], preferred_element_type=f32
            )
            return carry

        lax.fori_loop(0, 2, half, 0)

    def fold(dst, first, last, *terms):
        def chunk(step, carry):
            rows = pl.ds(pl.multiple_of(step * 128, 128), 128)
            total = acc[rows, :]
            for term, offset in terms:
                part_rows = pl.ds(pl.multiple_of(step * 128 - offset, 128), 128)
                total = total + term[part_rows, :].astype(f32)
            dst[rows, :] = total.astype(bf16)
            return carry

        lax.fori_loop(first // 128, last // 128, chunk, 0)

    def block_of(y, xh):
        return y * 2 + xh

    y2, yp, ym = lax.rem(y + 2, 4), lax.rem(y + 1, 4), lax.rem(y + 3, 4)
    z2i, zp, zm = lax.rem(z + 2, 4), lax.rem(z + 1, 4), lax.rem(z + 3, 4)
    columns = (1 - xh, xh)
    sides = (1 - xl, xl)
    low, high = pl.ds(0, 768), pl.ds(768, 768)

    start("twin", pgc, pgo, "twin")
    loads[0].wait()
    input_tiles(0)
    loads[1].wait()
    loads[2].wait()
    arrived("twin")
    for k in range(2):
        weight_part(block_of(y2, columns[k]))
        fold(part.at[k], 0, 1536)
        start(("2p", k), part.at[k, low], r2.at[k, 0], "up")
        start(("2m", k), part.at[k, high], r2.at[k, 1], "down")
    loads[3].wait()
    input_tiles(8)

    def ig_rows(side, z, first, count):
        return pl.ds(pl.multiple_of((side * 4 + z) * 64 + first, 32), count)

    for k in range(2):
        start(("z2p", k), ig.at[ig_rows(sides[k], z2i, 0, 32)], z2.at[k, 0], "above")
        start(("z2m", k), ig.at[ig_rows(sides[k], z2i, 32, 32)], z2.at[k, 1], "below")

    def ig_add(rows, *terms):
        total = ig[rows, :].astype(f32)
        for term in terms:
            total = total + term[...].astype(f32)
        return total

    for k in range(2):
        weight_part(block_of(yp, columns[k]))
        arrived(("2p", k))
        fold(part.at[2 + 2 * k], 0, 768, (r2.at[k, 0], 0))
        fold(part.at[2 + 2 * k], 768, 1536)
        start(("fp", k), part.at[2 + 2 * k], rf.at[k, 0], "up")
        weight_part(block_of(ym, columns[k]))
        arrived(("2m", k))
        fold(part.at[3 + 2 * k], 0, 768)
        fold(part.at[3 + 2 * k], 768, 1536, (r2.at[k, 1], 768))
        start(("fm", k), part.at[3 + 2 * k], rf.at[k, 1], "down")
        arrived(("z2p", k))
        rows = ig_rows(sides[k], zp, 0, 32)
        ig[rows, :] = ig_add(rows, z2.at[k, 0]).astype(bf16)
        start(("zfp", k), ig.at[ig_rows(sides[k], zp, 0, 64)], zf.at[k, 0], "above")
        arrived(("z2m", k))
        rows = ig_rows(sides[k], zm, 32, 32)
        ig[rows, :] = ig_add(rows, z2.at[k, 1]).astype(bf16)
        start(("zfm", k), ig.at[ig_rows(sides[k], zm, 0, 64)], zf.at[k, 1], "below")

    weight_part(block_of(y, columns[0]))
    arrived(("fp", 0))
    arrived(("fm", 0))
    fold(part.at[6], 0, 1536, (rf.at[0, 0], 0), (rf.at[0, 1], 0))
    start("xa", part.at[6, low], relay.at[0], "near")
    start("xb", part.at[6, high], relay.at[1], "far")
    arrived(("zfp", 0))
    arrived(("zfm", 0))
    rows = ig_rows(sides[0], z, 0, 64)
    ig[rows, :] = ig_add(rows, zf.at[0, 0], zf.at[0, 1]).astype(bf16)
    start("xz", ig.at[rows], xz, "near")
    arrived("xa")
    start("ya", relay.at[0], xr.at[low], "far")
    arrived("xb")
    start("yb", relay.at[1], xr.at[high], "near")
    weight_part(block_of(y, columns[1]))
    arrived(("zfp", 1))
    arrived(("zfm", 1))
    arrived("xz")
    ig_out[...] = ig_add(ig_rows(sides[1], z, 0, 64), zf.at[1, 0], zf.at[1, 1], xz).astype(bf16)
    arrived(("fp", 1))
    arrived(("fm", 1))
    arrived("ya")
    arrived("yb")
    fold(wg_out, 0, 1536, (rf.at[1, 0], 0), (rf.at[1, 1], 0), (xr, 0))
    for copy in sent.values():
        copy.wait_send()


def gradients(pgc, pgt, tokens, others, weight):
    bf16 = jnp.bfloat16
    vmem = lambda *shape: pltpu.VMEM(shape, bf16)
    return pl.pallas_call(
        reduce_kernel,
        out_shape=(
            jax.ShapeDtypeStruct((64, 4096), bf16),
            jax.ShapeDtypeStruct((1536, 256), bf16),
        ),
        in_specs=[IN_VMEM, IN_VMEM, ANY, ANY, ANY],
        out_specs=(IN_VMEM, IN_VMEM),
        scratch_shapes=[
            vmem(512, 4096),
            vmem(512, 2048),
            vmem(4096, 1536),
            vmem(1536, 512),
            vmem(512, 4096),
            pltpu.VMEM((1536, 256), jnp.float32),
            vmem(7, 1536, 256),
            vmem(2, 2, 768, 256),
            vmem(2, 2, 1536, 256),
            vmem(2, 768, 256),
            vmem(1536, 256),
            vmem(2, 2, 32, 4096),
            vmem(2, 2, 64, 4096),
            vmem(64, 4096),
            pltpu.SemaphoreType.DMA((22,)),
            pltpu.SemaphoreType.DMA((22,)),
            pltpu.SemaphoreType.DMA((4,)),
        ],
        compiler_params=pltpu.CompilerParams(
            collective_id=3, has_side_effects=True, vmem_limit_bytes=56 * 1024 * 1024
        ),
        cost_estimate=pl.CostEstimate(
            flops=4 * 512 * 4096 * 1536, bytes_accessed=24 * 1024 * 1024, transcendentals=0
        ),
    )(pgc, pgt, tokens, others, weight)


def project_kernel(tokens, weight, projected, whole, others, tok, wall, acc, send, recv, load):
    f32, bf16 = jnp.float32, jnp.bfloat16
    at = places()
    core, xh, y = at["core"], at["xh"], at["y"]
    me = lax.axis_index("ctx")
    at["across"] = {"ctx": (y * 2 + 1 - xh) * 2 + core}
    at["next"] = {"ctx": lax.rem(me + 1, N_CTX)}
    at["last"] = {"ctx": lax.rem(me + N_CTX - 1, N_CTX)}
    loads = [
        pltpu.make_async_copy(weight, wall.at[me], load.at[0]),
        pltpu.make_async_copy(tokens, tok.at[pl.ds(16, 512)], load.at[1]),
    ]
    for one in loads:
        one.start()
    greet([at[name] for name in ("twin", "up", "down", "across", "next", "last")])
    sent = {}

    def start(name, src, dst, peer):
        index = len(sent)
        copy = pltpu.make_async_remote_copy(
            src_ref=src,
            dst_ref=dst,
            send_sem=send.at[index],
            recv_sem=recv.at[index],
            device_id=at[peer],
            device_id_type=MESH,
        )
        copy.start()
        sent[name] = copy

    def arrived(*names):
        for name in names:
            sent[name].wait_recv()

    halves = (pl.ds(0, 128), pl.ds(128, 128))

    def half_of(index, half):
        return wall.at[index, halves[half]]

    def pass_on(name, index, half, peer):
        start(name, half_of(index, half), half_of(index, half), peer)

    def hand_over(name, index):
        start(name, wall.at[index], wall.at[index], "twin")

    stored = []

    def multiply(index, fresh=False):
        pair = index // 2
        columns = pl.ds(pl.multiple_of(pair * 512, 512), 512)
        store = pltpu.make_async_copy(
            wall.at[pl.ds(pair * 2, 2)], whole.at[pl.ds(pair * 2, 2)], load.at[2 + len(stored)]
        )
        store.start()
        stored.append(store)

        def tile(step, carry):
            place = pl.ds(pl.multiple_of(step * 512, 512), 512)
            value = jnp.dot(
                tok[:, columns],
                wall[pl.ds(pair * 2, 2), :, place].reshape(512, 512),
                preferred_element_type=f32,
            )
            acc[:, place] = value if fresh else acc[:, place] + value
            return carry

        lax.fori_loop(0, 3, tile, 0)

    def ctx_of(y, xh):
        return (lax.rem(y, 4) * 2 + xh) * 2 + core

    below, above, beyond = ctx_of(y + 3, xh), ctx_of(y + 1, xh), ctx_of(y + 2, xh)
    side = ctx_of(y, 1 - xh)
    side_below, side_above = ctx_of(y + 3, 1 - xh), ctx_of(y + 1, 1 - xh)
    side_beyond = ctx_of(y + 2, 1 - xh)

    start("up0", weight.at[halves[0]], half_of(me, 0), "up")
    start("down1", weight.at[halves[1]], half_of(me, 1), "down")
    start("across", weight, wall.at[me], "across")
    start("twin", weight, wall.at[me], "twin")
    start("halo", tokens.at[pl.ds(496, 16)], tok.at[pl.ds(0, 16)], "next")
    for j in range(8):
        columns = pl.ds(pl.multiple_of((2 * j + 1 - core) * 256, 256), 256)
        start(("swap", j), tokens.at[:, columns], others.at[:, pl.ds(j * 256, 256)], "twin")
    arrived("up0")
    pass_on("on0", below, 0, "up")
    arrived("down1")
    pass_on("on1", above, 1, "down")
    start("up1", weight.at[halves[1]], half_of(me, 1), "up")
    start("down0", weight.at[halves[0]], half_of(me, 0), "down")
    for one in loads:
        one.wait()
    arrived("halo", "twin")
    multiply(me, fresh=True)
    arrived("across")
    pass_on("side_up0", side, 0, "up")
    pass_on("side_down1", side, 1, "down")
    hand_over("twin_side", side)
    arrived("on0", "on1")
    start("across_beyond", wall.at[beyond], wall.at[beyond], "across")
    hand_over("twin_beyond", beyond)
    pass_on("side_up1", side, 1, "up")
    pass_on("side_down0", side, 0, "down")
    arrived("twin_side")
    multiply(side)
    arrived("up1")
    hand_over("twin_below", below)
    arrived("down0")
    hand_over("twin_above", above)
    arrived("twin_beyond")
    multiply(beyond)
    arrived("twin_below")
    multiply(below)
    arrived("twin_above")
    multiply(above)
    arrived("side_up0")
    pass_on("twin_sb0", side_below, 0, "twin")
    arrived("side_down1")
    pass_on("twin_sa1", side_above, 1, "twin")
    arrived("across_beyond")
    hand_over("twin_across", side_beyond)
    arrived("twin_across")
    multiply(side_beyond)
    arrived("side_up1")
    pass_on("twin_sb1", side_below, 1, "twin")
    arrived("side_down0")
    pass_on("twin_sa0", side_above, 0, "twin")
    arrived("twin_sb0", "twin_sb1")
    multiply(side_below)
    arrived("twin_sa0", "twin_sa1")
    multiply(side_above)

    def finish(step, carry):
        rows = pl.ds(pl.multiple_of(step * 48, 16), 48)
        projected[rows, :] = acc[rows, :].astype(bf16)
        return carry

    lax.fori_loop(0, 11, finish, 0)
    for j in range(8):
        arrived(("swap", j))
    for store in stored:
        store.wait()
    for copy in sent.values():
        copy.wait_send()


def project(tokens, weight):
    bf16 = jnp.bfloat16
    return pl.pallas_call(
        project_kernel,
        out_shape=(
            jax.ShapeDtypeStruct((528, 1536), bf16),
            jax.ShapeDtypeStruct((N_CTX, 256, 1536), bf16),
            jax.ShapeDtypeStruct((512, 2048), bf16),
        ),
        in_specs=[ANY, ANY],
        out_specs=(IN_VMEM, ANY, ANY),
        scratch_shapes=[
            pltpu.VMEM((528, 4096), bf16),
            pltpu.VMEM((N_CTX, 256, 1536), bf16),
            pltpu.VMEM((528, 1536), jnp.float32),
            pltpu.SemaphoreType.DMA((34,)),
            pltpu.SemaphoreType.DMA((34,)),
            pltpu.SemaphoreType.DMA((10,)),
        ],
        compiler_params=pltpu.CompilerParams(
            collective_id=4, has_side_effects=True, vmem_limit_bytes=48 * 1024 * 1024
        ),
        cost_estimate=pl.CostEstimate(
            flops=2 * 512 * 4096 * 1536, bytes_accessed=24 * 1024 * 1024, transcendentals=0
        ),
    )(tokens, weight)


def short_forward(values, before, taps):
    extended = jnp.concatenate([before, values], axis=2).astype(jnp.float32)
    return (
        taps[0][:, :, None] * extended[:, :, 2:]
        + taps[1][:, :, None] * extended[:, :, 1:-1]
        + taps[2][:, :, None] * extended[:, :, :-2]
    ).astype(jnp.bfloat16)


def short_backward(values, after, taps):
    extended = jnp.concatenate([values, after], axis=2).astype(jnp.float32)
    return (
        taps[0][:, :, None] * extended[:, :, :-2]
        + taps[1][:, :, None] * extended[:, :, 1:-1]
        + taps[2][:, :, None] * extended[:, :, 2:]
    ).astype(jnp.bfloat16)


def on_device(tokens, in_weight, short_taps, long_filter, skip_bias, out_grad):
    f32, bf16 = jnp.float32, jnp.bfloat16
    projected, whole_weight, others = project(tokens, in_weight.reshape(256, 1536))
    whole_weight = whole_weight.reshape(4096, 1536)
    projected = projected.T.reshape(3, 512, 528)
    before = jnp.where(lax.axis_index("ctx") == 0, jnp.zeros((), bf16), projected[:, :, 14:16])
    projected = projected[:, :, 16:]
    streams = short_forward(projected, before, short_taps).astype(f32)
    cotangent = out_grad.astype(f32)
    outgoing = jnp.stack([streams[1] * streams[2], cotangent * streams[0]]).astype(bf16)
    arrived = exchange(outgoing, (2, 32, 8192), rows_of, positions_of, 1)
    filter_grad, result = convolve(arrived, long_filter, skip_bias)
    returned = exchange(result, (2, 512, 512), positions_of, rows_of, 2).astype(f32)
    conv_grad = jnp.stack(
        [cotangent * returned[0], returned[1] * streams[2], returned[1] * streams[1]], axis=0
    ).astype(bf16)
    after = shifted(conv_grad[:, :, :2], "ctx", -1)
    proj_grad = short_backward(conv_grad, after, short_taps).reshape(1536, 512)
    input_grad, weight_grad = gradients(proj_grad, proj_grad.T, tokens, others, whole_weight)
    return (input_grad, weight_grad.T.reshape(256, 3, 512), filter_grad)


def solution(mesh):
    in_specs = (
        P("ctx", None),
        P("ctx", None, "tp"),
        P(None, None, "tp"),
        P(("tp", "ctx"), None),
        P(("tp", "ctx")),
        P("tp", "ctx"),
    )
    out_specs = (P(("ctx", "tp"), None), P("ctx", None, "tp"), P(("tp", "ctx"), None))
    return jax.shard_map(
        on_device, mesh=mesh, in_specs=in_specs, out_specs=out_specs, check_vma=False
    )
```

```python
import functools
import math

import jax
import jax.numpy as jnp
import numpy as np
from jax import lax
from jax.experimental import pallas as pl
from jax.experimental.pallas import tpu as pltpu
from jax.sharding import PartitionSpec as P

MESH = pl.DeviceIdType.MESH
ANY = pl.BlockSpec(memory_space=pl.ANY)
IN_VMEM = pl.BlockSpec(memory_space=pltpu.VMEM)
N_CTX = 16
LANES = 128
BLOCKS = 64
GROUP = 4


def exchange_kernel(pick, place, src, out, send_sem, recv_sem, local_sem):
    me = lax.axis_index("ctx")
    barrier = pltpu.get_barrier_semaphore()
    for step in range(1, N_CTX):
        pl.semaphore_signal(
            barrier, inc=1, device_id={"ctx": lax.rem(me + step, N_CTX)}, device_id_type=MESH
        )
    pl.semaphore_wait(barrier, N_CTX - 1)
    copies = []
    for step in range(1, N_CTX):
        peer = lax.rem(me + step, N_CTX)
        copy = pltpu.make_async_remote_copy(
            src_ref=pick(src, peer),
            dst_ref=place(out, me),
            send_sem=send_sem.at[step - 1],
            recv_sem=recv_sem.at[step - 1],
            device_id={"ctx": peer},
            device_id_type=MESH,
        )
        copy.start()
        copies.append(copy)
    own = pltpu.make_async_copy(pick(src, me), place(out, me), local_sem)
    own.start()
    own.wait()
    for copy in copies:
        copy.wait()


def rows_of(ref, index):
    return ref.at[:, pl.ds(pl.multiple_of(index * 32, 32), 32), :]


def positions_of(ref, index):
    return ref.at[:, :, pl.ds(pl.multiple_of(index * 512, 512), 512)]


def exchange(value, shape, pick, place, collective_id):
    return pl.pallas_call(
        functools.partial(exchange_kernel, pick, place),
        out_shape=jax.ShapeDtypeStruct(shape, value.dtype),
        in_specs=[ANY],
        out_specs=ANY,
        scratch_shapes=[
            pltpu.SemaphoreType.DMA((N_CTX - 1,)),
            pltpu.SemaphoreType.DMA((N_CTX - 1,)),
            pltpu.SemaphoreType.DMA,
        ],
        compiler_params=pltpu.CompilerParams(collective_id=collective_id, has_side_effects=True),
    )(value)


def tables():
    size = 2 * BLOCKS * LANES
    half = np.arange(BLOCKS) + 0.5
    n = np.arange(BLOCKS)
    m = np.arange(LANES)
    theta = 2 * np.pi * half[:, None] * n[None, :] / LANES
    phi = 2 * np.pi * half[:, None] * m[None, :] / size
    psi = 2 * np.pi * (m[:, None] * m[None, :] % LANES) / LANES
    first = np.concatenate([np.cos(theta), -np.sin(theta)], axis=0)
    second = np.block([[np.cos(psi), -np.sin(psi)], [np.sin(psi), np.cos(psi)]])
    second_back = np.block([[np.cos(psi), np.sin(psi)], [-np.sin(psi), np.cos(psi)]])
    first_back = np.concatenate([np.cos(theta).T, -np.sin(theta).T], axis=1)
    low = lambda value: jnp.asarray(value, jnp.bfloat16)
    turn = jnp.asarray(np.stack([np.cos(phi), np.sin(phi)]), jnp.float32)
    return low(first), low(second), low(second_back), low(first_back), turn


def convolve_kernel(
    arrived, filters, bias, first, second, second_back, first_back, turn, grad, result, held
):
    f32, bf16 = jnp.float32, jnp.bfloat16
    size = 2 * BLOCKS * LANES
    for n in range(BLOCKS):
        at = slice(n * LANES, (n + 1) * LANES)
        rows = slice(n * 32, (n + 1) * 32)
        held[0, rows, :] = arrived[0, :, at].astype(f32)
        held[1, rows, :] = arrived[1, :, at].astype(f32)
        held[2, rows, :] = filters[:, at]

    def dot(a, b):
        return jnp.dot(a, b, preferred_element_type=f32)

    def some(step, carry):
        cos, sin = turn[0], turn[1]
        pairs = [(j, s) for j in range(GROUP) for s in range(3)]
        signals = [
            held[s, pl.ds(step * GROUP + j, BLOCKS, stride=32), :].astype(bf16) for j, s in pairs
        ]
        mixed = dot(first[...], jnp.concatenate(signals, axis=1))
        turned = []
        for index in range(len(pairs)):
            at = slice(index * LANES, (index + 1) * LANES)
            re, im = mixed[:BLOCKS, at], mixed[BLOCKS:, at]
            turned.append(
                jnp.concatenate([re * cos + im * sin, im * cos - re * sin], axis=1).astype(bf16)
            )
        spectra = dot(jnp.concatenate(turned, axis=0), second[...])
        joined = []
        for j in range(GROUP):
            parts = []
            for s in range(3):
                rows = slice((3 * j + s) * BLOCKS, (3 * j + s + 1) * BLOCKS)
                parts.append((spectra[rows, :LANES], spectra[rows, LANES:]))
            (pr, pi), (wr, wi), (hr, hi) = parts
            joined.append(jnp.concatenate([pr * hr - pi * hi, pr * hi + pi * hr], axis=1))
            joined.append(jnp.concatenate([hr * wr + hi * wi, hr * wi - hi * wr], axis=1))
            joined.append(jnp.concatenate([pr * wr + pi * wi, pr * wi - pi * wr], axis=1))
        back = dot(jnp.concatenate(joined, axis=0).astype(bf16), second_back[...])
        cos, sin = cos * (2.0 / size), sin * (2.0 / size)
        unturned = []
        for index in range(len(pairs)):
            rows = slice(index * BLOCKS, (index + 1) * BLOCKS)
            re, im = back[rows, :LANES], back[rows, LANES:]
            unturned.append(
                jnp.concatenate([re * cos - im * sin, im * cos + re * sin], axis=0).astype(bf16)
            )
        final = dot(first_back[...], jnp.concatenate(unturned, axis=1))
        for index, (j, s) in enumerate(pairs):
            held[s, pl.ds(step * GROUP + j, BLOCKS, stride=32), :] = final[
                :, index * LANES : (index + 1) * LANES
            ]
        return carry

    lax.fori_loop(0, 32 // GROUP, some, 0)
    gain = bias[...]
    for n in range(BLOCKS):
        at = slice(n * LANES, (n + 1) * LANES)
        rows = slice(n * 32, (n + 1) * 32)
        for s in range(2):
            result[s, :, at] = (held[s, rows, :] + gain * arrived[s, :, at].astype(f32)).astype(bf16)
        grad[:, at] = held[2, rows, :]


def convolve(arrived, long_filter, skip_bias):
    bias = jnp.broadcast_to(skip_bias[:, None], (32, LANES))
    return pl.pallas_call(
        convolve_kernel,
        out_shape=(
            jax.ShapeDtypeStruct((32, BLOCKS * LANES), jnp.float32),
            jax.ShapeDtypeStruct((2, 32, BLOCKS * LANES), jnp.bfloat16),
        ),
        in_specs=[IN_VMEM] * 8,
        out_specs=(IN_VMEM, IN_VMEM),
        scratch_shapes=[pltpu.VMEM((3, 32 * BLOCKS, LANES), jnp.float32)],
        compiler_params=pltpu.CompilerParams(vmem_limit_bytes=48 * 1024 * 1024),
    )(arrived, long_filter, bias, *tables())


def places():
    me, b = lax.axis_index("ctx"), lax.axis_index("tp")
    core, xh, y = lax.rem(me, 2), lax.rem(me // 2, 2), me // 4
    z, xl = lax.rem(b, 4), b // 4
    ctx_of = lambda y, xh: (y * 2 + xh) * 2 + core
    return dict(
        core=core,
        xh=xh,
        y=y,
        z=z,
        xl=xl,
        twin={"ctx": me + 1 - 2 * core},
        up={"ctx": ctx_of(lax.rem(y + 1, 4), xh)},
        down={"ctx": ctx_of(lax.rem(y + 3, 4), xh)},
        near={"ctx": me, "tp": (1 - xl) * 4 + z},
        far={"ctx": ctx_of(y, 1 - xh), "tp": (1 - xl) * 4 + z},
        above={"tp": xl * 4 + lax.rem(z + 1, 4)},
        below={"tp": xl * 4 + lax.rem(z + 3, 4)},
    )


def greet(peers):
    barrier = pltpu.get_barrier_semaphore()
    for peer in peers:
        pl.semaphore_signal(barrier, inc=1, device_id=peer, device_id_type=MESH)
    pl.semaphore_wait(barrier, len(peers))


def tail_kernel(
    result, cotangent, keys, values, taps, tokens, others, weight, ig_out, wg_out,
    tok, oth, wei, ret, cgx, hout, hin, pgc, pgt, pgo, ig, acc, part, xin, r2, rf, xr, z2, zf, xz,
    send, recv, load,
):
    f32, bf16 = jnp.float32, jnp.bfloat16
    at = places()
    core, xh, y, z, xl = at["core"], at["xh"], at["y"], at["z"], at["xl"]
    me = lax.axis_index("ctx")
    at["across"] = {"ctx": (y * 2 + 1 - xh) * 2 + core}
    for step in range(1, N_CTX):
        at[step] = {"ctx": lax.rem(me + step, N_CTX)}
    loads = [
        pltpu.make_async_copy(weight.at[pl.ds(0, 2048)], wei.at[pl.ds(0, 2048)], load.at[0]),
        pltpu.make_async_copy(tokens, tok, load.at[1]),
        pltpu.make_async_copy(others, oth, load.at[2]),
        pltpu.make_async_copy(weight.at[pl.ds(2048, 2048)], wei.at[pl.ds(2048, 2048)], load.at[3]),
        pltpu.make_async_copy(positions_of(result, me), rows_of(ret, me), load.at[4]),
    ]
    greet([at[name] for name in (*range(1, N_CTX), "near", "above", "below")])
    sent = {}

    def start(name, src, dst, peer):
        index = len(sent)
        copy = pltpu.make_async_remote_copy(
            src_ref=src,
            dst_ref=dst,
            send_sem=send.at[index],
            recv_sem=recv.at[index],
            device_id=at[peer],
            device_id_type=MESH,
        )
        copy.start()
        sent[name] = copy

    def arrived(*names):
        for name in names:
            sent[name].wait_recv()

    for step in range(1, N_CTX):
        peer = lax.rem(me + step, N_CTX)
        start(step, positions_of(result, peer), rows_of(ret, me), step)
    for one in loads:
        one.start()
    loads[4].wait()
    arrived(*range(1, N_CTX))

    def lanes(p, chunk):
        return pl.ds(pl.multiple_of(p * 512 + chunk * 128, 128), 128)

    def stream_grads(chunk, carry):
        rows = pl.ds(pl.multiple_of(chunk * 128, 128), 128)
        one, two = ret[0, rows, :].astype(f32), ret[1, rows, :].astype(f32)
        factors = ((one, cotangent), (two, values), (two, keys))
        for p, (value, factor) in enumerate(factors):
            grad = (value * factor[rows, :].astype(f32)).astype(bf16)
            cgx[p, rows, 0:512] = grad
            hout[:, lanes(p, chunk)] = grad[:, 0:128].T[0:16, :]
        return carry

    lax.fori_loop(0, 4, stream_grads, 0)
    start("halo", hout, hin, N_CTX - 1)

    def tapped(p, rows, first, width, kept):
        x = cgx[p, rows, first : first + width].astype(f32)
        total = taps[rows, p : p + 1] * x
        for j in (1, 2):
            total = total + taps[rows, 3 * j + p : 3 * j + p + 1] * pltpu.roll(x, width - j, 1)
        return total[:, :kept].astype(bf16)

    def front(chunk, carry):
        rows = pl.ds(pl.multiple_of(chunk * 128, 128), 128)
        for p in range(3):
            grad = tapped(p, rows, 0, 512, 384)
            pgc[lanes(p, chunk), 0:384] = grad
            pgt[0:384, lanes(p, chunk)] = grad.T
        return carry

    lax.fori_loop(0, 4, front, 0)
    start("twin0", pgc.at[:, pl.ds(0, 384)], pgo.at[:, pl.ds(0, 384)], "twin")
    arrived("halo")

    def rest(chunk, carry):
        rows = pl.ds(pl.multiple_of(chunk * 128, 128), 128)
        for p in range(3):
            first = hin[:, lanes(p, chunk)].astype(f32)
            first = jnp.where(me == N_CTX - 1, jnp.zeros_like(first), first)
            first = jnp.concatenate([first, jnp.zeros((112, 128), f32)], axis=0)
            cgx[p, rows, 512:640] = first.T.astype(bf16)
            grad = tapped(p, rows, 384, 256, 128)
            pgc[lanes(p, chunk), 384:512] = grad
            pgt[384:512, lanes(p, chunk)] = grad.T
        return carry

    lax.fori_loop(0, 4, rest, 0)
    start("twin1", pgc.at[:, pl.ds(384, 128)], pgo.at[:, pl.ds(384, 128)], "twin")

    def input_tiles(first):
        def tile(step, carry):
            rows = pl.ds(pl.multiple_of((first + step) * 512, 512), 512)
            ig[:, rows] = lax.dot_general(
                pgt[...], wei[rows, :], (((1,), (1,)), ((), ())), preferred_element_type=f32
            ).astype(bf16)
            return carry

        lax.fori_loop(0, 4, tile, 0)

    def weight_part(slot, block):
        mine = pl.ds(pl.multiple_of((2 * block + core) * 256, 256), 256)
        theirs = pl.ds(pl.multiple_of(block * 256, 256), 256)

        def half(step, carry):
            rows = pl.ds(pl.multiple_of(step * 768, 256), 768)
            acc[slot, rows, :] = jnp.dot(
                pgc[rows, :], tok[:, mine], preferred_element_type=f32
            ) + jnp.dot(pgo[rows, :], oth[:, theirs], preferred_element_type=f32)
            return carry

        lax.fori_loop(0, 2, half, 0)

    def fold(dst, slot, first, last, *terms):
        def chunk(step, carry):
            rows = pl.ds(pl.multiple_of(step * 128, 128), 128)
            total = acc[slot, rows, :]
            for term, offset in terms:
                part_rows = pl.ds(pl.multiple_of(step * 128 - offset, 128), 128)
                total = total + term[part_rows, :].astype(f32)
            dst[rows, :] = total.astype(bf16)
            return carry

        lax.fori_loop(first // 128, last // 128, chunk, 0)

    def block_of(y, xh):
        return y * 2 + xh

    y2, yp, ym = lax.rem(y + 2, 4), lax.rem(y + 1, 4), lax.rem(y + 3, 4)
    ztwo, zp, zm = lax.rem(z + 2, 4), lax.rem(z + 1, 4), lax.rem(z + 3, 4)
    xo = 1 - xh
    sides = (1 - xl, xl)
    low, high = pl.ds(0, 768), pl.ds(768, 768)
    parts = (slice(0, 2048), slice(2048, 4096))

    def ig_rows(side, z, first, count):
        return pl.ds(pl.multiple_of((side * 4 + z) * 64 + first, 32), count)

    def ig_add(rows, h, *terms):
        total = ig[rows, parts[h]].astype(f32)
        for term in terms:
            total = total + term[...].astype(f32)
        return total.astype(bf16)

    def z_first(h):
        for k in range(2):
            src = ig.at[ig_rows(sides[k], ztwo, 0, 32), parts[h]]
            start(("z2p", h, k), src, z2.at[h, k, 0], "above")
            src = ig.at[ig_rows(sides[k], ztwo, 32, 32), parts[h]]
            start(("z2m", h, k), src, z2.at[h, k, 1], "below")

    def z_second(h):
        for k in range(2):
            arrived(("z2p", h, k))
            rows = ig_rows(sides[k], zp, 0, 32)
            ig[rows, parts[h]] = ig_add(rows, h, z2.at[h, k, 0])
            src = ig.at[ig_rows(sides[k], zp, 0, 64), parts[h]]
            start(("zfp", h, k), src, zf.at[h, k, 0], "above")
            arrived(("z2m", h, k))
            rows = ig_rows(sides[k], zm, 32, 32)
            ig[rows, parts[h]] = ig_add(rows, h, z2.at[h, k, 1])
            src = ig.at[ig_rows(sides[k], zm, 0, 64), parts[h]]
            start(("zfm", h, k), src, zf.at[h, k, 1], "below")

    def z_across(h):
        arrived(("zfp", h, 0), ("zfm", h, 0))
        rows = ig_rows(sides[0], z, 0, 64)
        ig[rows, parts[h]] = ig_add(rows, h, zf.at[h, 0, 0], zf.at[h, 0, 1])
        start(("xz", h), ig.at[rows, parts[h]], xz.at[h], "near")

    def z_last(h):
        arrived(("zfp", h, 1), ("zfm", h, 1), ("xz", h))
        rows = ig_rows(sides[1], z, 0, 64)
        ig_out[:, parts[h]] = ig_add(rows, h, zf.at[h, 1, 0], zf.at[h, 1, 1], xz.at[h])

    loads[0].wait()
    input_tiles(0)
    z_first(0)
    loads[1].wait()
    loads[2].wait()
    arrived("twin0", "twin1")
    weight_part(0, block_of(y2, xo))
    fold(part.at[0], 0, 0, 1536)
    start("across0", part.at[0], xin, "across")
    weight_part(0, block_of(yp, xo))
    fold(part.at[1], 0, 0, 1536)
    start("up0", part.at[1], rf.at[0, 0], "up")
    weight_part(0, block_of(ym, xo))
    fold(part.at[2], 0, 0, 1536)
    start("down0", part.at[2], rf.at[0, 1], "down")
    loads[3].wait()
    input_tiles(4)
    z_first(1)
    z_second(0)
    weight_part(1, block_of(yp, xh))
    weight_part(2, block_of(ym, xh))
    z_second(1)
    weight_part(0, block_of(y2, xh))
    arrived("across0")
    fold(part.at[3], 0, 0, 1536, (xin, 0))
    start("up2", part.at[3, low], r2.at[0], "up")
    start("down2", part.at[3, high], r2.at[1], "down")
    weight_part(0, block_of(y, xo))
    arrived("up0", "down0")
    fold(part.at[6], 0, 0, 1536, (rf.at[0, 0], 0), (rf.at[0, 1], 0))
    start("across1", part.at[6], xr, "across")
    fold(part.at[4], 1, 768, 1536)
    start("up1b", part.at[4, high], rf.at[1, 0, high], "up")
    fold(part.at[5], 2, 0, 768)
    start("down1a", part.at[5, low], rf.at[1, 1, low], "down")
    weight_part(0, block_of(y, xh))
    z_across(0)
    z_across(1)
    arrived("up2")
    fold(part.at[4], 1, 0, 768, (r2.at[0], 0))
    start("up1a", part.at[4, low], rf.at[1, 0, low], "up")
    arrived("down2")
    fold(part.at[5], 2, 768, 1536, (r2.at[1], 768))
    start("down1b", part.at[5, high], rf.at[1, 1, high], "down")
    z_last(0)
    z_last(1)
    arrived("across1", "up1a", "up1b", "down1a", "down1b")
    fold(wg_out, 0, 0, 1536, (rf.at[1, 0], 0), (rf.at[1, 1], 0), (xr, 0))
    for copy in sent.values():
        copy.wait_send()


def gradients(result, cotangent, keys, values, taps, tokens, others, weight):
    bf16 = jnp.bfloat16
    vmem = lambda *shape: pltpu.VMEM(shape, bf16)
    return pl.pallas_call(
        tail_kernel,
        out_shape=(
            jax.ShapeDtypeStruct((64, 4096), bf16),
            jax.ShapeDtypeStruct((1536, 256), bf16),
        ),
        in_specs=[ANY] + [IN_VMEM] * 4 + [ANY] * 3,
        out_specs=(IN_VMEM, IN_VMEM),
        scratch_shapes=[
            vmem(512, 4096),
            vmem(512, 2048),
            vmem(4096, 1536),
            vmem(2, 512, 512),
            vmem(3, 512, 640),
            vmem(16, 1536),
            vmem(16, 1536),
            vmem(1536, 512),
            vmem(512, 1536),
            vmem(1536, 512),
            vmem(512, 4096),
            pltpu.VMEM((3, 1536, 256), jnp.float32),
            vmem(7, 1536, 256),
            vmem(1536, 256),
            vmem(2, 768, 256),
            vmem(2, 2, 1536, 256),
            vmem(1536, 256),
            vmem(2, 2, 2, 32, 2048),
            vmem(2, 2, 2, 64, 2048),
            vmem(2, 64, 2048),
            pltpu.SemaphoreType.DMA((48,)),
            pltpu.SemaphoreType.DMA((48,)),
            pltpu.SemaphoreType.DMA((5,)),
        ],
        compiler_params=pltpu.CompilerParams(
            collective_id=3, has_side_effects=True, vmem_limit_bytes=60 * 1024 * 1024
        ),
        cost_estimate=pl.CostEstimate(
            flops=4 * 512 * 4096 * 1536, bytes_accessed=24 * 1024 * 1024, transcendentals=0
        ),
    )(result, cotangent, keys, values, taps, tokens, others, weight)


def project_kernel(tokens, weight, projected, whole, others, tok, wall, acc, send, recv, load):
    f32, bf16 = jnp.float32, jnp.bfloat16
    at = places()
    core, xh, y = at["core"], at["xh"], at["y"]
    me = lax.axis_index("ctx")
    at["across"] = {"ctx": (y * 2 + 1 - xh) * 2 + core}
    at["next"] = {"ctx": lax.rem(me + 1, N_CTX)}
    at["last"] = {"ctx": lax.rem(me + N_CTX - 1, N_CTX)}
    loads = [
        pltpu.make_async_copy(weight, wall.at[me], load.at[0]),
        pltpu.make_async_copy(tokens, tok.at[pl.ds(16, 512)], load.at[1]),
    ]
    for one in loads:
        one.start()
    greet([at[name] for name in ("twin", "up", "down", "across", "next", "last")])
    sent = {}

    def start(name, src, dst, peer):
        index = len(sent)
        copy = pltpu.make_async_remote_copy(
            src_ref=src,
            dst_ref=dst,
            send_sem=send.at[index],
            recv_sem=recv.at[index],
            device_id=at[peer],
            device_id_type=MESH,
        )
        copy.start()
        sent[name] = copy

    def arrived(*names):
        for name in names:
            sent[name].wait_recv()

    halves = (pl.ds(0, 128), pl.ds(128, 128))

    def half_of(index, half):
        return wall.at[index, halves[half]]

    def pass_on(name, index, half, peer):
        start(name, half_of(index, half), half_of(index, half), peer)

    def hand_over(name, index):
        start(name, wall.at[index], wall.at[index], "twin")

    stored = []

    def multiply(index, fresh=False):
        pair = index // 2
        columns = pl.ds(pl.multiple_of(pair * 512, 512), 512)
        store = pltpu.make_async_copy(
            wall.at[pl.ds(pair * 2, 2)], whole.at[pl.ds(pair * 2, 2)], load.at[2 + len(stored)]
        )
        store.start()
        stored.append(store)

        def tile(step, carry):
            place = pl.ds(pl.multiple_of(step * 512, 512), 512)
            value = jnp.dot(
                tok[:, columns],
                wall[pl.ds(pair * 2, 2), :, place].reshape(512, 512),
                preferred_element_type=f32,
            )
            acc[:, place] = value if fresh else acc[:, place] + value
            return carry

        lax.fori_loop(0, 3, tile, 0)

    def ctx_of(y, xh):
        return (lax.rem(y, 4) * 2 + xh) * 2 + core

    below, above, beyond = ctx_of(y + 3, xh), ctx_of(y + 1, xh), ctx_of(y + 2, xh)
    side = ctx_of(y, 1 - xh)
    side_below, side_above = ctx_of(y + 3, 1 - xh), ctx_of(y + 1, 1 - xh)
    side_beyond = ctx_of(y + 2, 1 - xh)

    start("up0", weight.at[halves[0]], half_of(me, 0), "up")
    start("down1", weight.at[halves[1]], half_of(me, 1), "down")
    start("across", weight, wall.at[me], "across")
    start("twin", weight, wall.at[me], "twin")
    start("halo", tokens.at[pl.ds(496, 16)], tok.at[pl.ds(0, 16)], "next")
    for j in range(8):
        columns = pl.ds(pl.multiple_of((2 * j + 1 - core) * 256, 256), 256)
        start(("swap", j), tokens.at[:, columns], others.at[:, pl.ds(j * 256, 256)], "twin")
    arrived("up0")
    pass_on("on0", below, 0, "up")
    arrived("down1")
    pass_on("on1", above, 1, "down")
    start("up1", weight.at[halves[1]], half_of(me, 1), "up")
    start("down0", weight.at[halves[0]], half_of(me, 0), "down")
    for one in loads:
        one.wait()
    arrived("halo", "twin")
    multiply(me, fresh=True)
    arrived("across")
    pass_on("side_up0", side, 0, "up")
    pass_on("side_down1", side, 1, "down")
    hand_over("twin_side", side)
    arrived("on0", "on1")
    start("across_beyond", wall.at[beyond], wall.at[beyond], "across")
    hand_over("twin_beyond", beyond)
    pass_on("side_up1", side, 1, "up")
    pass_on("side_down0", side, 0, "down")
    arrived("twin_side")
    multiply(side)
    arrived("up1")
    hand_over("twin_below", below)
    arrived("down0")
    hand_over("twin_above", above)
    arrived("twin_beyond")
    multiply(beyond)
    arrived("twin_below")
    multiply(below)
    arrived("twin_above")
    multiply(above)
    arrived("side_up0")
    pass_on("twin_sb0", side_below, 0, "twin")
    arrived("side_down1")
    pass_on("twin_sa1", side_above, 1, "twin")
    arrived("across_beyond")
    hand_over("twin_across", side_beyond)
    arrived("twin_across")
    multiply(side_beyond)
    arrived("side_up1")
    pass_on("twin_sb1", side_below, 1, "twin")
    arrived("side_down0")
    pass_on("twin_sa0", side_above, 0, "twin")
    arrived("twin_sb0", "twin_sb1")
    multiply(side_below)
    arrived("twin_sa0", "twin_sa1")
    multiply(side_above)

    def finish(step, carry):
        rows = pl.ds(pl.multiple_of(step * 48, 16), 48)
        projected[rows, :] = acc[rows, :].astype(bf16)
        return carry

    lax.fori_loop(0, 11, finish, 0)
    for j in range(8):
        arrived(("swap", j))
    for store in stored:
        store.wait()
    for copy in sent.values():
        copy.wait_send()


def project(tokens, weight):
    bf16 = jnp.bfloat16
    return pl.pallas_call(
        project_kernel,
        out_shape=(
            jax.ShapeDtypeStruct((528, 1536), bf16),
            jax.ShapeDtypeStruct((N_CTX, 256, 1536), bf16),
            jax.ShapeDtypeStruct((512, 2048), bf16),
        ),
        in_specs=[ANY, ANY],
        out_specs=(IN_VMEM, ANY, ANY),
        scratch_shapes=[
            pltpu.VMEM((528, 4096), bf16),
            pltpu.VMEM((N_CTX, 256, 1536), bf16),
            pltpu.VMEM((528, 1536), jnp.float32),
            pltpu.SemaphoreType.DMA((34,)),
            pltpu.SemaphoreType.DMA((34,)),
            pltpu.SemaphoreType.DMA((10,)),
        ],
        compiler_params=pltpu.CompilerParams(
            collective_id=4, has_side_effects=True, vmem_limit_bytes=48 * 1024 * 1024
        ),
        cost_estimate=pl.CostEstimate(
            flops=2 * 512 * 4096 * 1536, bytes_accessed=24 * 1024 * 1024, transcendentals=0
        ),
    )(tokens, weight)


def short_forward(values, before, taps):
    extended = jnp.concatenate([before, values], axis=2).astype(jnp.float32)
    return (
        taps[0][:, :, None] * extended[:, :, 2:]
        + taps[1][:, :, None] * extended[:, :, 1:-1]
        + taps[2][:, :, None] * extended[:, :, :-2]
    ).astype(jnp.bfloat16)


def on_device(tokens, in_weight, short_taps, long_filter, skip_bias, out_grad):
    f32, bf16 = jnp.float32, jnp.bfloat16
    projected, whole_weight, others = project(tokens, in_weight.reshape(256, 1536))
    whole_weight = whole_weight.reshape(4096, 1536)
    projected = projected.T.reshape(3, 512, 528)
    before = jnp.where(lax.axis_index("ctx") == 0, jnp.zeros((), bf16), projected[:, :, 14:16])
    projected = projected[:, :, 16:]
    streams = short_forward(projected, before, short_taps).astype(f32)
    cotangent = out_grad.astype(f32)
    outgoing = jnp.stack([streams[1] * streams[2], cotangent * streams[0]]).astype(bf16)
    arrived = exchange(outgoing, (2, 32, 8192), rows_of, positions_of, 1)
    filter_grad, result = convolve(arrived, long_filter, skip_bias)
    streams = streams.astype(bf16)
    taps = short_taps.reshape(9, 512).T
    input_grad, weight_grad = gradients(
        result, out_grad, streams[1], streams[2], taps, tokens, others, whole_weight
    )
    return (input_grad, weight_grad.T.reshape(256, 3, 512), filter_grad)


def solution(mesh):
    in_specs = (
        P("ctx", None),
        P("ctx", None, "tp"),
        P(None, None, "tp"),
        P(("tp", "ctx"), None),
        P(("tp", "ctx")),
        P("tp", "ctx"),
    )
    out_specs = (P(("ctx", "tp"), None), P("ctx", None, "tp"), P(("tp", "ctx"), None))
    return jax.shard_map(
        on_device, mesh=mesh, in_specs=in_specs, out_specs=out_specs, check_vma=False
    )
```

```python
import functools
import math

import jax
import jax.numpy as jnp
import numpy as np
from jax import lax
from jax.experimental import pallas as pl
from jax.experimental.pallas import tpu as pltpu
from jax.sharding import PartitionSpec as P

MESH = pl.DeviceIdType.MESH
ANY = pl.BlockSpec(memory_space=pl.ANY)
IN_VMEM = pl.BlockSpec(memory_space=pltpu.VMEM)
N_CTX = 16
LANES = 128
BLOCKS = 64
GROUP = 4


def tables():
    size = 2 * BLOCKS * LANES
    half = np.arange(BLOCKS) + 0.5
    n = np.arange(BLOCKS)
    m = np.arange(LANES)
    theta = 2 * np.pi * half[:, None] * n[None, :] / LANES
    phi = 2 * np.pi * half[:, None] * m[None, :] / size
    psi = 2 * np.pi * (m[:, None] * m[None, :] % LANES) / LANES
    first = np.concatenate([np.cos(theta), -np.sin(theta)], axis=0)
    second = np.block([[np.cos(psi), -np.sin(psi)], [np.sin(psi), np.cos(psi)]])
    second_back = np.block([[np.cos(psi), np.sin(psi)], [-np.sin(psi), np.cos(psi)]])
    first_back = np.concatenate([np.cos(theta).T, -np.sin(theta).T], axis=1)
    low = lambda value: jnp.asarray(value, jnp.bfloat16)
    turn = jnp.asarray(np.stack([np.cos(phi), np.sin(phi)]), jnp.float32)
    return low(first), low(second), low(second_back), low(first_back), turn


def turned(mixed, count, cos, sin):
    result = []
    for index in range(count):
        at = slice(index * LANES, (index + 1) * LANES)
        re, im = mixed[:BLOCKS, at], mixed[BLOCKS:, at]
        both = jnp.concatenate([re * cos + im * sin, im * cos - re * sin], axis=1)
        result.append(both.astype(jnp.bfloat16))
    return jnp.concatenate(result, axis=0)


def unturned(back, count, cos, sin):
    size = 2 * BLOCKS * LANES
    cos, sin = cos * (2.0 / size), sin * (2.0 / size)
    result = []
    for index in range(count):
        rows = slice(index * BLOCKS, (index + 1) * BLOCKS)
        re, im = back[rows, :LANES], back[rows, LANES:]
        both = jnp.concatenate([re * cos - im * sin, im * cos + re * sin], axis=0)
        result.append(both.astype(jnp.bfloat16))
    return jnp.concatenate(result, axis=1)


def places():
    me, b = lax.axis_index("ctx"), lax.axis_index("tp")
    core, xh, y = lax.rem(me, 2), lax.rem(me // 2, 2), me // 4
    z, xl = lax.rem(b, 4), b // 4
    ctx_of = lambda y, xh: (y * 2 + xh) * 2 + core
    return dict(
        core=core,
        xh=xh,
        y=y,
        z=z,
        xl=xl,
        twin={"ctx": me + 1 - 2 * core},
        up={"ctx": ctx_of(lax.rem(y + 1, 4), xh)},
        down={"ctx": ctx_of(lax.rem(y + 3, 4), xh)},
        near={"ctx": me, "tp": (1 - xl) * 4 + z},
        far={"ctx": ctx_of(y, 1 - xh), "tp": (1 - xl) * 4 + z},
        above={"tp": xl * 4 + lax.rem(z + 1, 4)},
        below={"tp": xl * 4 + lax.rem(z + 3, 4)},
    )


def greet(peers):
    barrier = pltpu.get_barrier_semaphore()
    for peer in peers:
        pl.semaphore_signal(barrier, inc=1, device_id=peer, device_id_type=MESH)
    pl.semaphore_wait(barrier, len(peers))


def rows_of(ref, index, group):
    first = pl.multiple_of(index * 32 + group * 16, 16)
    return ref.at[:, pl.ds(first, 16), :]


def positions_of(ref, index, group):
    return ref.at[:, pl.ds(group * 16, 16), pl.ds(pl.multiple_of(index * 512, 512), 512)]


def tail_kernel(
    projected, cotangent, rowtaps, taps, filters, bias, first, second, second_back, first_back,
    turn, tokens, others, weight, ig_out, wg_out, grad,
    tok, oth, wei, keys, values, out, arr, held, fgs,
    ret, cgx, hout, hin, pgc, pgt, pgo, ig, acc, part, xin, r2, rf, xr, z2, zf, xz,
    send, recv, load,
):
    f32, bf16 = jnp.float32, jnp.bfloat16
    at = places()
    core, xh, y, z, xl = at["core"], at["xh"], at["y"], at["z"], at["xl"]
    me = lax.axis_index("ctx")
    at["across"] = {"ctx": (y * 2 + 1 - xh) * 2 + core}
    steps = [(s, i) for s in range(4) for i in range(4)][1:]
    fourth = lax.rem(me, 4)

    def peer_of(s, i):
        return lax.rem(y + s, 4) * 4 + lax.rem(fourth + i, 4)

    for step in steps:
        at[step] = {"ctx": peer_of(*step)}
    at["last"] = {"ctx": lax.rem(me + N_CTX - 1, N_CTX)}
    loads = [
        pltpu.make_async_copy(weight.at[pl.ds(0, 2048)], wei.at[pl.ds(0, 2048)], load.at[0]),
        pltpu.make_async_copy(others, oth, load.at[1]),
        pltpu.make_async_copy(weight.at[pl.ds(2048, 2048)], wei.at[pl.ds(2048, 2048)], load.at[2]),
    ]
    for j in range(8):
        columns = pl.ds(pl.multiple_of((2 * j + core) * 256, 256), 256)
        loads.append(
            pltpu.make_async_copy(
                tokens.at[:, columns], tok.at[:, pl.ds(j * 256, 256)], load.at[3 + j]
            )
        )
    for one in loads:
        one.start()
    greet([at[name] for name in (*steps, "near", "above", "below")])
    sent = {}

    def start(name, src, dst, peer):
        index = len(sent)
        copy = pltpu.make_async_remote_copy(
            src_ref=src,
            dst_ref=dst,
            send_sem=send.at[index],
            recv_sem=recv.at[index],
            device_id=at[peer],
            device_id_type=MESH,
        )
        copy.start()
        sent[name] = copy

    def arrived(*names):
        for name in names:
            sent[name].wait_recv()

    def head(x):
        edge = x[0:16]
        return jnp.concatenate([jnp.where(me == 0, jnp.zeros_like(edge), edge), x[16:]], axis=0)

    def filtered(p, chunk):
        columns = pl.ds(pl.multiple_of(p * 512 + chunk * 128, 128), 128)
        own = pl.ds(pl.multiple_of(chunk * 128, 128), 128)
        x = head(projected[:, columns].astype(f32))
        total = rowtaps[p : p + 1, own] * x
        for j in (1, 2):
            total = total + rowtaps[3 * j + p : 3 * j + p + 1, own] * pltpu.roll(x, j, 0)
        return total[16:].astype(bf16).T

    def start_out(step, group):
        peer = peer_of(*step)
        start(("out", step, group), rows_of(out, peer, group), positions_of(arr, me, group), step)

    for s in range(4):
        chunk = lax.rem(y + s, 4)
        rows = pl.ds(pl.multiple_of(chunk * 128, 128), 128)
        query, key, value = (filtered(p, chunk) for p in range(3))
        keys[rows, :] = key
        values[rows, :] = value
        out[0, rows, :] = (key.astype(f32) * value.astype(f32)).astype(bf16)
        out[1, rows, :] = (cotangent[rows, :].astype(f32) * query.astype(f32)).astype(bf16)
        for step in steps:
            if step[0] == s:
                start_out(step, 0)
    for step in steps:
        start_out(step, 1)
    kept = []
    for group in range(2):
        copy = pltpu.make_async_copy(
            rows_of(out, me, group), positions_of(arr, me, group), load.at[11 + group]
        )
        copy.start()
        kept.append(copy)

    def dot(a, b):
        return jnp.dot(a, b, preferred_element_type=f32)

    def channel(index):
        return pl.ds(index, BLOCKS, stride=32)

    def block(n):
        return slice(n * LANES, (n + 1) * LANES)

    for n in range(BLOCKS):
        held[2, n * 32 : (n + 1) * 32, :] = filters[:, block(n)]

    def filter_spectra(step, carry):
        signals = [held[2, channel(step * 8 + j), :].astype(bf16) for j in range(8)]
        mixed = dot(first[...], jnp.concatenate(signals, axis=1))
        rows = pl.ds(pl.multiple_of(step * 512, 512), 512)
        acc[rows, :] = dot(turned(mixed, 8, turn[0], turn[1]), second[...])
        return carry

    lax.fori_loop(0, 4, filter_spectra, 0)

    def both_ways(start_at, step, carry):
        index = start_at + step * 4
        signals = [held[s, channel(index + j), :].astype(bf16) for j in range(4) for s in range(2)]
        mixed = dot(first[...], jnp.concatenate(signals, axis=1))
        spectra = dot(turned(mixed, 8, turn[0], turn[1]), second[...])
        rows = pl.ds(pl.multiple_of(index * 64, 256), 256)
        filt = acc[rows, :]
        joined, kept = [], []
        for j in range(4):
            parts = []
            for value in (
                spectra[j * 128 : j * 128 + 64],
                spectra[j * 128 + 64 : j * 128 + 128],
                filt[j * 64 : j * 64 + 64],
            ):
                parts.append((value[:, :LANES], value[:, LANES:]))
            (pr, pi), (wr, wi), (hr, hi) = parts
            joined.append(jnp.concatenate([pr * hr - pi * hi, pr * hi + pi * hr], axis=1))
            joined.append(jnp.concatenate([hr * wr + hi * wi, hr * wi - hi * wr], axis=1))
            kept.append(jnp.concatenate([pr * wr + pi * wi, pr * wi - pi * wr], axis=1))
        fgs[rows, :] = jnp.concatenate(kept, axis=0).astype(bf16)
        back = dot(jnp.concatenate(joined, axis=0).astype(bf16), second_back[...])
        final = dot(first_back[...], unturned(back, 8, turn[0], turn[1]))
        for j in range(4):
            for s in range(2):
                held[s, channel(index + j), :] = final[:, block(2 * j + s)]
        return carry

    for group in range(2):
        arrived(*(("out", step, group) for step in steps))
        kept[group].wait()
        own = slice(group * 16, group * 16 + 16)
        for n in range(BLOCKS):
            for s in range(2):
                rows = slice(n * 32 + group * 16, n * 32 + group * 16 + 16)
                held[s, rows, :] = arr[s, own, block(n)].astype(f32)
        lax.fori_loop(0, 4, functools.partial(both_ways, group * 16), 0)
        gain = bias[own, :]
        for n in range(BLOCKS):
            for s in range(2):
                rows = slice(n * 32 + group * 16, n * 32 + group * 16 + 16)
                direct = gain * arr[s, own, block(n)].astype(f32)
                arr[s, own, block(n)] = (held[s, rows, :] + direct).astype(bf16)
        for step in steps:
            src = positions_of(arr, peer_of(*step), group)
            start(("back", step, group), src, rows_of(ret, me, group), step)
        copy = pltpu.make_async_copy(
            positions_of(arr, me, group), rows_of(ret, me, group), load.at[13 + group]
        )
        copy.start()
        kept.append(copy)

    def filter_grads(step, carry):
        rows = pl.ds(pl.multiple_of(step * 512, 512), 512)
        back = dot(fgs[rows, :], second_back[...])
        final = dot(first_back[...], unturned(back, 8, turn[0], turn[1]))
        for j in range(8):
            held[2, channel(step * 8 + j), :] = final[:, block(j)]
        return carry

    lax.fori_loop(0, 4, filter_grads, 0)
    for n in range(BLOCKS):
        grad[:, block(n)] = held[2, n * 32 : (n + 1) * 32, :]
    for group in range(2):
        arrived(*(("back", step, group) for step in steps))
        kept[2 + group].wait()

    def lanes(p, chunk):
        return pl.ds(pl.multiple_of(p * 512 + chunk * 128, 128), 128)

    def stream_grads(chunk, carry):
        rows = pl.ds(pl.multiple_of(chunk * 128, 128), 128)
        one, two = ret[0, rows, :].astype(f32), ret[1, rows, :].astype(f32)
        factors = ((one, cotangent), (two, values), (two, keys))
        for p, (value, factor) in enumerate(factors):
            grad = (value * factor[rows, :].astype(f32)).astype(bf16)
            cgx[p, rows, 0:512] = grad
            hout[:, lanes(p, chunk)] = grad[:, 0:128].T[0:16, :]
        return carry

    lax.fori_loop(0, 4, stream_grads, 0)
    start("halo", hout, hin, "last")

    def tapped(p, rows, first, width, kept):
        x = cgx[p, rows, first : first + width].astype(f32)
        total = taps[rows, p : p + 1] * x
        for j in (1, 2):
            total = total + taps[rows, 3 * j + p : 3 * j + p + 1] * pltpu.roll(x, width - j, 1)
        return total[:, :kept].astype(bf16)

    def front(chunk, carry):
        rows = pl.ds(pl.multiple_of(chunk * 128, 128), 128)
        for p in range(3):
            grad = tapped(p, rows, 0, 512, 384)
            pgc[lanes(p, chunk), 0:384] = grad
            pgt[0:384, lanes(p, chunk)] = grad.T
        return carry

    lax.fori_loop(0, 4, front, 0)
    start("twin0", pgc.at[:, pl.ds(0, 384)], pgo.at[:, pl.ds(0, 384)], "twin")
    arrived("halo")

    def rest(chunk, carry):
        rows = pl.ds(pl.multiple_of(chunk * 128, 128), 128)
        for p in range(3):
            first = hin[:, lanes(p, chunk)].astype(f32)
            first = jnp.where(me == N_CTX - 1, jnp.zeros_like(first), first)
            first = jnp.concatenate([first, jnp.zeros((112, 128), f32)], axis=0)
            cgx[p, rows, 512:640] = first.T.astype(bf16)
            grad = tapped(p, rows, 384, 256, 128)
            pgc[lanes(p, chunk), 384:512] = grad
            pgt[384:512, lanes(p, chunk)] = grad.T
        return carry

    lax.fori_loop(0, 4, rest, 0)
    start("twin1", pgc.at[:, pl.ds(384, 128)], pgo.at[:, pl.ds(384, 128)], "twin")

    def input_tiles(first):
        def tile(step, carry):
            rows = pl.ds(pl.multiple_of((first + step) * 512, 512), 512)
            ig[:, rows] = lax.dot_general(
                pgt[...], wei[rows, :], (((1,), (1,)), ((), ())), preferred_element_type=f32
            ).astype(bf16)
            return carry

        lax.fori_loop(0, 4, tile, 0)

    def acc_rows(slot, row, count):
        return pl.ds(pl.multiple_of(slot * 1536 + row, 128), count)

    def weight_part(slot, block):
        columns = pl.ds(pl.multiple_of(block * 256, 256), 256)

        def half(step, carry):
            rows = pl.ds(pl.multiple_of(step * 768, 256), 768)
            value = dot(pgc[rows, :], tok[:, columns]) + dot(pgo[rows, :], oth[:, columns])
            acc[acc_rows(slot, step * 768, 768), :] = value
            return carry

        lax.fori_loop(0, 2, half, 0)

    def fold(dst, slot, first, last, *terms):
        def chunk(step, carry):
            rows = pl.ds(pl.multiple_of(step * 128, 128), 128)
            total = acc[acc_rows(slot, step * 128, 128), :]
            for term, offset in terms:
                part_rows = pl.ds(pl.multiple_of(step * 128 - offset, 128), 128)
                total = total + term[part_rows, :].astype(f32)
            dst[rows, :] = total.astype(bf16)
            return carry

        lax.fori_loop(first // 128, last // 128, chunk, 0)

    def block_of(y, xh):
        return y * 2 + xh

    y2, yp, ym = lax.rem(y + 2, 4), lax.rem(y + 1, 4), lax.rem(y + 3, 4)
    ztwo, zp, zm = lax.rem(z + 2, 4), lax.rem(z + 1, 4), lax.rem(z + 3, 4)
    xo = 1 - xh
    sides = (1 - xl, xl)
    low, high = pl.ds(0, 768), pl.ds(768, 768)
    parts = (slice(0, 2048), slice(2048, 4096))

    def ig_rows(side, z, first, count):
        return pl.ds(pl.multiple_of((side * 4 + z) * 64 + first, 32), count)

    def ig_add(rows, h, *terms):
        total = ig[rows, parts[h]].astype(f32)
        for term in terms:
            total = total + term[...].astype(f32)
        return total.astype(bf16)

    def z_first(h):
        for k in range(2):
            src = ig.at[ig_rows(sides[k], ztwo, 0, 32), parts[h]]
            start(("z2p", h, k), src, z2.at[h, k, 0], "above")
            src = ig.at[ig_rows(sides[k], ztwo, 32, 32), parts[h]]
            start(("z2m", h, k), src, z2.at[h, k, 1], "below")

    def z_second(h):
        for k in range(2):
            arrived(("z2p", h, k))
            rows = ig_rows(sides[k], zp, 0, 32)
            ig[rows, parts[h]] = ig_add(rows, h, z2.at[h, k, 0])
            src = ig.at[ig_rows(sides[k], zp, 0, 64), parts[h]]
            start(("zfp", h, k), src, zf.at[h, k, 0], "above")
            arrived(("z2m", h, k))
            rows = ig_rows(sides[k], zm, 32, 32)
            ig[rows, parts[h]] = ig_add(rows, h, z2.at[h, k, 1])
            src = ig.at[ig_rows(sides[k], zm, 0, 64), parts[h]]
            start(("zfm", h, k), src, zf.at[h, k, 1], "below")

    def z_across(h):
        arrived(("zfp", h, 0), ("zfm", h, 0))
        rows = ig_rows(sides[0], z, 0, 64)
        ig[rows, parts[h]] = ig_add(rows, h, zf.at[h, 0, 0], zf.at[h, 0, 1])
        start(("xz", h), ig.at[rows, parts[h]], xz.at[h], "near")

    def z_last(h):
        arrived(("zfp", h, 1), ("zfm", h, 1), ("xz", h))
        rows = ig_rows(sides[1], z, 0, 64)
        ig_out[:, parts[h]] = ig_add(rows, h, zf.at[h, 1, 0], zf.at[h, 1, 1], xz.at[h])

    loads[0].wait()
    input_tiles(0)
    z_first(0)
    for one in (loads[1], *loads[3:]):
        one.wait()
    arrived("twin0", "twin1")
    weight_part(0, block_of(y2, xo))
    fold(part.at[0], 0, 0, 1536)
    start("across0", part.at[0], xin, "across")
    weight_part(0, block_of(yp, xo))
    fold(part.at[1], 0, 0, 1536)
    start("up0", part.at[1], rf.at[0, 0], "up")
    weight_part(0, block_of(ym, xo))
    fold(part.at[2], 0, 0, 1536)
    start("down0", part.at[2], rf.at[0, 1], "down")
    loads[2].wait()
    input_tiles(4)
    z_first(1)
    z_second(0)
    weight_part(1, block_of(yp, xh))
    weight_part(2, block_of(ym, xh))
    z_second(1)
    weight_part(0, block_of(y2, xh))
    arrived("across0")
    fold(part.at[3], 0, 0, 1536, (xin, 0))
    start("up2", part.at[3, low], r2.at[0], "up")
    start("down2", part.at[3, high], r2.at[1], "down")
    weight_part(0, block_of(y, xo))
    arrived("up0", "down0")
    sent["across0"].wait_send()
    fold(part.at[0], 0, 0, 1536, (rf.at[0, 0], 0), (rf.at[0, 1], 0))
    start("across1", part.at[0], xr, "across")
    fold(part.at[4], 1, 768, 1536)
    start("up1b", part.at[4, high], rf.at[1, 0, high], "up")
    fold(part.at[5], 2, 0, 768)
    start("down1a", part.at[5, low], rf.at[1, 1, low], "down")
    weight_part(0, block_of(y, xh))
    z_across(0)
    z_across(1)
    arrived("up2")
    fold(part.at[4], 1, 0, 768, (r2.at[0], 0))
    start("up1a", part.at[4, low], rf.at[1, 0, low], "up")
    arrived("down2")
    fold(part.at[5], 2, 768, 1536, (r2.at[1], 768))
    start("down1b", part.at[5, high], rf.at[1, 1, high], "down")
    z_last(0)
    z_last(1)
    arrived("across1", "up1a", "up1b", "down1a", "down1b")
    fold(wg_out, 0, 0, 1536, (rf.at[1, 0], 0), (rf.at[1, 1], 0), (xr, 0))
    for name, copy in sent.items():
        if name != "across0":
            copy.wait_send()


def gradients(projected, out_grad, short_taps, long_filter, skip_bias, tokens, others, weight):
    bf16, f32 = jnp.bfloat16, jnp.float32
    vmem = lambda *shape: pltpu.VMEM(shape, bf16)
    rowtaps = short_taps.reshape(9, 512)
    bias = jnp.broadcast_to(skip_bias[:, None], (32, LANES))
    return pl.pallas_call(
        tail_kernel,
        out_shape=(
            jax.ShapeDtypeStruct((64, 4096), bf16),
            jax.ShapeDtypeStruct((1536, 256), bf16),
            jax.ShapeDtypeStruct((32, BLOCKS * LANES), f32),
        ),
        in_specs=[IN_VMEM] * 11 + [ANY] * 3,
        out_specs=(IN_VMEM,) * 3,
        scratch_shapes=[
            vmem(512, 2048),
            vmem(512, 2048),
            vmem(4096, 1536),
            vmem(512, 512),
            vmem(512, 512),
            vmem(2, 512, 512),
            vmem(2, 32, BLOCKS * LANES),
            pltpu.VMEM((3, 32 * BLOCKS, LANES), f32),
            vmem(32 * BLOCKS, 2 * LANES),
            vmem(2, 512, 512),
            vmem(3, 512, 640),
            vmem(16, 1536),
            vmem(16, 1536),
            vmem(1536, 512),
            vmem(512, 1536),
            vmem(1536, 512),
            vmem(512, 4096),
            pltpu.VMEM((4608, 256), f32),
            vmem(6, 1536, 256),
            vmem(1536, 256),
            vmem(2, 768, 256),
            vmem(2, 2, 1536, 256),
            vmem(1536, 256),
            vmem(2, 2, 2, 32, 2048),
            vmem(2, 2, 2, 64, 2048),
            vmem(2, 64, 2048),
            pltpu.SemaphoreType.DMA((91,)),
            pltpu.SemaphoreType.DMA((91,)),
            pltpu.SemaphoreType.DMA((15,)),
        ],
        compiler_params=pltpu.CompilerParams(
            collective_id=3, has_side_effects=True, vmem_limit_bytes=62 * 1024 * 1024
        ),
        cost_estimate=pl.CostEstimate(
            flops=4 * 512 * 4096 * 1536, bytes_accessed=24 * 1024 * 1024, transcendentals=0
        ),
    )(
        projected, out_grad, rowtaps, rowtaps.T, long_filter, bias, *tables(), tokens, others, weight
    )


def project_kernel(tokens, weight, projected, whole, others, tok, wall, acc, send, recv, load):
    f32, bf16 = jnp.float32, jnp.bfloat16
    at = places()
    core, xh, y = at["core"], at["xh"], at["y"]
    me = lax.axis_index("ctx")
    at["across"] = {"ctx": (y * 2 + 1 - xh) * 2 + core}
    at["next"] = {"ctx": lax.rem(me + 1, N_CTX)}
    at["last"] = {"ctx": lax.rem(me + N_CTX - 1, N_CTX)}
    loads = [
        pltpu.make_async_copy(weight, wall.at[me], load.at[0]),
        pltpu.make_async_copy(tokens, tok.at[pl.ds(16, 512)], load.at[1]),
    ]
    for one in loads:
        one.start()
    greet([at[name] for name in ("twin", "up", "down", "across", "next", "last")])
    sent = {}

    def start(name, src, dst, peer):
        index = len(sent)
        copy = pltpu.make_async_remote_copy(
            src_ref=src,
            dst_ref=dst,
            send_sem=send.at[index],
            recv_sem=recv.at[index],
            device_id=at[peer],
            device_id_type=MESH,
        )
        copy.start()
        sent[name] = copy

    def arrived(*names):
        for name in names:
            sent[name].wait_recv()

    halves = (pl.ds(0, 128), pl.ds(128, 128))

    def half_of(index, half):
        return wall.at[index, halves[half]]

    def pass_on(name, index, half, peer):
        start(name, half_of(index, half), half_of(index, half), peer)

    def hand_over(name, index):
        start(name, wall.at[index], wall.at[index], "twin")

    stored = []

    def multiply(index, fresh=False):
        pair = index // 2
        columns = pl.ds(pl.multiple_of(pair * 512, 512), 512)
        store = pltpu.make_async_copy(
            wall.at[pl.ds(pair * 2, 2)], whole.at[pl.ds(pair * 2, 2)], load.at[2 + len(stored)]
        )
        store.start()
        stored.append(store)

        def tile(step, carry):
            place = pl.ds(pl.multiple_of(step * 512, 512), 512)
            value = jnp.dot(
                tok[:, columns],
                wall[pl.ds(pair * 2, 2), :, place].reshape(512, 512),
                preferred_element_type=f32,
            )
            acc[:, place] = value if fresh else acc[:, place] + value
            return carry

        lax.fori_loop(0, 3, tile, 0)

    def ctx_of(y, xh):
        return (lax.rem(y, 4) * 2 + xh) * 2 + core

    below, above, beyond = ctx_of(y + 3, xh), ctx_of(y + 1, xh), ctx_of(y + 2, xh)
    side = ctx_of(y, 1 - xh)
    side_below, side_above = ctx_of(y + 3, 1 - xh), ctx_of(y + 1, 1 - xh)
    side_beyond = ctx_of(y + 2, 1 - xh)

    start("up0", weight.at[halves[0]], half_of(me, 0), "up")
    start("down1", weight.at[halves[1]], half_of(me, 1), "down")
    start("across", weight, wall.at[me], "across")
    start("twin", weight, wall.at[me], "twin")
    start("halo", tokens.at[pl.ds(496, 16)], tok.at[pl.ds(0, 16)], "next")
    for j in range(8):
        columns = pl.ds(pl.multiple_of((2 * j + 1 - core) * 256, 256), 256)
        start(("swap", j), tokens.at[:, columns], others.at[:, pl.ds(j * 256, 256)], "twin")
    arrived("up0")
    pass_on("on0", below, 0, "up")
    arrived("down1")
    pass_on("on1", above, 1, "down")
    start("up1", weight.at[halves[1]], half_of(me, 1), "up")
    start("down0", weight.at[halves[0]], half_of(me, 0), "down")
    for one in loads:
        one.wait()
    arrived("halo", "twin")
    multiply(me, fresh=True)
    arrived("across")
    pass_on("side_up0", side, 0, "up")
    pass_on("side_down1", side, 1, "down")
    hand_over("twin_side", side)
    arrived("on0", "on1")
    start("across_beyond", wall.at[beyond], wall.at[beyond], "across")
    hand_over("twin_beyond", beyond)
    pass_on("side_up1", side, 1, "up")
    pass_on("side_down0", side, 0, "down")
    arrived("twin_side")
    multiply(side)
    arrived("up1")
    hand_over("twin_below", below)
    arrived("down0")
    hand_over("twin_above", above)
    arrived("twin_beyond")
    multiply(beyond)
    arrived("twin_below")
    multiply(below)
    arrived("twin_above")
    multiply(above)
    arrived("side_up0")
    pass_on("twin_sb0", side_below, 0, "twin")
    arrived("side_down1")
    pass_on("twin_sa1", side_above, 1, "twin")
    arrived("across_beyond")
    hand_over("twin_across", side_beyond)
    arrived("twin_across")
    multiply(side_beyond)
    arrived("side_up1")
    pass_on("twin_sb1", side_below, 1, "twin")
    arrived("side_down0")
    pass_on("twin_sa0", side_above, 0, "twin")
    arrived("twin_sb0", "twin_sb1")
    multiply(side_below)
    arrived("twin_sa0", "twin_sa1")
    multiply(side_above)

    def finish(step, carry):
        rows = pl.ds(pl.multiple_of(step * 48, 16), 48)
        projected[rows, :] = acc[rows, :].astype(bf16)
        return carry

    lax.fori_loop(0, 11, finish, 0)
    for j in range(8):
        arrived(("swap", j))
    for store in stored:
        store.wait()
    for copy in sent.values():
        copy.wait_send()


def project(tokens, weight):
    bf16 = jnp.bfloat16
    return pl.pallas_call(
        project_kernel,
        out_shape=(
            jax.ShapeDtypeStruct((528, 1536), bf16),
            jax.ShapeDtypeStruct((N_CTX, 256, 1536), bf16),
            jax.ShapeDtypeStruct((512, 2048), bf16),
        ),
        in_specs=[ANY, ANY],
        out_specs=(IN_VMEM, ANY, ANY),
        scratch_shapes=[
            pltpu.VMEM((528, 4096), bf16),
            pltpu.VMEM((N_CTX, 256, 1536), bf16),
            pltpu.VMEM((528, 1536), jnp.float32),
            pltpu.SemaphoreType.DMA((34,)),
            pltpu.SemaphoreType.DMA((34,)),
            pltpu.SemaphoreType.DMA((10,)),
        ],
        compiler_params=pltpu.CompilerParams(
            collective_id=4, has_side_effects=True, vmem_limit_bytes=48 * 1024 * 1024
        ),
        cost_estimate=pl.CostEstimate(
            flops=2 * 512 * 4096 * 1536, bytes_accessed=24 * 1024 * 1024, transcendentals=0
        ),
    )(tokens, weight)


def on_device(tokens, in_weight, short_taps, long_filter, skip_bias, out_grad):
    projected, whole_weight, others = project(tokens, in_weight.reshape(256, 1536))
    input_grad, weight_grad, filter_grad = gradients(
        projected,
        out_grad,
        short_taps,
        long_filter,
        skip_bias,
        tokens,
        others,
        whole_weight.reshape(4096, 1536),
    )
    return (input_grad, weight_grad.T.reshape(256, 3, 512), filter_grad)


def solution(mesh):
    in_specs = (
        P("ctx", None),
        P("ctx", None, "tp"),
        P(None, None, "tp"),
        P(("tp", "ctx"), None),
        P(("tp", "ctx")),
        P("tp", "ctx"),
    )
    out_specs = (P(("ctx", "tp"), None), P("ctx", None, "tp"), P(("tp", "ctx"), None))
    return jax.shard_map(
        on_device, mesh=mesh, in_specs=in_specs, out_specs=out_specs, check_vma=False
    )
```

```python
import functools
import math

import jax
import jax.numpy as jnp
import numpy as np
from jax import lax
from jax.experimental import pallas as pl
from jax.experimental.pallas import tpu as pltpu
from jax.sharding import PartitionSpec as P

MESH = pl.DeviceIdType.MESH
ANY = pl.BlockSpec(memory_space=pl.ANY)
IN_VMEM = pl.BlockSpec(memory_space=pltpu.VMEM)
N_CTX = 16
LANES = 128
BLOCKS = 64
GROUP = 4


def tables():
    size = 2 * BLOCKS * LANES
    half = np.arange(BLOCKS) + 0.5
    n = np.arange(BLOCKS)
    m = np.arange(LANES)
    theta = 2 * np.pi * half[:, None] * n[None, :] / LANES
    phi = 2 * np.pi * half[:, None] * m[None, :] / size
    psi = 2 * np.pi * (m[:, None] * m[None, :] % LANES) / LANES
    first = np.concatenate([np.cos(theta), -np.sin(theta)], axis=0)
    second = np.block([[np.cos(psi), -np.sin(psi)], [np.sin(psi), np.cos(psi)]])
    second_back = np.block([[np.cos(psi), np.sin(psi)], [-np.sin(psi), np.cos(psi)]])
    first_back = np.concatenate([np.cos(theta).T, -np.sin(theta).T], axis=1)
    low = lambda value: jnp.asarray(value, jnp.bfloat16)
    turn = jnp.asarray(np.stack([np.cos(phi), np.sin(phi)]), jnp.float32)
    return low(first), low(second), low(second_back), low(first_back), turn


def turned(mixed, count, cos, sin):
    result = []
    for index in range(count):
        at = slice(index * LANES, (index + 1) * LANES)
        re, im = mixed[:BLOCKS, at], mixed[BLOCKS:, at]
        both = jnp.concatenate([re * cos + im * sin, im * cos - re * sin], axis=1)
        result.append(both.astype(jnp.bfloat16))
    return jnp.concatenate(result, axis=0)


def unturned(back, count, cos, sin):
    size = 2 * BLOCKS * LANES
    cos, sin = cos * (2.0 / size), sin * (2.0 / size)
    result = []
    for index in range(count):
        rows = slice(index * BLOCKS, (index + 1) * BLOCKS)
        re, im = back[rows, :LANES], back[rows, LANES:]
        both = jnp.concatenate([re * cos - im * sin, im * cos + re * sin], axis=0)
        result.append(both.astype(jnp.bfloat16))
    return jnp.concatenate(result, axis=1)


def places():
    me, b = lax.axis_index("ctx"), lax.axis_index("tp")
    core, xh, y = lax.rem(me, 2), lax.rem(me // 2, 2), me // 4
    z, xl = lax.rem(b, 4), b // 4
    ctx_of = lambda y, xh: (y * 2 + xh) * 2 + core
    return dict(
        core=core,
        xh=xh,
        y=y,
        z=z,
        xl=xl,
        twin={"ctx": me + 1 - 2 * core},
        up={"ctx": ctx_of(lax.rem(y + 1, 4), xh)},
        down={"ctx": ctx_of(lax.rem(y + 3, 4), xh)},
        near={"ctx": me, "tp": (1 - xl) * 4 + z},
        far={"ctx": ctx_of(y, 1 - xh), "tp": (1 - xl) * 4 + z},
        above={"tp": xl * 4 + lax.rem(z + 1, 4)},
        below={"tp": xl * 4 + lax.rem(z + 3, 4)},
    )


def greet(peers):
    barrier = pltpu.get_barrier_semaphore()
    for peer in peers:
        pl.semaphore_signal(barrier, inc=1, device_id=peer, device_id_type=MESH)
    pl.semaphore_wait(barrier, len(peers))


def rows_of(ref, index, group):
    first = pl.multiple_of(index * 32 + group * 16, 16)
    return ref.at[:, pl.ds(first, 16), :]


def positions_of(ref, index, group):
    return ref.at[:, pl.ds(group * 16, 16), pl.ds(pl.multiple_of(index * 512, 512), 512)]


def mixer_kernel(
    tokens, weight, cotangent_in, taps_in, filters_in, bias_in, first_in, second_in,
    second_back_in, first_back_in, turn_in, ig_out, wg_out, grad,
    tok, oth, wall, cotangent, taps, coltaps, filters, bias, gains, first, second, second_back, first_back,
    turn, keys, values, out, arr, held, fgs, ret, cgx, hout, hin, pgc, pgt, pgo, ig, acc, part,
    xin, r2, rf, xr, z2, zf, xz, send, recv, load,
):
    f32, bf16 = jnp.float32, jnp.bfloat16
    at = places()
    core, xh, y, z, xl = at["core"], at["xh"], at["y"], at["z"], at["xl"]
    me = lax.axis_index("ctx")
    at["across"] = {"ctx": (y * 2 + 1 - xh) * 2 + core}
    at["next"] = {"ctx": lax.rem(me + 1, N_CTX)}
    steps = [(s, i) for s in range(4) for i in range(4)][1:]
    fourth = lax.rem(me, 4)

    def peer_of(s, i):
        return lax.rem(y + s, 4) * 4 + lax.rem(fourth + i, 4)

    for step in steps:
        at[step] = {"ctx": peer_of(*step)}
    at["last"] = {"ctx": lax.rem(me + N_CTX - 1, N_CTX)}
    fetched = [
        (weight, wall.at[me]),
        (tokens, tok.at[pl.ds(16, 512)]),
        (cotangent_in, cotangent),
        (taps_in, taps),
        (filters_in, filters),
        (bias_in, bias),
        (first_in, first),
        (second_in, second),
        (second_back_in, second_back),
        (first_back_in, first_back),
        (turn_in, turn),
    ]
    loads = [
        pltpu.make_async_copy(src, dst, load.at[index]) for index, (src, dst) in enumerate(fetched)
    ]
    for one in loads:
        one.start()
    greet([at[name] for name in (*steps, "near", "above", "below")])
    sent = {}

    def start(name, src, dst, peer):
        index = len(sent)
        copy = pltpu.make_async_remote_copy(
            src_ref=src,
            dst_ref=dst,
            send_sem=send.at[index],
            recv_sem=recv.at[index],
            device_id=at[peer],
            device_id_type=MESH,
        )
        copy.start()
        sent[name] = copy

    def arrived(*names):
        for name in names:
            sent[name].wait_recv()

    halves = (pl.ds(0, 128), pl.ds(128, 128))

    def half_of(index, half):
        return wall.at[index, halves[half]]

    def pass_on(name, index, half, peer):
        start(name, half_of(index, half), half_of(index, half), peer)

    def hand_over(name, index):
        start(name, wall.at[index], wall.at[index], "twin")

    def multiply(index, fresh=False):
        pair = index // 2
        columns = pl.ds(pl.multiple_of(pair * 512, 512), 512)

        def tile(step, carry):
            place = pl.ds(pl.multiple_of(step * 512, 512), 512)
            value = jnp.dot(
                tok[:, columns],
                wall[pl.ds(pair * 2, 2), :, place].reshape(512, 512),
                preferred_element_type=f32,
            )
            for half in range(2):
                rows = pl.ds(pl.multiple_of(step * 1056 + half * 528, 16), 528)
                piece = value[:, half * 256 : half * 256 + 256]
                acc[rows, :] = piece if fresh else acc[rows, :] + piece
            return carry

        lax.fori_loop(0, 3, tile, 0)

    def ctx_of(y, xh):
        return (lax.rem(y, 4) * 2 + xh) * 2 + core

    below, above, beyond = ctx_of(y + 3, xh), ctx_of(y + 1, xh), ctx_of(y + 2, xh)
    side = ctx_of(y, 1 - xh)
    side_below, side_above = ctx_of(y + 3, 1 - xh), ctx_of(y + 1, 1 - xh)
    side_beyond = ctx_of(y + 2, 1 - xh)

    start("w_up0", weight.at[halves[0]], half_of(me, 0), "up")
    start("w_down1", weight.at[halves[1]], half_of(me, 1), "down")
    start("w_across", weight, wall.at[me], "across")
    start("w_twin", weight, wall.at[me], "twin")
    start("w_halo", tokens.at[pl.ds(496, 16)], tok.at[pl.ds(0, 16)], "next")
    for j in range(8):
        columns = pl.ds(pl.multiple_of((2 * j + 1 - core) * 256, 256), 256)
        start(("swap", j), tokens.at[:, columns], oth.at[:, pl.ds(j * 256, 256)], "twin")
    arrived("w_up0")
    pass_on("w_on0", below, 0, "up")
    arrived("w_down1")
    pass_on("w_on1", above, 1, "down")
    start("w_up1", weight.at[halves[1]], half_of(me, 1), "up")
    start("w_down0", weight.at[halves[0]], half_of(me, 0), "down")
    for one in loads:
        one.wait()
    arrived("w_halo", "w_twin")
    multiply(me, fresh=True)
    arrived("w_across")
    pass_on("w_side_up0", side, 0, "up")
    pass_on("w_side_down1", side, 1, "down")
    hand_over("w_twin_side", side)
    arrived("w_on0", "w_on1")
    start("w_across_beyond", wall.at[beyond], wall.at[beyond], "across")
    hand_over("w_twin_beyond", beyond)
    pass_on("w_side_up1", side, 1, "up")
    pass_on("w_side_down0", side, 0, "down")
    arrived("w_twin_side")
    multiply(side)
    arrived("w_up1")
    hand_over("w_twin_below", below)
    arrived("w_down0")
    hand_over("w_twin_above", above)
    arrived("w_twin_beyond")
    multiply(beyond)
    arrived("w_twin_below")
    multiply(below)
    arrived("w_twin_above")
    multiply(above)
    arrived("w_side_up0")
    pass_on("w_twin_sb0", side_below, 0, "twin")
    arrived("w_side_down1")
    pass_on("w_twin_sa1", side_above, 1, "twin")
    arrived("w_across_beyond")
    hand_over("w_twin_across", side_beyond)
    arrived("w_twin_across")
    multiply(side_beyond)
    arrived("w_side_up1")
    pass_on("w_twin_sb1", side_below, 1, "twin")
    arrived("w_side_down0")
    pass_on("w_twin_sa0", side_above, 0, "twin")
    arrived("w_twin_sb0", "w_twin_sb1")
    multiply(side_below)
    arrived("w_twin_sa0", "w_twin_sa1")
    multiply(side_above)

    for j in range(8):
        arrived(("swap", j))
    coltaps[...] = jnp.concatenate([taps[0], taps[1], taps[2], jnp.zeros((7, 512), f32)], axis=0).T
    diagonal = lax.broadcasted_iota(jnp.int32, (32, 32), 0) == lax.broadcasted_iota(
        jnp.int32, (32, 32), 1
    )
    gain = jnp.where(diagonal, jnp.broadcast_to(bias[...], (32, 32)), 0.0)
    gains[...] = jnp.broadcast_to(jnp.sum(gain, axis=1, keepdims=True), (32, LANES))

    def head(x):
        edge = x[0:16]
        return jnp.concatenate([jnp.where(me == 0, jnp.zeros_like(edge), edge), x[16:]], axis=0)

    def filtered(p, chunk):
        rows = pl.ds(pl.multiple_of((p * 2 + chunk // 2) * 528, 16), 528)
        columns = pl.ds(pl.multiple_of(lax.rem(chunk, 2) * 128, 128), 128)
        own = pl.ds(pl.multiple_of(chunk * 128, 128), 128)
        x = head(acc[rows, columns].astype(bf16).astype(f32))
        total = taps[0, p : p + 1, own] * x
        for j in (1, 2):
            total = total + taps[j, p : p + 1, own] * pltpu.roll(x, j, 0)
        return total[16:].astype(bf16).T

    def start_out(step, group):
        peer = peer_of(*step)
        start(("out", step, group), rows_of(out, peer, group), positions_of(arr, me, group), step)

    for s in range(4):
        chunk = lax.rem(y + s, 4)
        rows = pl.ds(pl.multiple_of(chunk * 128, 128), 128)
        query, key, value = (filtered(p, chunk) for p in range(3))
        keys[rows, :] = key
        values[rows, :] = value
        out[0, rows, :] = (key.astype(f32) * value.astype(f32)).astype(bf16)
        out[1, rows, :] = (cotangent[rows, :].astype(f32) * query.astype(f32)).astype(bf16)
        for step in steps:
            if step[0] == s:
                start_out(step, 0)
    for step in steps:
        start_out(step, 1)
    kept = []
    for group in range(2):
        copy = pltpu.make_async_copy(
            rows_of(out, me, group), positions_of(arr, me, group), load.at[11 + group]
        )
        copy.start()
        kept.append(copy)

    def dot(a, b):
        return jnp.dot(a, b, preferred_element_type=f32)

    def channel(index):
        return pl.ds(index, BLOCKS, stride=32)

    def block(n):
        return slice(n * LANES, (n + 1) * LANES)

    for n in range(BLOCKS):
        held[2, n * 32 : (n + 1) * 32, :] = filters[:, block(n)]

    def filter_spectra(step, carry):
        signals = [held[2, channel(step * 8 + j), :].astype(bf16) for j in range(8)]
        mixed = dot(first[...], jnp.concatenate(signals, axis=1))
        rows = pl.ds(pl.multiple_of(step * 512, 512), 512)
        acc[rows, :] = dot(turned(mixed, 8, turn[0], turn[1]), second[...])
        return carry

    lax.fori_loop(0, 4, filter_spectra, 0)

    def both_ways(start_at, step, carry):
        index = start_at + step * 4
        signals = [held[s, channel(index + j), :].astype(bf16) for j in range(4) for s in range(2)]
        mixed = dot(first[...], jnp.concatenate(signals, axis=1))
        spectra = dot(turned(mixed, 8, turn[0], turn[1]), second[...])
        rows = pl.ds(pl.multiple_of(index * 64, 256), 256)
        filt = acc[rows, :]
        joined, kept = [], []
        for j in range(4):
            parts = []
            for value in (
                spectra[j * 128 : j * 128 + 64],
                spectra[j * 128 + 64 : j * 128 + 128],
                filt[j * 64 : j * 64 + 64],
            ):
                parts.append((value[:, :LANES], value[:, LANES:]))
            (pr, pi), (wr, wi), (hr, hi) = parts
            joined.append(jnp.concatenate([pr * hr - pi * hi, pr * hi + pi * hr], axis=1))
            joined.append(jnp.concatenate([hr * wr + hi * wi, hr * wi - hi * wr], axis=1))
            kept.append(jnp.concatenate([pr * wr + pi * wi, pr * wi - pi * wr], axis=1))
        fgs[rows, :] = jnp.concatenate(kept, axis=0).astype(bf16)
        back = dot(jnp.concatenate(joined, axis=0).astype(bf16), second_back[...])
        final = dot(first_back[...], unturned(back, 8, turn[0], turn[1]))
        for j in range(4):
            for s in range(2):
                held[s, channel(index + j), :] = final[:, block(2 * j + s)]
        return carry

    for group in range(2):
        arrived(*(("out", step, group) for step in steps))
        kept[group].wait()
        own = slice(group * 16, group * 16 + 16)
        for n in range(BLOCKS):
            for s in range(2):
                rows = slice(n * 32 + group * 16, n * 32 + group * 16 + 16)
                held[s, rows, :] = arr[s, own, block(n)].astype(f32)
        lax.fori_loop(0, 4, functools.partial(both_ways, group * 16), 0)
        gain = gains[own, :]
        for n in range(BLOCKS):
            for s in range(2):
                rows = slice(n * 32 + group * 16, n * 32 + group * 16 + 16)
                direct = gain * arr[s, own, block(n)].astype(f32)
                arr[s, own, block(n)] = (held[s, rows, :] + direct).astype(bf16)
        for step in steps:
            src = positions_of(arr, peer_of(*step), group)
            start(("back", step, group), src, rows_of(ret, me, group), step)
        copy = pltpu.make_async_copy(
            positions_of(arr, me, group), rows_of(ret, me, group), load.at[13 + group]
        )
        copy.start()
        kept.append(copy)

    def filter_grads(step, carry):
        rows = pl.ds(pl.multiple_of(step * 512, 512), 512)
        back = dot(fgs[rows, :], second_back[...])
        final = dot(first_back[...], unturned(back, 8, turn[0], turn[1]))
        for j in range(8):
            held[2, channel(step * 8 + j), :] = final[:, block(j)]
        return carry

    lax.fori_loop(0, 4, filter_grads, 0)
    for n in range(BLOCKS):
        grad[:, block(n)] = held[2, n * 32 : (n + 1) * 32, :]
    for group in range(2):
        arrived(*(("back", step, group) for step in steps))
        kept[2 + group].wait()

    def lanes(p, chunk):
        return pl.ds(pl.multiple_of(p * 512 + chunk * 128, 128), 128)

    def stream_grads(chunk, carry):
        rows = pl.ds(pl.multiple_of(chunk * 128, 128), 128)
        one, two = ret[0, rows, :].astype(f32), ret[1, rows, :].astype(f32)
        factors = ((one, cotangent), (two, values), (two, keys))
        for p, (value, factor) in enumerate(factors):
            grad = (value * factor[rows, :].astype(f32)).astype(bf16)
            cgx[p, rows, 0:512] = grad
            hout[:, lanes(p, chunk)] = grad[:, 0:128].T[0:16, :]
        return carry

    lax.fori_loop(0, 4, stream_grads, 0)
    start("halo", hout, hin, "last")

    def tapped(p, rows, first, width, kept):
        x = cgx[p, rows, first : first + width].astype(f32)
        total = coltaps[rows, p : p + 1] * x
        for j in (1, 2):
            total = total + coltaps[rows, 3 * j + p : 3 * j + p + 1] * pltpu.roll(x, width - j, 1)
        return total[:, :kept].astype(bf16)

    def front(chunk, carry):
        rows = pl.ds(pl.multiple_of(chunk * 128, 128), 128)
        for p in range(3):
            grad = tapped(p, rows, 0, 512, 384)
            pgc[lanes(p, chunk), 0:384] = grad
            pgt[0:384, lanes(p, chunk)] = grad.T
        return carry

    lax.fori_loop(0, 4, front, 0)
    start("twin0", pgc.at[:, pl.ds(0, 384)], pgo.at[:, pl.ds(0, 384)], "twin")
    arrived("halo")

    def rest(chunk, carry):
        rows = pl.ds(pl.multiple_of(chunk * 128, 128), 128)
        for p in range(3):
            first = hin[:, lanes(p, chunk)].astype(f32)
            first = jnp.where(me == N_CTX - 1, jnp.zeros_like(first), first)
            first = jnp.concatenate([first, jnp.zeros((112, 128), f32)], axis=0)
            cgx[p, rows, 512:640] = first.T.astype(bf16)
            grad = tapped(p, rows, 384, 256, 128)
            pgc[lanes(p, chunk), 384:512] = grad
            pgt[384:512, lanes(p, chunk)] = grad.T
        return carry

    lax.fori_loop(0, 4, rest, 0)
    start("twin1", pgc.at[:, pl.ds(384, 128)], pgo.at[:, pl.ds(384, 128)], "twin")

    def input_tiles(first):
        def tile(step, carry):
            rows = pl.ds(pl.multiple_of((first + step) * 512, 512), 512)
            ig[:, rows] = lax.dot_general(
                pgt[...],
                wall[pl.ds((first + step) * 2, 2)].reshape(512, 1536),
                (((1,), (1,)), ((), ())),
                preferred_element_type=f32,
            ).astype(bf16)
            return carry

        lax.fori_loop(0, 4, tile, 0)

    def acc_rows(slot, row, count):
        return pl.ds(pl.multiple_of(slot * 1536 + row, 128), count)

    def weight_part(slot, block, own=True, theirs=True):
        mine = pl.ds(pl.multiple_of((2 * block + core) * 256, 256), 256)
        columns = pl.ds(pl.multiple_of(block * 256, 256), 256)

        def half(step, carry):
            rows = pl.ds(pl.multiple_of(step * 768, 256), 768)
            kept = acc_rows(slot, step * 768, 768)
            value = dot(pgc[rows, :], tok[16:528, mine]) if own else acc[kept, :]
            if theirs:
                value = value + dot(pgo[rows, :], oth[:, columns])
            acc[kept, :] = value
            return carry

        lax.fori_loop(0, 2, half, 0)

    def fold(dst, slot, first, last, *terms):
        def chunk(step, carry):
            rows = pl.ds(pl.multiple_of(step * 128, 128), 128)
            total = acc[acc_rows(slot, step * 128, 128), :]
            for term, offset in terms:
                part_rows = pl.ds(pl.multiple_of(step * 128 - offset, 128), 128)
                total = total + term[part_rows, :].astype(f32)
            dst[rows, :] = total.astype(bf16)
            return carry

        lax.fori_loop(first // 128, last // 128, chunk, 0)

    def block_of(y, xh):
        return y * 2 + xh

    y2, yp, ym = lax.rem(y + 2, 4), lax.rem(y + 1, 4), lax.rem(y + 3, 4)
    ztwo, zp, zm = lax.rem(z + 2, 4), lax.rem(z + 1, 4), lax.rem(z + 3, 4)
    xo = 1 - xh
    sides = (1 - xl, xl)
    low, high = pl.ds(0, 768), pl.ds(768, 768)
    parts = (slice(0, 2048), slice(2048, 4096))

    def ig_rows(side, z, first, count):
        return pl.ds(pl.multiple_of((side * 4 + z) * 64 + first, 32), count)

    def ig_add(rows, h, *terms):
        total = ig[rows, parts[h]].astype(f32)
        for term in terms:
            total = total + term[...].astype(f32)
        return total.astype(bf16)

    def z_first(h):
        for k in range(2):
            src = ig.at[ig_rows(sides[k], ztwo, 0, 32), parts[h]]
            start(("z2p", h, k), src, z2.at[h, k, 0], "above")
            src = ig.at[ig_rows(sides[k], ztwo, 32, 32), parts[h]]
            start(("z2m", h, k), src, z2.at[h, k, 1], "below")

    def z_second(h):
        for k in range(2):
            arrived(("z2p", h, k))
            rows = ig_rows(sides[k], zp, 0, 32)
            ig[rows, parts[h]] = ig_add(rows, h, z2.at[h, k, 0])
            src = ig.at[ig_rows(sides[k], zp, 0, 64), parts[h]]
            start(("zfp", h, k), src, zf.at[h, k, 0], "above")
            arrived(("z2m", h, k))
            rows = ig_rows(sides[k], zm, 32, 32)
            ig[rows, parts[h]] = ig_add(rows, h, z2.at[h, k, 1])
            src = ig.at[ig_rows(sides[k], zm, 0, 64), parts[h]]
            start(("zfm", h, k), src, zf.at[h, k, 1], "below")

    def z_across(h):
        arrived(("zfp", h, 0), ("zfm", h, 0))
        rows = ig_rows(sides[0], z, 0, 64)
        ig[rows, parts[h]] = ig_add(rows, h, zf.at[h, 0, 0], zf.at[h, 0, 1])
        start(("xz", h), ig.at[rows, parts[h]], xz.at[h], "near")

    def z_last(h):
        arrived(("zfp", h, 1), ("zfm", h, 1), ("xz", h))
        rows = ig_rows(sides[1], z, 0, 64)
        ig_out[:, parts[h]] = ig_add(rows, h, zf.at[h, 1, 0], zf.at[h, 1, 1], xz.at[h])

    early = ((y2, xo), (yp, xo), (ym, xo))
    for slot, place in enumerate(early):
        weight_part(slot, block_of(*place), theirs=False)
    arrived("twin0", "twin1")
    for slot, place in enumerate(early):
        weight_part(slot, block_of(*place), own=False)
        fold(part.at[slot], slot, 0, 1536)
        dst, peer = ((xin, "across"), (rf.at[0, 0], "up"), (rf.at[0, 1], "down"))[slot]
        start((peer, 0), part.at[slot], dst, peer)
    input_tiles(0)
    z_first(0)
    input_tiles(4)
    z_first(1)
    z_second(0)
    weight_part(1, block_of(yp, xh))
    weight_part(2, block_of(ym, xh))
    z_second(1)
    weight_part(0, block_of(y2, xh))
    arrived(("across", 0))
    fold(part.at[3], 0, 0, 1536, (xin, 0))
    start("up2", part.at[3, low], r2.at[0], "up")
    start("down2", part.at[3, high], r2.at[1], "down")
    weight_part(0, block_of(y, xo))
    arrived(("up", 0), ("down", 0))
    sent[("across", 0)].wait_send()
    fold(part.at[0], 0, 0, 1536, (rf.at[0, 0], 0), (rf.at[0, 1], 0))
    start("across1", part.at[0], xr, "across")
    fold(part.at[4], 1, 768, 1536)
    start("up1b", part.at[4, high], rf.at[1, 0, high], "up")
    fold(part.at[5], 2, 0, 768)
    start("down1a", part.at[5, low], rf.at[1, 1, low], "down")
    weight_part(0, block_of(y, xh))
    z_across(0)
    z_across(1)
    arrived("up2")
    fold(part.at[4], 1, 0, 768, (r2.at[0], 0))
    start("up1a", part.at[4, low], rf.at[1, 0, low], "up")
    arrived("down2")
    fold(part.at[5], 2, 768, 1536, (r2.at[1], 768))
    start("down1b", part.at[5, high], rf.at[1, 1, high], "down")
    z_last(0)
    z_last(1)
    arrived("across1", "up1a", "up1b", "down1a", "down1b")
    fold(wg_out, 0, 0, 1536, (rf.at[1, 0], 0), (rf.at[1, 1], 0), (xr, 0))
    for name, copy in sent.items():
        if name != ("across", 0):
            copy.wait_send()


def mixer(tokens, weight, out_grad, short_taps, long_filter, skip_bias):
    bf16, f32 = jnp.bfloat16, jnp.float32
    vmem = lambda *shape: pltpu.VMEM(shape, bf16)
    wide = lambda *shape: pltpu.VMEM(shape, f32)
    return pl.pallas_call(
        mixer_kernel,
        out_shape=(
            jax.ShapeDtypeStruct((64, 4096), bf16),
            jax.ShapeDtypeStruct((1536, 256), bf16),
            jax.ShapeDtypeStruct((32, BLOCKS * LANES), f32),
        ),
        in_specs=[ANY] * 11,
        out_specs=(IN_VMEM,) * 3,
        scratch_shapes=[
            vmem(528, 4096),
            vmem(512, 2048),
            vmem(N_CTX, 256, 1536),
            vmem(512, 512),
            wide(3, 3, 512),
            wide(512, 16),
            wide(32, BLOCKS * LANES),
            wide(1, 32),
            wide(32, LANES),
            vmem(128, 64),
            vmem(256, 256),
            vmem(256, 256),
            vmem(64, 128),
            wide(2, 64, LANES),
            vmem(512, 512),
            vmem(512, 512),
            vmem(2, 512, 512),
            vmem(2, 32, BLOCKS * LANES),
            wide(3, 32 * BLOCKS, LANES),
            vmem(32 * BLOCKS, 2 * LANES),
            vmem(2, 512, 512),
            vmem(3, 512, 640),
            vmem(16, 1536),
            vmem(16, 1536),
            vmem(1536, 512),
            vmem(512, 1536),
            vmem(1536, 512),
            vmem(512, 4096),
            wide(4608, 256),
            vmem(6, 1536, 256),
            vmem(1536, 256),
            vmem(2, 768, 256),
            vmem(2, 2, 1536, 256),
            vmem(1536, 256),
            vmem(2, 2, 2, 32, 2048),
            vmem(2, 2, 2, 64, 2048),
            vmem(2, 64, 2048),
            pltpu.SemaphoreType.DMA((125,)),
            pltpu.SemaphoreType.DMA((125,)),
            pltpu.SemaphoreType.DMA((15,)),
        ],
        compiler_params=pltpu.CompilerParams(
            collective_id=1, has_side_effects=True, vmem_limit_bytes=63 * 1024 * 1024
        ),
    )(
        tokens, weight, out_grad, short_taps, long_filter, skip_bias.reshape(1, 32), *tables()
    )


def hand_out_kernel(ig_in, wg_in, grad_in, ig_out, wg_out, grad_out, wg, sem):
    copies = [
        pltpu.make_async_copy(wg_in, wg, sem.at[0]),
        pltpu.make_async_copy(ig_in, ig_out, sem.at[1]),
        pltpu.make_async_copy(grad_in, grad_out, sem.at[2]),
    ]
    for copy in copies:
        copy.start()
    copies[0].wait()
    for p in range(3):
        wg_out[:, p, :] = wg[p * 512 : (p + 1) * 512, :].T
    for copy in copies[1:]:
        copy.wait()


def hand_out(input_grad, weight_grad, filter_grad):
    bf16 = jnp.bfloat16
    return pl.pallas_call(
        hand_out_kernel,
        out_shape=(
            jax.ShapeDtypeStruct((64, 4096), bf16),
            jax.ShapeDtypeStruct((256, 3, 512), bf16),
            jax.ShapeDtypeStruct((32, BLOCKS * LANES), jnp.float32),
        ),
        in_specs=[ANY] * 3,
        out_specs=(ANY, IN_VMEM, ANY),
        scratch_shapes=[pltpu.VMEM((1536, 256), bf16), pltpu.SemaphoreType.DMA((3,))],
        compiler_params=pltpu.CompilerParams(vmem_limit_bytes=32 * 1024 * 1024),
    )(input_grad, weight_grad, filter_grad)


def on_device(tokens, in_weight, short_taps, long_filter, skip_bias, out_grad):
    weight = in_weight.reshape(256, 1536)
    results = mixer(tokens, weight, out_grad, short_taps, long_filter, skip_bias)
    return hand_out(*results)


def solution(mesh):
    in_specs = (
        P("ctx", None),
        P("ctx", None, "tp"),
        P(None, None, "tp"),
        P(("tp", "ctx"), None),
        P(("tp", "ctx")),
        P("tp", "ctx"),
    )
    out_specs = (P(("ctx", "tp"), None), P("ctx", None, "tp"), P(("tp", "ctx"), None))
    return jax.shard_map(
        on_device, mesh=mesh, in_specs=in_specs, out_specs=out_specs, check_vma=False
    )
```

```python
import functools
import math

import jax
import jax.numpy as jnp
import numpy as np
from jax import lax
from jax.experimental import pallas as pl
from jax.experimental.pallas import tpu as pltpu
from jax.sharding import PartitionSpec as P

MESH = pl.DeviceIdType.MESH
ANY = pl.BlockSpec(memory_space=pl.ANY)
IN_VMEM = pl.BlockSpec(memory_space=pltpu.VMEM)
N_CTX = 16
LANES = 128
BLOCKS = 64
GROUP = 4


def tables():
    size = 2 * BLOCKS * LANES
    half = np.arange(BLOCKS) + 0.5
    n = np.arange(BLOCKS)
    m = np.arange(LANES)
    theta = 2 * np.pi * half[:, None] * n[None, :] / LANES
    phi = 2 * np.pi * half[:, None] * m[None, :] / size
    psi = 2 * np.pi * (m[:, None] * m[None, :] % LANES) / LANES
    first = np.concatenate([np.cos(theta), -np.sin(theta)], axis=0)
    second = np.block([[np.cos(psi), -np.sin(psi)], [np.sin(psi), np.cos(psi)]])
    second_back = np.block([[np.cos(psi), np.sin(psi)], [-np.sin(psi), np.cos(psi)]])
    first_back = np.concatenate([np.cos(theta).T, -np.sin(theta).T], axis=1)
    low = lambda value: jnp.asarray(value, jnp.bfloat16)
    turn = jnp.asarray(np.stack([np.cos(phi), np.sin(phi)]), jnp.float32)
    return low(first), low(second), low(second_back), low(first_back), turn


def turned(mixed, count, cos, sin):
    result = []
    for index in range(count):
        at = slice(index * LANES, (index + 1) * LANES)
        re, im = mixed[:BLOCKS, at], mixed[BLOCKS:, at]
        both = jnp.concatenate([re * cos + im * sin, im * cos - re * sin], axis=1)
        result.append(both.astype(jnp.bfloat16))
    return jnp.concatenate(result, axis=0)


def unturned(back, count, cos, sin):
    size = 2 * BLOCKS * LANES
    cos, sin = cos * (2.0 / size), sin * (2.0 / size)
    result = []
    for index in range(count):
        rows = slice(index * BLOCKS, (index + 1) * BLOCKS)
        re, im = back[rows, :LANES], back[rows, LANES:]
        both = jnp.concatenate([re * cos - im * sin, im * cos + re * sin], axis=0)
        result.append(both.astype(jnp.bfloat16))
    return jnp.concatenate(result, axis=1)


def places():
    me, b = lax.axis_index("ctx"), lax.axis_index("tp")
    core, xh, y = lax.rem(me, 2), lax.rem(me // 2, 2), me // 4
    z, xl = lax.rem(b, 4), b // 4
    ctx_of = lambda y, xh: (y * 2 + xh) * 2 + core
    return dict(
        core=core,
        xh=xh,
        y=y,
        z=z,
        xl=xl,
        twin={"ctx": me + 1 - 2 * core},
        up={"ctx": ctx_of(lax.rem(y + 1, 4), xh)},
        down={"ctx": ctx_of(lax.rem(y + 3, 4), xh)},
        near={"ctx": me, "tp": (1 - xl) * 4 + z},
        far={"ctx": ctx_of(y, 1 - xh), "tp": (1 - xl) * 4 + z},
        above={"tp": xl * 4 + lax.rem(z + 1, 4)},
        below={"tp": xl * 4 + lax.rem(z + 3, 4)},
    )


def greet(peers):
    barrier = pltpu.get_barrier_semaphore()
    for peer in peers:
        pl.semaphore_signal(barrier, inc=1, device_id=peer, device_id_type=MESH)
    pl.semaphore_wait(barrier, len(peers))


def rows_of(ref, index, group):
    first = pl.multiple_of(index * 32 + group * 16, 16)
    return ref.at[:, pl.ds(first, 16), :]


def positions_of(ref, index, group):
    return ref.at[:, pl.ds(group * 16, 16), pl.ds(pl.multiple_of(index * 512, 512), 512)]


def mixer_kernel(
    tokens, weight, cotangent_in, taps_in, filters_in, bias_in, first_in, second_in,
    second_back_in, first_back_in, turn_in, ig_out, wg_out, grad,
    tok, oth, wall, cotangent, taps, coltaps, filters, bias, gains, first, second, second_back, first_back,
    turn, keys, values, out, arr, held, fgs, ret, cgx, hout, hin, pgc, pgt, pgo, ig, acc, part,
    xin, r2, rf, xr, z2, zf, xz, send, recv, load,
):
    f32, bf16 = jnp.float32, jnp.bfloat16
    at = places()
    core, xh, y, z, xl = at["core"], at["xh"], at["y"], at["z"], at["xl"]
    me = lax.axis_index("ctx")
    at["across"] = {"ctx": (y * 2 + 1 - xh) * 2 + core}
    at["next"] = {"ctx": lax.rem(me + 1, N_CTX)}
    steps = [(s, i) for s in range(4) for i in range(4)][1:]
    fourth = lax.rem(me, 4)

    def peer_of(s, i):
        return lax.rem(y + s, 4) * 4 + lax.rem(fourth + i, 4)

    for step in steps:
        at[step] = {"ctx": peer_of(*step)}
    at["last"] = {"ctx": lax.rem(me + N_CTX - 1, N_CTX)}
    fetched = [
        (tokens, tok.at[pl.ds(16, 512)]),
        (cotangent_in, cotangent),
        (taps_in, taps),
        (filters_in, filters),
        (bias_in, bias),
        (first_in, first),
        (second_in, second),
        (second_back_in, second_back),
        (first_back_in, first_back),
        (turn_in, turn),
    ]
    loads = [
        pltpu.make_async_copy(src, dst, load.at[index]) for index, (src, dst) in enumerate(fetched)
    ]
    own_weight = [
        pltpu.make_async_copy(
            weight.at[p], wall.at[me, :, pl.ds(p * 512, 512)], load.at[15 + p]
        )
        for p in range(3)
    ]
    for one in (*own_weight, *loads):
        one.start()
    greet([at[name] for name in (*steps, "near", "above", "below")])
    sent = {}

    def start(name, src, dst, peer):
        index = len(sent)
        copy = pltpu.make_async_remote_copy(
            src_ref=src,
            dst_ref=dst,
            send_sem=send.at[index],
            recv_sem=recv.at[index],
            device_id=at[peer],
            device_id_type=MESH,
        )
        copy.start()
        sent[name] = copy

    def arrived(*names):
        for name in names:
            sent[name].wait_recv()

    halves = (pl.ds(0, 128), pl.ds(128, 128))

    def half_of(index, half):
        return wall.at[index, halves[half]]

    def pass_on(name, index, half, peer):
        start(name, half_of(index, half), half_of(index, half), peer)

    def hand_over(name, index):
        start(name, wall.at[index], wall.at[index], "twin")

    def multiply(index, fresh=False):
        pair = index // 2
        columns = pl.ds(pl.multiple_of(pair * 512, 512), 512)

        def tile(step, carry):
            place = pl.ds(pl.multiple_of(step * 512, 512), 512)
            value = jnp.dot(
                tok[:, columns],
                wall[pl.ds(pair * 2, 2), :, place].reshape(512, 512),
                preferred_element_type=f32,
            )
            for half in range(2):
                rows = pl.ds(pl.multiple_of(step * 1056 + half * 528, 16), 528)
                piece = value[:, half * 256 : half * 256 + 256]
                acc[rows, :] = piece if fresh else acc[rows, :] + piece
            return carry

        lax.fori_loop(0, 3, tile, 0)

    def ctx_of(y, xh):
        return (lax.rem(y, 4) * 2 + xh) * 2 + core

    below, above, beyond = ctx_of(y + 3, xh), ctx_of(y + 1, xh), ctx_of(y + 2, xh)
    side = ctx_of(y, 1 - xh)
    side_below, side_above = ctx_of(y + 3, 1 - xh), ctx_of(y + 1, 1 - xh)
    side_beyond = ctx_of(y + 2, 1 - xh)

    for one in own_weight:
        one.wait()
    pass_on("w_up0", me, 0, "up")
    pass_on("w_down1", me, 1, "down")
    start("w_across", wall.at[me], wall.at[me], "across")
    hand_over("w_twin", me)
    start("w_halo", tokens.at[pl.ds(496, 16)], tok.at[pl.ds(0, 16)], "next")
    for j in range(8):
        columns = pl.ds(pl.multiple_of((2 * j + 1 - core) * 256, 256), 256)
        start(("swap", j), tokens.at[:, columns], oth.at[:, pl.ds(j * 256, 256)], "twin")
    arrived("w_up0")
    pass_on("w_on0", below, 0, "up")
    arrived("w_down1")
    pass_on("w_on1", above, 1, "down")
    pass_on("w_up1", me, 1, "up")
    pass_on("w_down0", me, 0, "down")
    for one in loads:
        one.wait()
    arrived("w_halo", "w_twin")
    multiply(me, fresh=True)
    arrived("w_across")
    pass_on("w_side_up0", side, 0, "up")
    pass_on("w_side_down1", side, 1, "down")
    hand_over("w_twin_side", side)
    arrived("w_on0", "w_on1")
    start("w_across_beyond", wall.at[beyond], wall.at[beyond], "across")
    hand_over("w_twin_beyond", beyond)
    pass_on("w_side_up1", side, 1, "up")
    pass_on("w_side_down0", side, 0, "down")
    arrived("w_twin_side")
    multiply(side)
    arrived("w_up1")
    hand_over("w_twin_below", below)
    arrived("w_down0")
    hand_over("w_twin_above", above)
    arrived("w_twin_beyond")
    multiply(beyond)
    arrived("w_twin_below")
    multiply(below)
    arrived("w_twin_above")
    multiply(above)
    arrived("w_side_up0")
    pass_on("w_twin_sb0", side_below, 0, "twin")
    arrived("w_side_down1")
    pass_on("w_twin_sa1", side_above, 1, "twin")
    arrived("w_across_beyond")
    hand_over("w_twin_across", side_beyond)
    arrived("w_twin_across")
    multiply(side_beyond)
    arrived("w_side_up1")
    pass_on("w_twin_sb1", side_below, 1, "twin")
    arrived("w_side_down0")
    pass_on("w_twin_sa0", side_above, 0, "twin")
    arrived("w_twin_sb0", "w_twin_sb1")
    multiply(side_below)
    arrived("w_twin_sa0", "w_twin_sa1")
    multiply(side_above)

    for j in range(8):
        arrived(("swap", j))
    coltaps[...] = jnp.concatenate([taps[0], taps[1], taps[2], jnp.zeros((7, 512), f32)], axis=0).T
    diagonal = lax.broadcasted_iota(jnp.int32, (32, 32), 0) == lax.broadcasted_iota(
        jnp.int32, (32, 32), 1
    )
    gain = jnp.where(diagonal, jnp.broadcast_to(bias[...], (32, 32)), 0.0)
    gains[...] = jnp.broadcast_to(jnp.sum(gain, axis=1, keepdims=True), (32, LANES))

    def head(x):
        edge = x[0:16]
        return jnp.concatenate([jnp.where(me == 0, jnp.zeros_like(edge), edge), x[16:]], axis=0)

    def filtered(p, chunk):
        rows = pl.ds(pl.multiple_of((p * 2 + chunk // 2) * 528, 16), 528)
        columns = pl.ds(pl.multiple_of(lax.rem(chunk, 2) * 128, 128), 128)
        own = pl.ds(pl.multiple_of(chunk * 128, 128), 128)
        x = head(acc[rows, columns].astype(bf16).astype(f32))
        total = taps[0, p : p + 1, own] * x
        for j in (1, 2):
            total = total + taps[j, p : p + 1, own] * pltpu.roll(x, j, 0)
        return total[16:].astype(bf16).T

    def start_out(step, group):
        peer = peer_of(*step)
        start(("out", step, group), rows_of(out, peer, group), positions_of(arr, me, group), step)

    for s in range(4):
        chunk = lax.rem(y + s, 4)
        rows = pl.ds(pl.multiple_of(chunk * 128, 128), 128)
        query, key, value = (filtered(p, chunk) for p in range(3))
        keys[rows, :] = key
        values[rows, :] = value
        out[0, rows, :] = (key.astype(f32) * value.astype(f32)).astype(bf16)
        out[1, rows, :] = (cotangent[rows, :].astype(f32) * query.astype(f32)).astype(bf16)
        for step in steps:
            if step[0] == s:
                start_out(step, 0)
    for step in steps:
        start_out(step, 1)
    kept = []
    for group in range(2):
        copy = pltpu.make_async_copy(
            rows_of(out, me, group), positions_of(arr, me, group), load.at[11 + group]
        )
        copy.start()
        kept.append(copy)

    def dot(a, b):
        return jnp.dot(a, b, preferred_element_type=f32)

    def channel(index):
        return pl.ds(index, BLOCKS, stride=32)

    def block(n):
        return slice(n * LANES, (n + 1) * LANES)

    for n in range(BLOCKS):
        held[2, n * 32 : (n + 1) * 32, :] = filters[:, block(n)]

    def filter_spectra(step, carry):
        signals = [held[2, channel(step * 8 + j), :].astype(bf16) for j in range(8)]
        mixed = dot(first[...], jnp.concatenate(signals, axis=1))
        rows = pl.ds(pl.multiple_of(step * 512, 512), 512)
        acc[rows, :] = dot(turned(mixed, 8, turn[0], turn[1]), second[...])
        return carry

    lax.fori_loop(0, 4, filter_spectra, 0)

    def both_ways(start_at, step, carry):
        index = start_at + step * 4
        signals = [held[s, channel(index + j), :].astype(bf16) for j in range(4) for s in range(2)]
        mixed = dot(first[...], jnp.concatenate(signals, axis=1))
        spectra = dot(turned(mixed, 8, turn[0], turn[1]), second[...])
        rows = pl.ds(pl.multiple_of(index * 64, 256), 256)
        filt = acc[rows, :]
        joined, kept = [], []
        for j in range(4):
            parts = []
            for value in (
                spectra[j * 128 : j * 128 + 64],
                spectra[j * 128 + 64 : j * 128 + 128],
                filt[j * 64 : j * 64 + 64],
            ):
                parts.append((value[:, :LANES], value[:, LANES:]))
            (pr, pi), (wr, wi), (hr, hi) = parts
            joined.append(jnp.concatenate([pr * hr - pi * hi, pr * hi + pi * hr], axis=1))
            joined.append(jnp.concatenate([hr * wr + hi * wi, hr * wi - hi * wr], axis=1))
            kept.append(jnp.concatenate([pr * wr + pi * wi, pr * wi - pi * wr], axis=1))
        fgs[rows, :] = jnp.concatenate(kept, axis=0).astype(bf16)
        back = dot(jnp.concatenate(joined, axis=0).astype(bf16), second_back[...])
        final = dot(first_back[...], unturned(back, 8, turn[0], turn[1]))
        for j in range(4):
            for s in range(2):
                held[s, channel(index + j), :] = final[:, block(2 * j + s)]
        return carry

    for group in range(2):
        arrived(*(("out", step, group) for step in steps))
        kept[group].wait()
        own = slice(group * 16, group * 16 + 16)
        for n in range(BLOCKS):
            for s in range(2):
                rows = slice(n * 32 + group * 16, n * 32 + group * 16 + 16)
                held[s, rows, :] = arr[s, own, block(n)].astype(f32)
        lax.fori_loop(0, 4, functools.partial(both_ways, group * 16), 0)
        gain = gains[own, :]
        for n in range(BLOCKS):
            for s in range(2):
                rows = slice(n * 32 + group * 16, n * 32 + group * 16 + 16)
                direct = gain * arr[s, own, block(n)].astype(f32)
                arr[s, own, block(n)] = (held[s, rows, :] + direct).astype(bf16)
        for step in steps:
            src = positions_of(arr, peer_of(*step), group)
            start(("back", step, group), src, rows_of(ret, me, group), step)
        copy = pltpu.make_async_copy(
            positions_of(arr, me, group), rows_of(ret, me, group), load.at[13 + group]
        )
        copy.start()
        kept.append(copy)

    def filter_grads(step, carry):
        rows = pl.ds(pl.multiple_of(step * 512, 512), 512)
        back = dot(fgs[rows, :], second_back[...])
        final = dot(first_back[...], unturned(back, 8, turn[0], turn[1]))
        for j in range(8):
            held[2, channel(step * 8 + j), :] = final[:, block(j)]
        return carry

    lax.fori_loop(0, 4, filter_grads, 0)
    for n in range(BLOCKS):
        grad[:, block(n)] = held[2, n * 32 : (n + 1) * 32, :]
    for group in range(2):
        arrived(*(("back", step, group) for step in steps))
        kept[2 + group].wait()

    def lanes(p, chunk):
        return pl.ds(pl.multiple_of(p * 512 + chunk * 128, 128), 128)

    def stream_grads(chunk, carry):
        rows = pl.ds(pl.multiple_of(chunk * 128, 128), 128)
        one, two = ret[0, rows, :].astype(f32), ret[1, rows, :].astype(f32)
        factors = ((one, cotangent), (two, values), (two, keys))
        for p, (value, factor) in enumerate(factors):
            grad = (value * factor[rows, :].astype(f32)).astype(bf16)
            cgx[p, rows, 0:512] = grad
            hout[:, lanes(p, chunk)] = grad[:, 0:128].T[0:16, :]
        return carry

    lax.fori_loop(0, 4, stream_grads, 0)
    start("halo", hout, hin, "last")

    def tapped(p, rows, first, width, kept):
        x = cgx[p, rows, first : first + width].astype(f32)
        total = coltaps[rows, p : p + 1] * x
        for j in (1, 2):
            total = total + coltaps[rows, 3 * j + p : 3 * j + p + 1] * pltpu.roll(x, width - j, 1)
        return total[:, :kept].astype(bf16)

    def front(chunk, carry):
        rows = pl.ds(pl.multiple_of(chunk * 128, 128), 128)
        for p in range(3):
            grad = tapped(p, rows, 0, 512, 384)
            pgc[lanes(p, chunk), 0:384] = grad
            pgt[0:384, lanes(p, chunk)] = grad.T
        return carry

    lax.fori_loop(0, 4, front, 0)
    start("twin0", pgc.at[:, pl.ds(0, 384)], pgo.at[:, pl.ds(0, 384)], "twin")
    arrived("halo")

    def rest(chunk, carry):
        rows = pl.ds(pl.multiple_of(chunk * 128, 128), 128)
        for p in range(3):
            first = hin[:, lanes(p, chunk)].astype(f32)
            first = jnp.where(me == N_CTX - 1, jnp.zeros_like(first), first)
            first = jnp.concatenate([first, jnp.zeros((112, 128), f32)], axis=0)
            cgx[p, rows, 512:640] = first.T.astype(bf16)
            grad = tapped(p, rows, 384, 256, 128)
            pgc[lanes(p, chunk), 384:512] = grad
            pgt[384:512, lanes(p, chunk)] = grad.T
        return carry

    lax.fori_loop(0, 4, rest, 0)
    start("twin1", pgc.at[:, pl.ds(384, 128)], pgo.at[:, pl.ds(384, 128)], "twin")

    def input_tiles(first):
        def tile(step, carry):
            rows = pl.ds(pl.multiple_of((first + step) * 512, 512), 512)
            ig[:, rows] = lax.dot_general(
                pgt[...],
                wall[pl.ds((first + step) * 2, 2)].reshape(512, 1536),
                (((1,), (1,)), ((), ())),
                preferred_element_type=f32,
            ).astype(bf16)
            return carry

        lax.fori_loop(0, 4, tile, 0)

    def acc_rows(slot, row, count):
        return pl.ds(pl.multiple_of(slot * 1536 + row, 128), count)

    def weight_part(slot, block, own=True, theirs=True):
        mine = pl.ds(pl.multiple_of((2 * block + core) * 256, 256), 256)
        columns = pl.ds(pl.multiple_of(block * 256, 256), 256)

        def half(step, carry):
            rows = pl.ds(pl.multiple_of(step * 768, 256), 768)
            kept = acc_rows(slot, step * 768, 768)
            value = dot(pgc[rows, :], tok[16:528, mine]) if own else acc[kept, :]
            if theirs:
                value = value + dot(pgo[rows, :], oth[:, columns])
            acc[kept, :] = value
            return carry

        lax.fori_loop(0, 2, half, 0)

    def fold(dst, slot, first, last, *terms):
        def chunk(step, carry):
            rows = pl.ds(pl.multiple_of(step * 128, 128), 128)
            total = acc[acc_rows(slot, step * 128, 128), :]
            for term, offset in terms:
                part_rows = pl.ds(pl.multiple_of(step * 128 - offset, 128), 128)
                total = total + term[part_rows, :].astype(f32)
            dst[rows, :] = total.astype(bf16)
            return carry

        lax.fori_loop(first // 128, last // 128, chunk, 0)

    def block_of(y, xh):
        return y * 2 + xh

    y2, yp, ym = lax.rem(y + 2, 4), lax.rem(y + 1, 4), lax.rem(y + 3, 4)
    ztwo, zp, zm = lax.rem(z + 2, 4), lax.rem(z + 1, 4), lax.rem(z + 3, 4)
    xo = 1 - xh
    sides = (1 - xl, xl)
    low, high = pl.ds(0, 768), pl.ds(768, 768)
    parts = (slice(0, 2048), slice(2048, 4096))

    def ig_rows(side, z, first, count):
        return pl.ds(pl.multiple_of((side * 4 + z) * 64 + first, 32), count)

    def ig_add(rows, h, *terms):
        total = ig[rows, parts[h]].astype(f32)
        for term in terms:
            total = total + term[...].astype(f32)
        return total.astype(bf16)

    def z_first(h):
        for k in range(2):
            src = ig.at[ig_rows(sides[k], ztwo, 0, 32), parts[h]]
            start(("z2p", h, k), src, z2.at[h, k, 0], "above")
            src = ig.at[ig_rows(sides[k], ztwo, 32, 32), parts[h]]
            start(("z2m", h, k), src, z2.at[h, k, 1], "below")

    def z_second(h):
        for k in range(2):
            arrived(("z2p", h, k))
            rows = ig_rows(sides[k], zp, 0, 32)
            ig[rows, parts[h]] = ig_add(rows, h, z2.at[h, k, 0])
            src = ig.at[ig_rows(sides[k], zp, 0, 64), parts[h]]
            start(("zfp", h, k), src, zf.at[h, k, 0], "above")
            arrived(("z2m", h, k))
            rows = ig_rows(sides[k], zm, 32, 32)
            ig[rows, parts[h]] = ig_add(rows, h, z2.at[h, k, 1])
            src = ig.at[ig_rows(sides[k], zm, 0, 64), parts[h]]
            start(("zfm", h, k), src, zf.at[h, k, 1], "below")

    def z_across(h):
        arrived(("zfp", h, 0), ("zfm", h, 0))
        rows = ig_rows(sides[0], z, 0, 64)
        ig[rows, parts[h]] = ig_add(rows, h, zf.at[h, 0, 0], zf.at[h, 0, 1])
        start(("xz", h), ig.at[rows, parts[h]], xz.at[h], "near")

    def z_last(h):
        arrived(("zfp", h, 1), ("zfm", h, 1), ("xz", h))
        rows = ig_rows(sides[1], z, 0, 64)
        ig_out[:, parts[h]] = ig_add(rows, h, zf.at[h, 1, 0], zf.at[h, 1, 1], xz.at[h])

    early = ((y2, xo), (yp, xo), (ym, xo))
    for slot, place in enumerate(early):
        weight_part(slot, block_of(*place), theirs=False)
    arrived("twin0", "twin1")
    for slot, place in enumerate(early):
        weight_part(slot, block_of(*place), own=False)
        fold(part.at[slot], slot, 0, 1536)
        dst, peer = ((xin, "across"), (rf.at[0, 0], "up"), (rf.at[0, 1], "down"))[slot]
        start((peer, 0), part.at[slot], dst, peer)
    input_tiles(0)
    z_first(0)
    input_tiles(4)
    z_first(1)
    z_second(0)
    weight_part(1, block_of(yp, xh))
    weight_part(2, block_of(ym, xh))
    z_second(1)
    weight_part(0, block_of(y2, xh))
    arrived(("across", 0))
    fold(part.at[3], 0, 0, 1536, (xin, 0))
    start("up2", part.at[3, low], r2.at[0], "up")
    start("down2", part.at[3, high], r2.at[1], "down")
    weight_part(0, block_of(y, xo))
    arrived(("up", 0), ("down", 0))
    sent[("across", 0)].wait_send()
    fold(part.at[0], 0, 0, 1536, (rf.at[0, 0], 0), (rf.at[0, 1], 0))
    start("across1", part.at[0], xr, "across")
    fold(part.at[4], 1, 768, 1536)
    start("up1b", part.at[4, high], rf.at[1, 0, high], "up")
    fold(part.at[5], 2, 0, 768)
    start("down1a", part.at[5, low], rf.at[1, 1, low], "down")
    weight_part(0, block_of(y, xh))
    z_across(0)
    z_across(1)
    arrived("up2")
    fold(part.at[4], 1, 0, 768, (r2.at[0], 0))
    start("up1a", part.at[4, low], rf.at[1, 0, low], "up")
    arrived("down2")
    fold(part.at[5], 2, 768, 1536, (r2.at[1], 768))
    start("down1b", part.at[5, high], rf.at[1, 1, high], "down")
    z_last(0)
    z_last(1)
    arrived("across1", "up1a", "up1b", "down1a", "down1b")

    def last_fold(step, carry):
        rows = pl.ds(pl.multiple_of(step * 128, 128), 128)
        total = acc[rows, :]
        for term in (rf.at[1, 0], rf.at[1, 1], xr):
            total = total + term[rows, :].astype(f32)
        columns = pl.ds(pl.multiple_of(lax.rem(step, 4) * 128, 128), 128)
        wg_out[step // 4, :, columns] = total.T.astype(bf16)
        return carry

    lax.fori_loop(0, 12, last_fold, 0)
    for name, copy in sent.items():
        if name != ("across", 0):
            copy.wait_send()


def mixer(tokens, weight, out_grad, short_taps, long_filter, skip_bias):
    bf16, f32 = jnp.bfloat16, jnp.float32
    vmem = lambda *shape: pltpu.VMEM(shape, bf16)
    wide = lambda *shape: pltpu.VMEM(shape, f32)
    return pl.pallas_call(
        mixer_kernel,
        out_shape=(
            jax.ShapeDtypeStruct((64, 4096), bf16),
            jax.ShapeDtypeStruct((3, 256, 512), bf16),
            jax.ShapeDtypeStruct((32, BLOCKS * LANES), f32),
        ),
        in_specs=[ANY] * 11,
        out_specs=(IN_VMEM,) * 3,
        scratch_shapes=[
            vmem(528, 4096),
            vmem(512, 2048),
            vmem(N_CTX, 256, 1536),
            vmem(512, 512),
            wide(3, 3, 512),
            wide(512, 16),
            wide(32, BLOCKS * LANES),
            wide(1, 32),
            wide(32, LANES),
            vmem(128, 64),
            vmem(256, 256),
            vmem(256, 256),
            vmem(64, 128),
            wide(2, 64, LANES),
            vmem(512, 512),
            vmem(512, 512),
            vmem(2, 512, 512),
            vmem(2, 32, BLOCKS * LANES),
            wide(3, 32 * BLOCKS, LANES),
            vmem(32 * BLOCKS, 2 * LANES),
            vmem(2, 512, 512),
            vmem(3, 512, 640),
            vmem(16, 1536),
            vmem(16, 1536),
            vmem(1536, 512),
            vmem(512, 1536),
            vmem(1536, 512),
            vmem(512, 4096),
            wide(4608, 256),
            vmem(6, 1536, 256),
            vmem(1536, 256),
            vmem(2, 768, 256),
            vmem(2, 2, 1536, 256),
            vmem(1536, 256),
            vmem(2, 2, 2, 32, 2048),
            vmem(2, 2, 2, 64, 2048),
            vmem(2, 64, 2048),
            pltpu.SemaphoreType.DMA((125,)),
            pltpu.SemaphoreType.DMA((125,)),
            pltpu.SemaphoreType.DMA((18,)),
        ],
        compiler_params=pltpu.CompilerParams(
            collective_id=1, has_side_effects=True, vmem_limit_bytes=63 * 1024 * 1024
        ),
    )(
        tokens, weight, out_grad, short_taps, long_filter, skip_bias.reshape(1, 32), *tables()
    )


def hand_out_kernel(*refs):
    count = len(refs) // 2
    copies = [
        pltpu.make_async_copy(refs[index], refs[count + index], refs[-1].at[index])
        for index in range(count)
    ]
    for copy in copies:
        copy.start()
    for copy in copies:
        copy.wait()


def hand_out(results):
    in_hbm = pl.BlockSpec(memory_space=pltpu.HBM)
    return pl.pallas_call(
        hand_out_kernel,
        out_shape=[jax.ShapeDtypeStruct(value.shape, value.dtype) for value in results],
        in_specs=[in_hbm] * len(results),
        out_specs=[in_hbm] * len(results),
        scratch_shapes=[pltpu.SemaphoreType.DMA((len(results),))],
        compiler_params=pltpu.CompilerParams(vmem_limit_bytes=63 * 1024 * 1024),
    )(*results)


def on_device(tokens, in_weight, short_taps, long_filter, skip_bias, out_grad):
    weight = jnp.transpose(in_weight, (1, 0, 2))
    results = mixer(tokens, weight, out_grad, short_taps, long_filter, skip_bias)
    input_grad, weight_grad, filter_grad = hand_out(results)
    return input_grad, jnp.transpose(weight_grad, (1, 0, 2)), filter_grad


def solution(mesh):
    in_specs = (
        P("ctx", None),
        P("ctx", None, "tp"),
        P(None, None, "tp"),
        P(("tp", "ctx"), None),
        P(("tp", "ctx")),
        P("tp", "ctx"),
    )
    out_specs = (P(("ctx", "tp"), None), P("ctx", None, "tp"), P(("tp", "ctx"), None))
    return jax.shard_map(
        on_device, mesh=mesh, in_specs=in_specs, out_specs=out_specs, check_vma=False
    )
```

```python
import functools
import math

import jax
import jax.numpy as jnp
import numpy as np
from jax import lax
from jax.experimental import pallas as pl
from jax.experimental.pallas import tpu as pltpu
from jax.sharding import PartitionSpec as P

MESH = pl.DeviceIdType.MESH
ANY = pl.BlockSpec(memory_space=pl.ANY)
IN_VMEM = pl.BlockSpec(memory_space=pltpu.VMEM)
N_CTX = 16
LANES = 128
BLOCKS = 64
GROUP = 4


def tables():
    size = 2 * BLOCKS * LANES
    half = np.arange(BLOCKS) + 0.5
    n = np.arange(BLOCKS)
    m = np.arange(LANES)
    theta = 2 * np.pi * half[:, None] * n[None, :] / LANES
    phi = 2 * np.pi * half[:, None] * m[None, :] / size
    psi = 2 * np.pi * (m[:, None] * m[None, :] % LANES) / LANES
    first = np.concatenate([np.cos(theta), -np.sin(theta)], axis=0)
    second = np.block([[np.cos(psi), -np.sin(psi)], [np.sin(psi), np.cos(psi)]])
    second_back = np.block([[np.cos(psi), np.sin(psi)], [-np.sin(psi), np.cos(psi)]])
    first_back = np.concatenate([np.cos(theta).T, -np.sin(theta).T], axis=1)
    low = lambda value: jnp.asarray(value, jnp.bfloat16)
    turn = jnp.asarray(np.stack([np.cos(phi), np.sin(phi)]), jnp.float32)
    return low(first), low(second), low(second_back), low(first_back), turn


def turned(mixed, count, cos, sin):
    result = []
    for index in range(count):
        at = slice(index * LANES, (index + 1) * LANES)
        re, im = mixed[:BLOCKS, at], mixed[BLOCKS:, at]
        both = jnp.concatenate([re * cos + im * sin, im * cos - re * sin], axis=1)
        result.append(both.astype(jnp.bfloat16))
    return jnp.concatenate(result, axis=0)


def unturned(back, count, cos, sin):
    size = 2 * BLOCKS * LANES
    cos, sin = cos * (2.0 / size), sin * (2.0 / size)
    result = []
    for index in range(count):
        rows = slice(index * BLOCKS, (index + 1) * BLOCKS)
        re, im = back[rows, :LANES], back[rows, LANES:]
        both = jnp.concatenate([re * cos - im * sin, im * cos + re * sin], axis=0)
        result.append(both.astype(jnp.bfloat16))
    return jnp.concatenate(result, axis=1)


def places():
    me, b = lax.axis_index("ctx"), lax.axis_index("tp")
    core, xh, y = lax.rem(me, 2), lax.rem(me // 2, 2), me // 4
    z, xl = lax.rem(b, 4), b // 4
    ctx_of = lambda y, xh: (y * 2 + xh) * 2 + core
    return dict(
        core=core,
        xh=xh,
        y=y,
        z=z,
        xl=xl,
        twin={"ctx": me + 1 - 2 * core},
        up={"ctx": ctx_of(lax.rem(y + 1, 4), xh)},
        down={"ctx": ctx_of(lax.rem(y + 3, 4), xh)},
        near={"ctx": me, "tp": (1 - xl) * 4 + z},
        far={"ctx": ctx_of(y, 1 - xh), "tp": (1 - xl) * 4 + z},
        above={"tp": xl * 4 + lax.rem(z + 1, 4)},
        below={"tp": xl * 4 + lax.rem(z + 3, 4)},
    )


def greet(peers):
    barrier = pltpu.get_barrier_semaphore()
    for peer in peers:
        pl.semaphore_signal(barrier, inc=1, device_id=peer, device_id_type=MESH)
    pl.semaphore_wait(barrier, len(peers))


def rows_of(ref, index, group):
    first = pl.multiple_of(index * 32 + group * 16, 16)
    return ref.at[:, pl.ds(first, 16), :]


def positions_of(ref, index, group):
    return ref.at[:, pl.ds(group * 16, 16), pl.ds(pl.multiple_of(index * 512, 512), 512)]


def mixer_kernel(
    tokens, weight, cotangent_in, taps_in, filters_in, bias_in, first_in, second_in,
    second_back_in, first_back_in, turn_in, ig_out, wg_out, grad,
    tok, oth, wall, cotangent, taps, coltaps, filters, bias, gains, first, second, second_back, first_back,
    turn, keys, values, out, arr, held, fgs, ret, cgx, hout, hin, pgc, pgt, pgo, ig, acc, part,
    xin, r2, rf, xr, z2, zf, xz, send, recv, load,
):
    f32, bf16 = jnp.float32, jnp.bfloat16
    at = places()
    core, xh, y, z, xl = at["core"], at["xh"], at["y"], at["z"], at["xl"]
    me = lax.axis_index("ctx")
    at["across"] = {"ctx": (y * 2 + 1 - xh) * 2 + core}
    at["next"] = {"ctx": lax.rem(me + 1, N_CTX)}
    steps = [(s, i) for s in range(4) for i in range(4)][1:]
    fourth = lax.rem(me, 4)

    def peer_of(s, i):
        return lax.rem(y + s, 4) * 4 + lax.rem(fourth + i, 4)

    for step in steps:
        at[step] = {"ctx": peer_of(*step)}
    at["last"] = {"ctx": lax.rem(me + N_CTX - 1, N_CTX)}
    fetched = [
        (tokens, tok.at[pl.ds(16, 512)]),
        (cotangent_in, cotangent),
        (taps_in, taps),
        (filters_in, filters),
        (bias_in, bias),
        (first_in, first),
        (second_in, second),
        (second_back_in, second_back),
        (first_back_in, first_back),
        (turn_in, turn),
    ]
    loads = [
        pltpu.make_async_copy(src, dst, load.at[index]) for index, (src, dst) in enumerate(fetched)
    ]
    own_weight = [
        pltpu.make_async_copy(
            weight.at[p], wall.at[me, :, pl.ds(p * 512, 512)], load.at[15 + p]
        )
        for p in range(3)
    ]
    for one in (*own_weight, *loads):
        one.start()
    greet([at[name] for name in (*steps, "near", "above", "below")])
    sent = {}

    def start(name, src, dst, peer):
        index = len(sent)
        copy = pltpu.make_async_remote_copy(
            src_ref=src,
            dst_ref=dst,
            send_sem=send.at[index],
            recv_sem=recv.at[index],
            device_id=at[peer],
            device_id_type=MESH,
        )
        copy.start()
        sent[name] = copy

    def arrived(*names):
        for name in names:
            sent[name].wait_recv()

    halves = (pl.ds(0, 128), pl.ds(128, 128))

    def half_of(index, half):
        return wall.at[index, halves[half]]

    def pass_on(name, index, half, peer):
        start(name, half_of(index, half), half_of(index, half), peer)

    def hand_over(name, index):
        start(name, wall.at[index], wall.at[index], "twin")

    def multiply(index, fresh=False):
        pair = index // 2
        columns = pl.ds(pl.multiple_of(pair * 512, 512), 512)

        def tile(step, carry):
            place = pl.ds(pl.multiple_of(step * 512, 512), 512)
            value = jnp.dot(
                tok[:, columns],
                wall[pl.ds(pair * 2, 2), :, place].reshape(512, 512),
                preferred_element_type=f32,
            )
            for half in range(2):
                rows = pl.ds(pl.multiple_of(step * 1056 + half * 528, 16), 528)
                piece = value[:, half * 256 : half * 256 + 256]
                acc[rows, :] = piece if fresh else acc[rows, :] + piece
            return carry

        lax.fori_loop(0, 3, tile, 0)

    def ctx_of(y, xh):
        return (lax.rem(y, 4) * 2 + xh) * 2 + core

    below, above, beyond = ctx_of(y + 3, xh), ctx_of(y + 1, xh), ctx_of(y + 2, xh)
    side = ctx_of(y, 1 - xh)
    side_below, side_above = ctx_of(y + 3, 1 - xh), ctx_of(y + 1, 1 - xh)
    side_beyond = ctx_of(y + 2, 1 - xh)

    for one in own_weight:
        one.wait()
    pass_on("w_up0", me, 0, "up")
    pass_on("w_down1", me, 1, "down")
    start("w_across", wall.at[me], wall.at[me], "across")
    hand_over("w_twin", me)
    start("w_halo", tokens.at[pl.ds(496, 16)], tok.at[pl.ds(0, 16)], "next")
    for j in range(8):
        columns = pl.ds(pl.multiple_of((2 * j + 1 - core) * 256, 256), 256)
        start(("swap", j), tokens.at[:, columns], oth.at[:, pl.ds(j * 256, 256)], "twin")
    arrived("w_up0")
    pass_on("w_on0", below, 0, "up")
    arrived("w_down1")
    pass_on("w_on1", above, 1, "down")
    pass_on("w_up1", me, 1, "up")
    pass_on("w_down0", me, 0, "down")
    for one in loads:
        one.wait()
    arrived("w_halo", "w_twin")
    multiply(me, fresh=True)
    arrived("w_across")
    pass_on("w_side_up0", side, 0, "up")
    pass_on("w_side_down1", side, 1, "down")
    hand_over("w_twin_side", side)
    arrived("w_on0", "w_on1")
    start("w_across_beyond", wall.at[beyond], wall.at[beyond], "across")
    hand_over("w_twin_beyond", beyond)
    pass_on("w_side_up1", side, 1, "up")
    pass_on("w_side_down0", side, 0, "down")
    arrived("w_twin_side")
    multiply(side)
    arrived("w_up1")
    hand_over("w_twin_below", below)
    arrived("w_down0")
    hand_over("w_twin_above", above)
    arrived("w_twin_beyond")
    multiply(beyond)
    arrived("w_twin_below")
    multiply(below)
    arrived("w_twin_above")
    multiply(above)
    arrived("w_side_up0")
    pass_on("w_twin_sb0", side_below, 0, "twin")
    arrived("w_side_down1")
    pass_on("w_twin_sa1", side_above, 1, "twin")
    arrived("w_across_beyond")
    hand_over("w_twin_across", side_beyond)
    arrived("w_twin_across")
    multiply(side_beyond)
    arrived("w_side_up1")
    pass_on("w_twin_sb1", side_below, 1, "twin")
    arrived("w_side_down0")
    pass_on("w_twin_sa0", side_above, 0, "twin")
    arrived("w_twin_sb0", "w_twin_sb1")
    multiply(side_below)
    arrived("w_twin_sa0", "w_twin_sa1")
    multiply(side_above)

    for j in range(8):
        arrived(("swap", j))
    columns = jnp.concatenate([taps[0], taps[1], taps[2], jnp.zeros((7, 512), f32)], axis=0).T
    for group in range(2):
        pieces = [columns[i * 32 + group * 16 : i * 32 + group * 16 + 16] for i in range(N_CTX)]
        coltaps[group] = jnp.concatenate(pieces, axis=0)
    diagonal = lax.broadcasted_iota(jnp.int32, (32, 32), 0) == lax.broadcasted_iota(
        jnp.int32, (32, 32), 1
    )
    gain = jnp.where(diagonal, jnp.broadcast_to(bias[...], (32, 32)), 0.0)
    gains[...] = jnp.broadcast_to(jnp.sum(gain, axis=1, keepdims=True), (32, LANES))

    def head(x):
        edge = x[0:16]
        return jnp.concatenate([jnp.where(me == 0, jnp.zeros_like(edge), edge), x[16:]], axis=0)

    def filtered(p, chunk):
        rows = pl.ds(pl.multiple_of((p * 2 + chunk // 2) * 528, 16), 528)
        columns = pl.ds(pl.multiple_of(lax.rem(chunk, 2) * 128, 128), 128)
        own = pl.ds(pl.multiple_of(chunk * 128, 128), 128)
        x = head(acc[rows, columns].astype(bf16).astype(f32))
        total = taps[0, p : p + 1, own] * x
        for j in (1, 2):
            total = total + taps[j, p : p + 1, own] * pltpu.roll(x, j, 0)
        return total[16:].astype(bf16).T

    def start_out(step, group):
        peer = peer_of(*step)
        start(("out", step, group), rows_of(out, peer, group), positions_of(arr, me, group), step)

    for s in range(4):
        chunk = lax.rem(y + s, 4)
        rows = pl.ds(pl.multiple_of(chunk * 128, 128), 128)
        query, key, value = (filtered(p, chunk) for p in range(3))
        for group in range(2):
            compact = pl.ds(pl.multiple_of(chunk * 64, 16), 64)
            for dst, src in ((keys, key), (values, value)):
                pieces = [src[i * 32 + group * 16 : i * 32 + group * 16 + 16] for i in range(4)]
                dst[group, compact, :] = jnp.concatenate(pieces, axis=0)
        out[0, rows, :] = (key.astype(f32) * value.astype(f32)).astype(bf16)
        out[1, rows, :] = (cotangent[rows, :].astype(f32) * query.astype(f32)).astype(bf16)
        for step in steps:
            if step[0] == s:
                start_out(step, 0)
    for step in steps:
        start_out(step, 1)
    kept = []
    for group in range(2):
        copy = pltpu.make_async_copy(
            rows_of(out, me, group), positions_of(arr, me, group), load.at[11 + group]
        )
        copy.start()
        kept.append(copy)

    def dot(a, b):
        return jnp.dot(a, b, preferred_element_type=f32)

    def channel(index):
        return pl.ds(index, BLOCKS, stride=32)

    def block(n):
        return slice(n * LANES, (n + 1) * LANES)

    for n in range(BLOCKS):
        held[2, n * 32 : (n + 1) * 32, :] = filters[:, block(n)]

    def filter_spectra(step, carry):
        signals = [held[2, channel(step * 8 + j), :].astype(bf16) for j in range(8)]
        mixed = dot(first[...], jnp.concatenate(signals, axis=1))
        rows = pl.ds(pl.multiple_of(step * 512, 512), 512)
        acc[rows, :] = dot(turned(mixed, 8, turn[0], turn[1]), second[...])
        return carry

    lax.fori_loop(0, 4, filter_spectra, 0)

    def both_ways(start_at, step, carry):
        index = start_at + step * 4
        signals = [held[s, channel(index + j), :].astype(bf16) for j in range(4) for s in range(2)]
        mixed = dot(first[...], jnp.concatenate(signals, axis=1))
        spectra = dot(turned(mixed, 8, turn[0], turn[1]), second[...])
        rows = pl.ds(pl.multiple_of(index * 64, 256), 256)
        filt = acc[rows, :]
        joined, kept = [], []
        for j in range(4):
            parts = []
            for value in (
                spectra[j * 128 : j * 128 + 64],
                spectra[j * 128 + 64 : j * 128 + 128],
                filt[j * 64 : j * 64 + 64],
            ):
                parts.append((value[:, :LANES], value[:, LANES:]))
            (pr, pi), (wr, wi), (hr, hi) = parts
            joined.append(jnp.concatenate([pr * hr - pi * hi, pr * hi + pi * hr], axis=1))
            joined.append(jnp.concatenate([hr * wr + hi * wi, hr * wi - hi * wr], axis=1))
            kept.append(jnp.concatenate([pr * wr + pi * wi, pr * wi - pi * wr], axis=1))
        fgs[rows, :] = jnp.concatenate(kept, axis=0).astype(bf16)
        back = dot(jnp.concatenate(joined, axis=0).astype(bf16), second_back[...])
        final = dot(first_back[...], unturned(back, 8, turn[0], turn[1]))
        for j in range(4):
            for s in range(2):
                held[s, channel(index + j), :] = final[:, block(2 * j + s)]
        return carry

    def compact_of(group):
        return ret.at[group, :, pl.ds(pl.multiple_of(me * 16, 16), 16), :]

    for group in range(2):
        arrived(*(("out", step, group) for step in steps))
        kept[group].wait()
        own = slice(group * 16, group * 16 + 16)
        for n in range(BLOCKS):
            for s in range(2):
                rows = slice(n * 32 + group * 16, n * 32 + group * 16 + 16)
                held[s, rows, :] = arr[s, own, block(n)].astype(f32)
        lax.fori_loop(0, 4, functools.partial(both_ways, group * 16), 0)
        gain = gains[own, :]
        for n in range(BLOCKS):
            for s in range(2):
                rows = slice(n * 32 + group * 16, n * 32 + group * 16 + 16)
                direct = gain * arr[s, own, block(n)].astype(f32)
                arr[s, own, block(n)] = (held[s, rows, :] + direct).astype(bf16)
        for step in steps:
            src = positions_of(arr, peer_of(*step), group)
            start(("back", step, group), src, compact_of(group), step)
        copy = pltpu.make_async_copy(
            positions_of(arr, me, group), compact_of(group), load.at[13 + group]
        )
        copy.start()
        kept.append(copy)

    def filter_grads(step, carry):
        rows = pl.ds(pl.multiple_of(step * 512, 512), 512)
        back = dot(fgs[rows, :], second_back[...])
        final = dot(first_back[...], unturned(back, 8, turn[0], turn[1]))
        for j in range(8):
            held[2, channel(step * 8 + j), :] = final[:, block(j)]
        return carry

    def stream_grads(group, chunk, carry):
        rows = pl.ds(pl.multiple_of(chunk * 128, 128), 128)
        one, two = ret[group, 0, rows, :].astype(f32), ret[group, 1, rows, :].astype(f32)
        owners = [
            cotangent[pl.ds(pl.multiple_of((chunk * 8 + i) * 32 + group * 16, 16), 16), :]
            for i in range(8)
        ]
        factors = (
            (one, jnp.concatenate(owners, axis=0)),
            (two, values[group, rows, :]),
            (two, keys[group, rows, :]),
        )
        for p, (value, factor) in enumerate(factors):
            grads = (value * factor.astype(f32)).astype(bf16)
            cgx[group * 3 + p, rows, 0:512] = grads
            columns = pl.ds(pl.multiple_of(p * 256 + chunk * 128, 128), 128)
            hout[group, :, columns] = grads[:, 0:128].T[0:16, :]
        return carry

    def tapped(group, p, rows, first, width, kept):
        x = cgx[group * 3 + p, rows, first : first + width].astype(f32)
        total = coltaps[group, rows, p : p + 1] * x
        for j in (1, 2):
            tap = coltaps[group, rows, 3 * j + p : 3 * j + p + 1]
            total = total + tap * pltpu.roll(x, width - j, 1)
        return total[:, :kept].astype(bf16)

    def grad_rows(group, p, chunk):
        return pl.ds(pl.multiple_of(group * 768 + p * 256 + chunk * 128, 128), 128)

    def front(group, chunk, carry):
        rows = pl.ds(pl.multiple_of(chunk * 128, 128), 128)
        for p in range(3):
            pgc[grad_rows(group, p, chunk), 0:384] = tapped(group, p, rows, 0, 512, 384)
        return carry

    def rest(group, chunk, carry):
        rows = pl.ds(pl.multiple_of(chunk * 128, 128), 128)
        for p in range(3):
            columns = pl.ds(pl.multiple_of(p * 256 + chunk * 128, 128), 128)
            edge = hin[group, :, columns].astype(f32)
            edge = jnp.where(me == N_CTX - 1, jnp.zeros_like(edge), edge)
            edge = jnp.concatenate([edge, jnp.zeros((112, 128), f32)], axis=0)
            cgx[group * 3 + p, rows, 512:640] = edge.T.astype(bf16)
            pgc[grad_rows(group, p, chunk), 384:512] = tapped(group, p, rows, 384, 256, 128)
        return carry

    def swap(group, part, first, count):
        places = (pl.ds(group * 768, 768), pl.ds(first, count))
        start(("grads", group, part), pgc.at[places], pgo.at[places], "twin")

    def to_stream_grads(group, meanwhile):
        arrived(*(("back", step, group) for step in steps))
        kept[2 + group].wait()
        lax.fori_loop(0, 2, functools.partial(stream_grads, group), 0)
        start(("halo", group), hout.at[group], hin.at[group], "last")
        lax.fori_loop(0, 2, functools.partial(front, group), 0)
        swap(group, 0, 0, 384)
        meanwhile()
        arrived(("halo", group))
        lax.fori_loop(0, 2, functools.partial(rest, group), 0)
        swap(group, 1, 384, 128)

    def whole_filter_grads():
        lax.fori_loop(0, 4, filter_grads, 0)
        for n in range(BLOCKS):
            grad[:, block(n)] = held[2, n * 32 : (n + 1) * 32, :]

    def by_position(chunk, carry):
        for p in range(3):
            pieces = []
            for i in range(4):
                for group in range(2):
                    first = group * 768 + p * 256 + chunk * 64 + i * 16
                    pieces.append(pgc[pl.ds(pl.multiple_of(first, 16), 16), :])
            columns = pl.ds(pl.multiple_of(p * 512 + chunk * 128, 128), 128)
            pgt[:, columns] = jnp.concatenate(pieces, axis=0).T
        return carry

    def input_tiles(first):
        def tile(step, carry):
            rows = pl.ds(pl.multiple_of((first + step) * 512, 512), 512)
            ig[:, rows] = lax.dot_general(
                pgt[...],
                wall[pl.ds((first + step) * 2, 2)].reshape(512, 1536),
                (((1,), (1,)), ((), ())),
                preferred_element_type=f32,
            ).astype(bf16)
            return carry

        lax.fori_loop(0, 4, tile, 0)

    def acc_rows(slot, row, count):
        return pl.ds(pl.multiple_of(slot * 768 + row, 16), count)

    def weight_part(slot, group, block, own=True, theirs=True):
        mine = pl.ds(pl.multiple_of((2 * block + core) * 256, 256), 256)
        columns = pl.ds(pl.multiple_of(block * 256, 256), 256)
        rows, kept = slice(group * 768, group * 768 + 768), acc_rows(slot, 0, 768)
        value = dot(pgc[rows, :], tok[16:528, mine]) if own else acc[kept, :]
        if theirs:
            value = value + dot(pgo[rows, :], oth[:, columns])
        acc[kept, :] = value

    def fold(dst, slot, first, last, *terms):
        def chunk(step, carry):
            rows = pl.ds(pl.multiple_of(step * 128, 128), 128)
            total = acc[acc_rows(slot, step * 128, 128), :]
            for term, offset in terms:
                part_rows = pl.ds(pl.multiple_of(step * 128 - offset, 128), 128)
                total = total + term[part_rows, :].astype(f32)
            dst[rows, :] = total.astype(bf16)
            return carry

        lax.fori_loop(first // 128, last // 128, chunk, 0)

    def block_of(y, xh):
        return y * 2 + xh

    y2, yp, ym = lax.rem(y + 2, 4), lax.rem(y + 1, 4), lax.rem(y + 3, 4)
    ztwo, zp, zm = lax.rem(z + 2, 4), lax.rem(z + 1, 4), lax.rem(z + 3, 4)
    xo = 1 - xh
    sides = (1 - xl, xl)
    low, high = pl.ds(0, 384), pl.ds(384, 384)
    parts = (slice(0, 2048), slice(2048, 4096))

    def ig_rows(side, z, first, count):
        return pl.ds(pl.multiple_of((side * 4 + z) * 64 + first, 32), count)

    def ig_add(rows, h, *terms):
        total = ig[rows, parts[h]].astype(f32)
        for term in terms:
            total = total + term[...].astype(f32)
        return total.astype(bf16)

    def z_first(h):
        for k in range(2):
            src = ig.at[ig_rows(sides[k], ztwo, 0, 32), parts[h]]
            start(("z2p", h, k), src, z2.at[h, k, 0], "above")
            src = ig.at[ig_rows(sides[k], ztwo, 32, 32), parts[h]]
            start(("z2m", h, k), src, z2.at[h, k, 1], "below")

    def z_second(h):
        for k in range(2):
            arrived(("z2p", h, k))
            rows = ig_rows(sides[k], zp, 0, 32)
            ig[rows, parts[h]] = ig_add(rows, h, z2.at[h, k, 0])
            src = ig.at[ig_rows(sides[k], zp, 0, 64), parts[h]]
            start(("zfp", h, k), src, zf.at[h, k, 0], "above")
            arrived(("z2m", h, k))
            rows = ig_rows(sides[k], zm, 32, 32)
            ig[rows, parts[h]] = ig_add(rows, h, z2.at[h, k, 1])
            src = ig.at[ig_rows(sides[k], zm, 0, 64), parts[h]]
            start(("zfm", h, k), src, zf.at[h, k, 1], "below")

    def z_across(h):
        arrived(("zfp", h, 0), ("zfm", h, 0))
        rows = ig_rows(sides[0], z, 0, 64)
        ig[rows, parts[h]] = ig_add(rows, h, zf.at[h, 0, 0], zf.at[h, 0, 1])
        start(("xz", h), ig.at[rows, parts[h]], xz.at[h], "near")

    def z_last(h):
        arrived(("zfp", h, 1), ("zfm", h, 1), ("xz", h))
        rows = ig_rows(sides[1], z, 0, 64)
        ig_out[:, parts[h]] = ig_add(rows, h, zf.at[h, 1, 0], zf.at[h, 1, 1], xz.at[h])

    early = ((y2, xo), (yp, xo), (ym, xo))

    def first_blocks(group):
        for n, place in enumerate(early):
            weight_part(3 * group + n, group, block_of(*place), theirs=False)
        arrived(("grads", group, 0), ("grads", group, 1))
        for n, place in enumerate(early):
            slot = 3 * group + n
            weight_part(slot, group, block_of(*place), own=False)
            fold(part.at[group, n], slot, 0, 768)
            dst = (xin.at[group], rf.at[group, 0, 0], rf.at[group, 0, 1])[n]
            peer = ("across", "up", "down")[n]
            start((peer, 0, group), part.at[group, n], dst, peer)

    def second_blocks(group):
        weight_part(0, group, block_of(y2, xh))
        arrived(("across", 0, group))
        fold(part.at[group, 3], 0, 0, 768, (xin.at[group], 0))
        start(("up", 2, group), part.at[group, 3, low], r2.at[group, 0], "up")
        start(("down", 2, group), part.at[group, 3, high], r2.at[group, 1], "down")

    def free_halves(group):
        weight_part(2 * group, group, block_of(yp, xh))
        fold(part.at[group, 4], 2 * group, 384, 768)
        start(("upb", 1, group), part.at[group, 4, high], rf.at[group, 1, 0, high], "up")
        weight_part(2 * group + 1, group, block_of(ym, xh))
        fold(part.at[group, 5], 2 * group + 1, 0, 384)
        start(("downa", 1, group), part.at[group, 5, low], rf.at[group, 1, 1, low], "down")

    def side_blocks(group):
        weight_part(4, group, block_of(y, xo))
        arrived(("up", 0, group), ("down", 0, group))
        sent[("across", 0, group)].wait_send()
        terms = ((rf.at[group, 0, 0], 0), (rf.at[group, 0, 1], 0))
        fold(part.at[group, 0], 4, 0, 768, *terms)
        start(("across", 1, group), part.at[group, 0], xr.at[group], "across")

    def bound_halves(group):
        arrived(("up", 2, group))
        fold(part.at[group, 4], 2 * group, 0, 384, (r2.at[group, 0], 0))
        start(("upa", 1, group), part.at[group, 4, low], rf.at[group, 1, 0, low], "up")
        arrived(("down", 2, group))
        fold(part.at[group, 5], 2 * group + 1, 384, 768, (r2.at[group, 1], 384))
        start(("downb", 1, group), part.at[group, 5, high], rf.at[group, 1, 1, high], "down")

    def own_blocks(group):
        names = (("across", 1), ("upa", 1), ("upb", 1), ("downa", 1), ("downb", 1))
        arrived(*((*name, group) for name in names))

        def chunk(step, carry):
            rows = pl.ds(pl.multiple_of(step * 128, 128), 128)
            place = acc_rows(4 + group, step * 128, 128)
            total = acc[place, :]
            for term in (rf.at[group, 1, 0], rf.at[group, 1, 1], xr.at[group]):
                total = total + term[rows, :].astype(f32)
            acc[place, :] = total
            return carry

        lax.fori_loop(0, 6, chunk, 0)

    def last_fold(step, carry):
        p, chunk = step // 4, lax.rem(step, 4)
        pieces = []
        for i in range(4):
            for group in range(2):
                pieces.append(acc[acc_rows(4 + group, p * 256 + chunk * 64 + i * 16, 16), :])
        columns = pl.ds(pl.multiple_of(chunk * 128, 128), 128)
        wg_out[p, :, columns] = jnp.concatenate(pieces, axis=0).T.astype(bf16)
        return carry

    to_stream_grads(0, whole_filter_grads)
    first_blocks(0)
    to_stream_grads(1, lambda: None)
    first_blocks(1)
    lax.fori_loop(0, 4, by_position, 0)
    input_tiles(0)
    z_first(0)
    second_blocks(0)
    input_tiles(4)
    z_first(1)
    second_blocks(1)
    z_second(0)
    free_halves(0)
    free_halves(1)
    side_blocks(0)
    side_blocks(1)
    z_second(1)
    bound_halves(0)
    bound_halves(1)
    for group in range(2):
        weight_part(4 + group, group, block_of(y, xh))
    z_across(0)
    z_across(1)
    own_blocks(0)
    z_last(0)
    z_last(1)
    own_blocks(1)
    lax.fori_loop(0, 12, last_fold, 0)
    for name, copy in sent.items():
        if name[:2] != ("across", 0):
            copy.wait_send()


def mixer(tokens, weight, out_grad, short_taps, long_filter, skip_bias):
    bf16, f32 = jnp.bfloat16, jnp.float32
    vmem = lambda *shape: pltpu.VMEM(shape, bf16)
    wide = lambda *shape: pltpu.VMEM(shape, f32)
    return pl.pallas_call(
        mixer_kernel,
        out_shape=(
            jax.ShapeDtypeStruct((64, 4096), bf16),
            jax.ShapeDtypeStruct((3, 256, 512), bf16),
            jax.ShapeDtypeStruct((32, BLOCKS * LANES), f32),
        ),
        in_specs=[ANY] * 11,
        out_specs=(IN_VMEM,) * 3,
        scratch_shapes=[
            vmem(528, 4096),
            vmem(512, 2048),
            vmem(N_CTX, 256, 1536),
            vmem(512, 512),
            wide(3, 3, 512),
            wide(2, 256, 16),
            wide(32, BLOCKS * LANES),
            wide(1, 32),
            wide(32, LANES),
            vmem(128, 64),
            vmem(256, 256),
            vmem(256, 256),
            vmem(64, 128),
            wide(2, 64, LANES),
            vmem(2, 256, 512),
            vmem(2, 256, 512),
            vmem(2, 512, 512),
            vmem(2, 32, BLOCKS * LANES),
            wide(3, 32 * BLOCKS, LANES),
            vmem(32 * BLOCKS, 2 * LANES),
            vmem(2, 2, 256, 512),
            vmem(6, 256, 640),
            vmem(2, 16, 768),
            vmem(2, 16, 768),
            vmem(1536, 512),
            vmem(512, 1536),
            vmem(1536, 512),
            vmem(512, 4096),
            wide(4608, 256),
            vmem(2, 6, 768, 256),
            vmem(2, 768, 256),
            vmem(2, 2, 384, 256),
            vmem(2, 2, 2, 768, 256),
            vmem(2, 768, 256),
            vmem(2, 2, 2, 32, 2048),
            vmem(2, 2, 2, 64, 2048),
            vmem(2, 64, 2048),
            pltpu.SemaphoreType.DMA((136,)),
            pltpu.SemaphoreType.DMA((136,)),
            pltpu.SemaphoreType.DMA((18,)),
        ],
        compiler_params=pltpu.CompilerParams(
            collective_id=1, has_side_effects=True, vmem_limit_bytes=63 * 1024 * 1024
        ),
    )(
        tokens, weight, out_grad, short_taps, long_filter, skip_bias.reshape(1, 32), *tables()
    )


def hand_out_kernel(*refs):
    count = (len(refs) - 1) // 3
    given, results, held, sem = refs[:count], refs[count : 2 * count], refs[2 * count : -1], refs[-1]
    inward = [pltpu.make_async_copy(given[n], held[n], sem.at[n]) for n in range(count)]
    outward = [pltpu.make_async_copy(held[n], results[n], sem.at[count + n]) for n in range(count)]
    for copy in inward:
        copy.start()
    for first, then in zip(inward, outward):
        first.wait()
        then.start()
    for copy in outward:
        copy.wait()


def hand_out(results):
    count = len(results)
    return pl.pallas_call(
        hand_out_kernel,
        out_shape=[jax.ShapeDtypeStruct(value.shape, value.dtype) for value in results],
        in_specs=[ANY] * count,
        out_specs=[ANY] * count,
        scratch_shapes=[pltpu.VMEM(value.shape, value.dtype) for value in results]
        + [pltpu.SemaphoreType.DMA((2 * count,))],
        compiler_params=pltpu.CompilerParams(vmem_limit_bytes=63 * 1024 * 1024),
    )(*results)


def on_device(tokens, in_weight, short_taps, long_filter, skip_bias, out_grad):
    weight = jnp.transpose(in_weight, (1, 0, 2))
    results = mixer(tokens, weight, out_grad, short_taps, long_filter, skip_bias)
    input_grad, weight_grad, filter_grad = hand_out(results)
    return input_grad, jnp.transpose(weight_grad, (1, 0, 2)), filter_grad


def solution(mesh):
    in_specs = (
        P("ctx", None),
        P("ctx", None, "tp"),
        P(None, None, "tp"),
        P(("tp", "ctx"), None),
        P(("tp", "ctx")),
        P("tp", "ctx"),
    )
    out_specs = (P(("ctx", "tp"), None), P("ctx", None, "tp"), P(("tp", "ctx"), None))
    return jax.shard_map(
        on_device, mesh=mesh, in_specs=in_specs, out_specs=out_specs, check_vma=False
    )
```

```python
import functools
import math

import jax
import jax.numpy as jnp
import numpy as np
from jax import lax
from jax.experimental import pallas as pl
from jax.experimental.pallas import tpu as pltpu
from jax.sharding import PartitionSpec as P

MESH = pl.DeviceIdType.MESH
ANY = pl.BlockSpec(memory_space=pl.ANY)
IN_VMEM = pl.BlockSpec(memory_space=pltpu.VMEM)
N_CTX = 16
LANES = 128
BLOCKS = 64
GROUP = 4


def tables():
    size = 2 * BLOCKS * LANES
    half = np.arange(BLOCKS) + 0.5
    n = np.arange(BLOCKS)
    m = np.arange(LANES)
    theta = 2 * np.pi * half[:, None] * n[None, :] / LANES
    phi = 2 * np.pi * half[:, None] * m[None, :] / size
    psi = 2 * np.pi * (m[:, None] * m[None, :] % LANES) / LANES
    first = np.concatenate([np.cos(theta), -np.sin(theta)], axis=0)
    second = np.block([[np.cos(psi), -np.sin(psi)], [np.sin(psi), np.cos(psi)]])
    second_back = np.block([[np.cos(psi), np.sin(psi)], [-np.sin(psi), np.cos(psi)]])
    first_back = np.concatenate([np.cos(theta).T, -np.sin(theta).T], axis=1)
    low = lambda value: jnp.asarray(value, jnp.bfloat16)
    turn = jnp.asarray(np.stack([np.cos(phi), np.sin(phi)]), jnp.float32)
    return low(first), low(second), low(second_back), low(first_back), turn


def turned(mixed, count, cos, sin):
    result = []
    for index in range(count):
        at = slice(index * LANES, (index + 1) * LANES)
        re, im = mixed[:BLOCKS, at], mixed[BLOCKS:, at]
        both = jnp.concatenate([re * cos + im * sin, im * cos - re * sin], axis=1)
        result.append(both.astype(jnp.bfloat16))
    return jnp.concatenate(result, axis=0)


def unturned(back, count, cos, sin):
    size = 2 * BLOCKS * LANES
    cos, sin = cos * (2.0 / size), sin * (2.0 / size)
    result = []
    for index in range(count):
        rows = slice(index * BLOCKS, (index + 1) * BLOCKS)
        re, im = back[rows, :LANES], back[rows, LANES:]
        both = jnp.concatenate([re * cos - im * sin, im * cos + re * sin], axis=0)
        result.append(both.astype(jnp.bfloat16))
    return jnp.concatenate(result, axis=1)


def places():
    me, b = lax.axis_index("ctx"), lax.axis_index("tp")
    core, xh, y = lax.rem(me, 2), lax.rem(me // 2, 2), me // 4
    z, xl = lax.rem(b, 4), b // 4
    ctx_of = lambda y, xh: (y * 2 + xh) * 2 + core
    return dict(
        core=core,
        xh=xh,
        y=y,
        z=z,
        xl=xl,
        twin={"ctx": me + 1 - 2 * core},
        up={"ctx": ctx_of(lax.rem(y + 1, 4), xh)},
        down={"ctx": ctx_of(lax.rem(y + 3, 4), xh)},
        near={"ctx": me, "tp": (1 - xl) * 4 + z},
        far={"ctx": ctx_of(y, 1 - xh), "tp": (1 - xl) * 4 + z},
        above={"tp": xl * 4 + lax.rem(z + 1, 4)},
        below={"tp": xl * 4 + lax.rem(z + 3, 4)},
    )


def greet(peers):
    barrier = pltpu.get_barrier_semaphore()
    for peer in peers:
        pl.semaphore_signal(barrier, inc=1, device_id=peer, device_id_type=MESH)
    pl.semaphore_wait(barrier, len(peers))


def rows_of(ref, index, group):
    first = pl.multiple_of(index * 32 + group * 16, 16)
    return ref.at[:, pl.ds(first, 16), :]


def positions_of(ref, index, group):
    return ref.at[:, pl.ds(group * 16, 16), pl.ds(pl.multiple_of(index * 512, 512), 512)]


def mixer_kernel(
    tokens, weight, cotangent_in, taps_in, filters_in, bias_in, first_in, second_in,
    second_back_in, first_back_in, turn_in, ig_out, wg_out, grad,
    tok, oth, wall, cotangent, taps, coltaps, filters, bias, gains, first, second, second_back, first_back,
    turn, keys, values, out, arr, held, fgs, ret, cgx, hout, hin, pgc, pgt, pgo, ig, acc, part,
    xin, r2, rf, xr, z2, zf, xz, send, recv, load,
):
    f32, bf16 = jnp.float32, jnp.bfloat16
    at = places()
    core, xh, y, z, xl = at["core"], at["xh"], at["y"], at["z"], at["xl"]
    me = lax.axis_index("ctx")
    at["across"] = {"ctx": (y * 2 + 1 - xh) * 2 + core}
    at["next"] = {"ctx": lax.rem(me + 1, N_CTX)}
    steps = [(s, i) for s in range(4) for i in range(4)][1:]
    fourth = lax.rem(me, 4)

    def peer_of(s, i):
        return lax.rem(y + s, 4) * 4 + lax.rem(fourth + i, 4)

    for step in steps:
        at[step] = {"ctx": peer_of(*step)}
    at["last"] = {"ctx": lax.rem(me + N_CTX - 1, N_CTX)}
    fetched = [
        (tokens, tok.at[pl.ds(16, 512)]),
        (cotangent_in, cotangent),
        (taps_in, taps),
        (filters_in, filters),
        (bias_in, bias),
        (first_in, first),
        (second_in, second),
        (second_back_in, second_back),
        (first_back_in, first_back),
        (turn_in, turn),
    ]
    loads = [
        pltpu.make_async_copy(src, dst, load.at[index]) for index, (src, dst) in enumerate(fetched)
    ]
    own_weight = [
        pltpu.make_async_copy(
            weight.at[p], wall.at[me, :, pl.ds(p * 512, 512)], load.at[15 + p]
        )
        for p in range(3)
    ]
    for one in (*own_weight, *loads):
        one.start()
    greet([at[name] for name in (*steps, "near", "above", "below")])
    sent = {}

    def start(name, src, dst, peer):
        index = len(sent)
        copy = pltpu.make_async_remote_copy(
            src_ref=src,
            dst_ref=dst,
            send_sem=send.at[index],
            recv_sem=recv.at[index],
            device_id=at[peer],
            device_id_type=MESH,
        )
        copy.start()
        sent[name] = copy

    def arrived(*names):
        for name in names:
            sent[name].wait_recv()

    halves = (pl.ds(0, 128), pl.ds(128, 128))

    def half_of(index, half):
        return wall.at[index, halves[half]]

    def pass_on(name, index, half, peer):
        start(name, half_of(index, half), half_of(index, half), peer)

    def hand_over(name, index):
        start(name, wall.at[index], wall.at[index], "twin")

    def multiply(index, fresh=False):
        pair = index // 2
        columns = pl.ds(pl.multiple_of(pair * 512, 512), 512)

        def tile(step, carry):
            place = pl.ds(pl.multiple_of(step * 512, 512), 512)
            value = jnp.dot(
                tok[:, columns],
                wall[pl.ds(pair * 2, 2), :, place].reshape(512, 512),
                preferred_element_type=f32,
            )
            for half in range(2):
                rows = pl.ds(pl.multiple_of(step * 1056 + half * 528, 16), 528)
                piece = value[:, half * 256 : half * 256 + 256]
                acc[rows, :] = piece if fresh else acc[rows, :] + piece
            return carry

        lax.fori_loop(0, 3, tile, 0)

    def ctx_of(y, xh):
        return (lax.rem(y, 4) * 2 + xh) * 2 + core

    below, above, beyond = ctx_of(y + 3, xh), ctx_of(y + 1, xh), ctx_of(y + 2, xh)
    side = ctx_of(y, 1 - xh)
    side_below, side_above = ctx_of(y + 3, 1 - xh), ctx_of(y + 1, 1 - xh)
    side_beyond = ctx_of(y + 2, 1 - xh)

    for one in own_weight:
        one.wait()
    pass_on("w_up0", me, 0, "up")
    pass_on("w_down1", me, 1, "down")
    start("w_across", wall.at[me], wall.at[me], "across")
    hand_over("w_twin", me)
    start("w_halo", tokens.at[pl.ds(496, 16)], tok.at[pl.ds(0, 16)], "next")
    for j in range(8):
        columns = pl.ds(pl.multiple_of((2 * j + 1 - core) * 256, 256), 256)
        start(("swap", j), tokens.at[:, columns], oth.at[:, pl.ds(j * 256, 256)], "twin")
    arrived("w_up0")
    pass_on("w_on0", below, 0, "up")
    arrived("w_down1")
    pass_on("w_on1", above, 1, "down")
    for one in loads:
        one.wait()
    arrived("w_halo", "w_twin")
    multiply(me, fresh=True)
    arrived("w_across")
    hand_over("w_twin_side", side)
    arrived("w_on0")
    pass_on("w_up1", me, 1, "up")
    arrived("w_on1")
    pass_on("w_down0", me, 0, "down")
    start("w_across_beyond", wall.at[beyond], wall.at[beyond], "across")
    pass_on("w_side_up0", side, 0, "up")
    pass_on("w_side_down1", side, 1, "down")
    hand_over("w_twin_beyond", beyond)
    arrived("w_twin_side")
    multiply(side)
    arrived("w_twin_beyond")
    multiply(beyond)
    arrived("w_up1")
    hand_over("w_twin_below", below)
    arrived("w_down0")
    hand_over("w_twin_above", above)
    arrived("w_side_up0")
    pass_on("w_side_up1", side, 1, "up")
    pass_on("w_twin_sb0", side_below, 0, "twin")
    arrived("w_side_down1")
    pass_on("w_side_down0", side, 0, "down")
    pass_on("w_twin_sa1", side_above, 1, "twin")
    arrived("w_twin_below")
    multiply(below)
    arrived("w_twin_above")
    multiply(above)
    arrived("w_across_beyond")
    hand_over("w_twin_across", side_beyond)
    arrived("w_twin_across")
    multiply(side_beyond)
    arrived("w_side_up1")
    pass_on("w_twin_sb1", side_below, 1, "twin")
    arrived("w_side_down0")
    pass_on("w_twin_sa0", side_above, 0, "twin")
    arrived("w_twin_sb0", "w_twin_sb1")
    multiply(side_below)
    arrived("w_twin_sa0", "w_twin_sa1")
    multiply(side_above)

    for j in range(8):
        arrived(("swap", j))
    columns = jnp.concatenate([taps[0], taps[1], taps[2], jnp.zeros((7, 512), f32)], axis=0).T
    for group in range(2):
        pieces = [columns[i * 32 + group * 16 : i * 32 + group * 16 + 16] for i in range(N_CTX)]
        coltaps[group] = jnp.concatenate(pieces, axis=0)
    diagonal = lax.broadcasted_iota(jnp.int32, (32, 32), 0) == lax.broadcasted_iota(
        jnp.int32, (32, 32), 1
    )
    gain = jnp.where(diagonal, jnp.broadcast_to(bias[...], (32, 32)), 0.0)
    gains[...] = jnp.broadcast_to(jnp.sum(gain, axis=1, keepdims=True), (32, LANES))

    def head(x):
        edge = x[0:16]
        return jnp.concatenate([jnp.where(me == 0, jnp.zeros_like(edge), edge), x[16:]], axis=0)

    def filtered(p, chunk):
        rows = pl.ds(pl.multiple_of((p * 2 + chunk // 2) * 528, 16), 528)
        columns = pl.ds(pl.multiple_of(lax.rem(chunk, 2) * 128, 128), 128)
        own = pl.ds(pl.multiple_of(chunk * 128, 128), 128)
        x = head(acc[rows, columns].astype(bf16).astype(f32))
        total = taps[0, p : p + 1, own] * x
        for j in (1, 2):
            total = total + taps[j, p : p + 1, own] * pltpu.roll(x, j, 0)
        return total[16:].astype(bf16).T

    def start_out(step, group):
        peer = peer_of(*step)
        start(("out", step, group), rows_of(out, peer, group), positions_of(arr, me, group), step)

    for s in range(4):
        chunk = lax.rem(y + s, 4)
        rows = pl.ds(pl.multiple_of(chunk * 128, 128), 128)
        query, key, value = (filtered(p, chunk) for p in range(3))
        for group in range(2):
            compact = pl.ds(pl.multiple_of(chunk * 64, 16), 64)
            for dst, src in ((keys, key), (values, value)):
                pieces = [src[i * 32 + group * 16 : i * 32 + group * 16 + 16] for i in range(4)]
                dst[group, compact, :] = jnp.concatenate(pieces, axis=0)
        out[0, rows, :] = (key.astype(f32) * value.astype(f32)).astype(bf16)
        out[1, rows, :] = (cotangent[rows, :].astype(f32) * query.astype(f32)).astype(bf16)
        for step in steps:
            if step[0] == s:
                start_out(step, 0)
    kept = []
    for group in range(2):
        copy = pltpu.make_async_copy(
            rows_of(out, me, group), positions_of(arr, me, group), load.at[11 + group]
        )
        copy.start()
        kept.append(copy)

    def dot(a, b):
        return jnp.dot(a, b, preferred_element_type=f32)

    def channel(index):
        return pl.ds(index, BLOCKS, stride=32)

    def block(n):
        return slice(n * LANES, (n + 1) * LANES)

    for n in range(BLOCKS):
        held[2, n * 32 : (n + 1) * 32, :] = filters[:, block(n)]

    def filter_spectra(step, carry):
        signals = [held[2, channel(step * 8 + j), :].astype(bf16) for j in range(8)]
        mixed = dot(first[...], jnp.concatenate(signals, axis=1))
        rows = pl.ds(pl.multiple_of(step * 512, 512), 512)
        acc[rows, :] = dot(turned(mixed, 8, turn[0], turn[1]), second[...])
        return carry

    lax.fori_loop(0, 4, filter_spectra, 0)

    def both_ways(start_at, step, carry):
        index = start_at + step * 4
        signals = [held[s, channel(index + j), :].astype(bf16) for j in range(4) for s in range(2)]
        mixed = dot(first[...], jnp.concatenate(signals, axis=1))
        spectra = dot(turned(mixed, 8, turn[0], turn[1]), second[...])
        rows = pl.ds(pl.multiple_of(index * 64, 256), 256)
        filt = acc[rows, :]
        joined, kept = [], []
        for j in range(4):
            parts = []
            for value in (
                spectra[j * 128 : j * 128 + 64],
                spectra[j * 128 + 64 : j * 128 + 128],
                filt[j * 64 : j * 64 + 64],
            ):
                parts.append((value[:, :LANES], value[:, LANES:]))
            (pr, pi), (wr, wi), (hr, hi) = parts
            joined.append(jnp.concatenate([pr * hr - pi * hi, pr * hi + pi * hr], axis=1))
            joined.append(jnp.concatenate([hr * wr + hi * wi, hr * wi - hi * wr], axis=1))
            kept.append(jnp.concatenate([pr * wr + pi * wi, pr * wi - pi * wr], axis=1))
        fgs[rows, :] = jnp.concatenate(kept, axis=0).astype(bf16)
        back = dot(jnp.concatenate(joined, axis=0).astype(bf16), second_back[...])
        final = dot(first_back[...], unturned(back, 8, turn[0], turn[1]))
        for j in range(4):
            for s in range(2):
                held[s, channel(index + j), :] = final[:, block(2 * j + s)]
        return carry

    def compact_of(group):
        return ret.at[group, :, pl.ds(pl.multiple_of(me * 16, 16), 16), :]

    for group in range(2):
        arrived(*(("out", step, group) for step in steps))
        if group == 0:
            for step in steps:
                start_out(step, 1)
        kept[group].wait()
        own = slice(group * 16, group * 16 + 16)
        for n in range(BLOCKS):
            for s in range(2):
                rows = slice(n * 32 + group * 16, n * 32 + group * 16 + 16)
                held[s, rows, :] = arr[s, own, block(n)].astype(f32)
        lax.fori_loop(0, 4, functools.partial(both_ways, group * 16), 0)
        gain = gains[own, :]
        for n in range(BLOCKS):
            for s in range(2):
                rows = slice(n * 32 + group * 16, n * 32 + group * 16 + 16)
                direct = gain * arr[s, own, block(n)].astype(f32)
                arr[s, own, block(n)] = (held[s, rows, :] + direct).astype(bf16)
        for step in steps:
            src = positions_of(arr, peer_of(*step), group)
            start(("back", step, group), src, compact_of(group), step)
        copy = pltpu.make_async_copy(
            positions_of(arr, me, group), compact_of(group), load.at[13 + group]
        )
        copy.start()
        kept.append(copy)

    def filter_grads(step, carry):
        rows = pl.ds(pl.multiple_of(step * 512, 512), 512)
        back = dot(fgs[rows, :], second_back[...])
        final = dot(first_back[...], unturned(back, 8, turn[0], turn[1]))
        for j in range(8):
            held[2, channel(step * 8 + j), :] = final[:, block(j)]
        return carry

    def stream_grads(group, chunk, carry):
        rows = pl.ds(pl.multiple_of(chunk * 128, 128), 128)
        one, two = ret[group, 0, rows, :].astype(f32), ret[group, 1, rows, :].astype(f32)
        owners = [
            cotangent[pl.ds(pl.multiple_of((chunk * 8 + i) * 32 + group * 16, 16), 16), :]
            for i in range(8)
        ]
        factors = (
            (one, jnp.concatenate(owners, axis=0)),
            (two, values[group, rows, :]),
            (two, keys[group, rows, :]),
        )
        for p, (value, factor) in enumerate(factors):
            grads = (value * factor.astype(f32)).astype(bf16)
            cgx[group * 3 + p, rows, 0:512] = grads
            columns = pl.ds(pl.multiple_of(p * 256 + chunk * 128, 128), 128)
            hout[group, :, columns] = grads[:, 0:128].T[0:16, :]
        return carry

    def tapped(group, p, rows, first, width, kept):
        x = cgx[group * 3 + p, rows, first : first + width].astype(f32)
        total = coltaps[group, rows, p : p + 1] * x
        for j in (1, 2):
            tap = coltaps[group, rows, 3 * j + p : 3 * j + p + 1]
            total = total + tap * pltpu.roll(x, width - j, 1)
        return total[:, :kept].astype(bf16)

    def grad_rows(group, p, chunk):
        return pl.ds(pl.multiple_of(group * 768 + p * 256 + chunk * 128, 128), 128)

    def front(group, chunk, carry):
        rows = pl.ds(pl.multiple_of(chunk * 128, 128), 128)
        for p in range(3):
            pgc[grad_rows(group, p, chunk), 0:384] = tapped(group, p, rows, 0, 512, 384)
        return carry

    def rest(group, chunk, carry):
        rows = pl.ds(pl.multiple_of(chunk * 128, 128), 128)
        for p in range(3):
            columns = pl.ds(pl.multiple_of(p * 256 + chunk * 128, 128), 128)
            edge = hin[group, :, columns].astype(f32)
            edge = jnp.where(me == N_CTX - 1, jnp.zeros_like(edge), edge)
            edge = jnp.concatenate([edge, jnp.zeros((112, 128), f32)], axis=0)
            cgx[group * 3 + p, rows, 512:640] = edge.T.astype(bf16)
            pgc[grad_rows(group, p, chunk), 384:512] = tapped(group, p, rows, 384, 256, 128)
        return carry

    def swap(group, part, first, count):
        places = (pl.ds(group * 768, 768), pl.ds(first, count))
        start(("grads", group, part), pgc.at[places], pgo.at[places], "twin")

    def begin_grads(group):
        arrived(*(("back", step, group) for step in steps))
        kept[2 + group].wait()
        lax.fori_loop(0, 2, functools.partial(stream_grads, group), 0)
        start(("halo", group), hout.at[group], hin.at[group], "last")

    def most_grads(group):
        lax.fori_loop(0, 2, functools.partial(front, group), 0)
        swap(group, 0, 0, 384)

    def last_grads(group):
        arrived(("halo", group))
        lax.fori_loop(0, 2, functools.partial(rest, group), 0)
        swap(group, 1, 384, 128)

    def whole_filter_grads():
        lax.fori_loop(0, 4, filter_grads, 0)
        for n in range(BLOCKS):
            grad[:, block(n)] = held[2, n * 32 : (n + 1) * 32, :]

    def by_position(chunk, carry):
        for p in range(3):
            pieces = []
            for i in range(4):
                for group in range(2):
                    first = group * 768 + p * 256 + chunk * 64 + i * 16
                    pieces.append(pgc[pl.ds(pl.multiple_of(first, 16), 16), :])
            columns = pl.ds(pl.multiple_of(p * 512 + chunk * 128, 128), 128)
            pgt[:, columns] = jnp.concatenate(pieces, axis=0).T
        return carry

    def input_tiles(first):
        def tile(step, carry):
            rows = pl.ds(pl.multiple_of((first + step) * 512, 512), 512)
            ig[:, rows] = lax.dot_general(
                pgt[...],
                wall[pl.ds((first + step) * 2, 2)].reshape(512, 1536),
                (((1,), (1,)), ((), ())),
                preferred_element_type=f32,
            ).astype(bf16)
            return carry

        lax.fori_loop(0, 4, tile, 0)

    def acc_rows(slot, row, count):
        return pl.ds(pl.multiple_of(slot * 768 + row, 16), count)

    def weight_part(slot, group, block, own=True, theirs=True):
        mine = pl.ds(pl.multiple_of((2 * block + core) * 256, 256), 256)
        columns = pl.ds(pl.multiple_of(block * 256, 256), 256)
        rows, kept = slice(group * 768, group * 768 + 768), acc_rows(slot, 0, 768)
        value = dot(pgc[rows, :], tok[16:528, mine]) if own else acc[kept, :]
        if theirs:
            value = value + dot(pgo[rows, :], oth[:, columns])
        acc[kept, :] = value

    def fold(dst, slot, first, last, *terms):
        def chunk(step, carry):
            rows = pl.ds(pl.multiple_of(step * 128, 128), 128)
            total = acc[acc_rows(slot, step * 128, 128), :]
            for term, offset in terms:
                part_rows = pl.ds(pl.multiple_of(step * 128 - offset, 128), 128)
                total = total + term[part_rows, :].astype(f32)
            dst[rows, :] = total.astype(bf16)
            return carry

        lax.fori_loop(first // 128, last // 128, chunk, 0)

    def block_of(y, xh):
        return y * 2 + xh

    y2, yp, ym = lax.rem(y + 2, 4), lax.rem(y + 1, 4), lax.rem(y + 3, 4)
    ztwo, zp, zm = lax.rem(z + 2, 4), lax.rem(z + 1, 4), lax.rem(z + 3, 4)
    xo = 1 - xh
    sides = (1 - xl, xl)
    low, high = pl.ds(0, 384), pl.ds(384, 384)
    parts = (slice(0, 2048), slice(2048, 4096))

    def ig_rows(side, z, first, count):
        return pl.ds(pl.multiple_of((side * 4 + z) * 64 + first, 32), count)

    def ig_add(rows, h, *terms):
        total = ig[rows, parts[h]].astype(f32)
        for term in terms:
            total = total + term[...].astype(f32)
        return total.astype(bf16)

    def z_first(h):
        for k in range(2):
            src = ig.at[ig_rows(sides[k], ztwo, 0, 32), parts[h]]
            start(("z2p", h, k), src, z2.at[h, k, 0], "above")
            src = ig.at[ig_rows(sides[k], ztwo, 32, 32), parts[h]]
            start(("z2m", h, k), src, z2.at[h, k, 1], "below")

    def z_second(h):
        for k in range(2):
            arrived(("z2p", h, k))
            rows = ig_rows(sides[k], zp, 0, 32)
            ig[rows, parts[h]] = ig_add(rows, h, z2.at[h, k, 0])
            src = ig.at[ig_rows(sides[k], zp, 0, 64), parts[h]]
            start(("zfp", h, k), src, zf.at[h, k, 0], "above")
            arrived(("z2m", h, k))
            rows = ig_rows(sides[k], zm, 32, 32)
            ig[rows, parts[h]] = ig_add(rows, h, z2.at[h, k, 1])
            src = ig.at[ig_rows(sides[k], zm, 0, 64), parts[h]]
            start(("zfm", h, k), src, zf.at[h, k, 1], "below")

    def z_across(h):
        arrived(("zfp", h, 0), ("zfm", h, 0))
        rows = ig_rows(sides[0], z, 0, 64)
        ig[rows, parts[h]] = ig_add(rows, h, zf.at[h, 0, 0], zf.at[h, 0, 1])
        start(("xz", h), ig.at[rows, parts[h]], xz.at[h], "near")

    def z_last(h):
        arrived(("zfp", h, 1), ("zfm", h, 1), ("xz", h))
        rows = ig_rows(sides[1], z, 0, 64)
        ig_out[:, parts[h]] = ig_add(rows, h, zf.at[h, 1, 0], zf.at[h, 1, 1], xz.at[h])

    early = ((y2, xo), (yp, xo), (ym, xo))

    def own_halves(group):
        for n, place in enumerate(early):
            weight_part(3 * group + n, group, block_of(*place), theirs=False)

    def first_blocks(group):
        arrived(("grads", group, 0), ("grads", group, 1))
        for n, place in enumerate(early):
            slot = 3 * group + n
            weight_part(slot, group, block_of(*place), own=False)
            fold(part.at[group, n], slot, 0, 768)
            dst = (xin.at[group], rf.at[group, 0, 0], rf.at[group, 0, 1])[n]
            peer = ("across", "up", "down")[n]
            start((peer, 0, group), part.at[group, n], dst, peer)

    def second_blocks(group):
        weight_part(0, group, block_of(y2, xh))
        arrived(("across", 0, group))
        fold(part.at[group, 3], 0, 0, 768, (xin.at[group], 0))
        start(("up", 2, group), part.at[group, 3, low], r2.at[group, 0], "up")
        start(("down", 2, group), part.at[group, 3, high], r2.at[group, 1], "down")

    def free_halves(group):
        weight_part(2 * group, group, block_of(yp, xh))
        fold(part.at[group, 4], 2 * group, 384, 768)
        start(("upb", 1, group), part.at[group, 4, high], rf.at[group, 1, 0, high], "up")
        weight_part(2 * group + 1, group, block_of(ym, xh))
        fold(part.at[group, 5], 2 * group + 1, 0, 384)
        start(("downa", 1, group), part.at[group, 5, low], rf.at[group, 1, 1, low], "down")

    def side_blocks(group):
        weight_part(4, group, block_of(y, xo))
        arrived(("up", 0, group), ("down", 0, group))
        sent[("across", 0, group)].wait_send()
        terms = ((rf.at[group, 0, 0], 0), (rf.at[group, 0, 1], 0))
        fold(part.at[group, 0], 4, 0, 768, *terms)
        start(("across", 1, group), part.at[group, 0], xr.at[group], "across")

    def bound_halves(group):
        arrived(("up", 2, group))
        fold(part.at[group, 4], 2 * group, 0, 384, (r2.at[group, 0], 0))
        start(("upa", 1, group), part.at[group, 4, low], rf.at[group, 1, 0, low], "up")
        arrived(("down", 2, group))
        fold(part.at[group, 5], 2 * group + 1, 384, 768, (r2.at[group, 1], 384))
        start(("downb", 1, group), part.at[group, 5, high], rf.at[group, 1, 1, high], "down")

    def own_blocks(group):
        names = (("across", 1), ("upa", 1), ("upb", 1), ("downa", 1), ("downb", 1))
        arrived(*((*name, group) for name in names))

        def chunk(step, carry):
            rows = pl.ds(pl.multiple_of(step * 128, 128), 128)
            place = acc_rows(4 + group, step * 128, 128)
            total = acc[place, :]
            for term in (rf.at[group, 1, 0], rf.at[group, 1, 1], xr.at[group]):
                total = total + term[rows, :].astype(f32)
            acc[place, :] = total
            return carry

        lax.fori_loop(0, 6, chunk, 0)

    def last_fold(step, carry):
        p, chunk = step // 4, lax.rem(step, 4)
        pieces = []
        for i in range(4):
            for group in range(2):
                pieces.append(acc[acc_rows(4 + group, p * 256 + chunk * 64 + i * 16, 16), :])
        columns = pl.ds(pl.multiple_of(chunk * 128, 128), 128)
        wg_out[p, :, columns] = jnp.concatenate(pieces, axis=0).T.astype(bf16)
        return carry

    begin_grads(0)
    most_grads(0)
    whole_filter_grads()
    last_grads(0)
    own_halves(0)
    begin_grads(1)
    first_blocks(0)
    most_grads(1)
    last_grads(1)
    lax.fori_loop(0, 4, by_position, 0)
    input_tiles(0)
    z_first(0)
    own_halves(1)
    first_blocks(1)
    second_blocks(0)
    input_tiles(4)
    z_first(1)
    second_blocks(1)
    z_second(0)
    free_halves(0)
    free_halves(1)
    side_blocks(0)
    side_blocks(1)
    z_second(1)
    bound_halves(0)
    bound_halves(1)
    for group in range(2):
        weight_part(4 + group, group, block_of(y, xh))
    z_across(0)
    z_across(1)
    own_blocks(0)
    z_last(0)
    z_last(1)
    own_blocks(1)
    lax.fori_loop(0, 12, last_fold, 0)
    for name, copy in sent.items():
        if name[:2] != ("across", 0):
            copy.wait_send()


def mixer(tokens, weight, out_grad, short_taps, long_filter, skip_bias):
    bf16, f32 = jnp.bfloat16, jnp.float32
    vmem = lambda *shape: pltpu.VMEM(shape, bf16)
    wide = lambda *shape: pltpu.VMEM(shape, f32)
    return pl.pallas_call(
        mixer_kernel,
        out_shape=(
            jax.ShapeDtypeStruct((64, 4096), bf16),
            jax.ShapeDtypeStruct((3, 256, 512), bf16),
            jax.ShapeDtypeStruct((32, BLOCKS * LANES), f32),
        ),
        in_specs=[ANY] * 11,
        out_specs=(IN_VMEM,) * 3,
        scratch_shapes=[
            vmem(528, 4096),
            vmem(512, 2048),
            vmem(N_CTX, 256, 1536),
            vmem(512, 512),
            wide(3, 3, 512),
            wide(2, 256, 16),
            wide(32, BLOCKS * LANES),
            wide(1, 32),
            wide(32, LANES),
            vmem(128, 64),
            vmem(256, 256),
            vmem(256, 256),
            vmem(64, 128),
            wide(2, 64, LANES),
            vmem(2, 256, 512),
            vmem(2, 256, 512),
            vmem(2, 512, 512),
            vmem(2, 32, BLOCKS * LANES),
            wide(3, 32 * BLOCKS, LANES),
            vmem(32 * BLOCKS, 2 * LANES),
            vmem(2, 2, 256, 512),
            vmem(6, 256, 640),
            vmem(2, 16, 768),
            vmem(2, 16, 768),
            vmem(1536, 512),
            vmem(512, 1536),
            vmem(1536, 512),
            vmem(512, 4096),
            wide(4608, 256),
            vmem(2, 6, 768, 256),
            vmem(2, 768, 256),
            vmem(2, 2, 384, 256),
            vmem(2, 2, 2, 768, 256),
            vmem(2, 768, 256),
            vmem(2, 2, 2, 32, 2048),
            vmem(2, 2, 2, 64, 2048),
            vmem(2, 64, 2048),
            pltpu.SemaphoreType.DMA((136,)),
            pltpu.SemaphoreType.DMA((136,)),
            pltpu.SemaphoreType.DMA((18,)),
        ],
        compiler_params=pltpu.CompilerParams(
            collective_id=1, has_side_effects=True, vmem_limit_bytes=63 * 1024 * 1024
        ),
    )(
        tokens, weight, out_grad, short_taps, long_filter, skip_bias.reshape(1, 32), *tables()
    )


def hand_out_kernel(*refs):
    count = (len(refs) - 1) // 3
    given, results, held, sem = refs[:count], refs[count : 2 * count], refs[2 * count : -1], refs[-1]
    inward = [pltpu.make_async_copy(given[n], held[n], sem.at[n]) for n in range(count)]
    outward = [pltpu.make_async_copy(held[n], results[n], sem.at[count + n]) for n in range(count)]
    for copy in inward:
        copy.start()
    for first, then in zip(inward, outward):
        first.wait()
        then.start()
    for copy in outward:
        copy.wait()


def hand_out(results):
    count = len(results)
    return pl.pallas_call(
        hand_out_kernel,
        out_shape=[jax.ShapeDtypeStruct(value.shape, value.dtype) for value in results],
        in_specs=[ANY] * count,
        out_specs=[ANY] * count,
        scratch_shapes=[pltpu.VMEM(value.shape, value.dtype) for value in results]
        + [pltpu.SemaphoreType.DMA((2 * count,))],
        compiler_params=pltpu.CompilerParams(vmem_limit_bytes=63 * 1024 * 1024),
    )(*results)


def on_device(tokens, in_weight, short_taps, long_filter, skip_bias, out_grad):
    weight = jnp.transpose(in_weight, (1, 0, 2))
    results = mixer(tokens, weight, out_grad, short_taps, long_filter, skip_bias)
    input_grad, weight_grad, filter_grad = hand_out(results)
    return input_grad, jnp.transpose(weight_grad, (1, 0, 2)), filter_grad


def solution(mesh):
    in_specs = (
        P("ctx", None),
        P("ctx", None, "tp"),
        P(None, None, "tp"),
        P(("tp", "ctx"), None),
        P(("tp", "ctx")),
        P("tp", "ctx"),
    )
    out_specs = (P(("ctx", "tp"), None), P("ctx", None, "tp"), P(("tp", "ctx"), None))
    return jax.shard_map(
        on_device, mesh=mesh, in_specs=in_specs, out_specs=out_specs, check_vma=False
    )
```

```python
import functools
import math

import jax
import jax.numpy as jnp
import numpy as np
from jax import lax
from jax.experimental import pallas as pl
from jax.experimental.pallas import tpu as pltpu
from jax.sharding import PartitionSpec as P

MESH = pl.DeviceIdType.MESH
ANY = pl.BlockSpec(memory_space=pl.ANY)
IN_VMEM = pl.BlockSpec(memory_space=pltpu.VMEM)
N_CTX = 16
LANES = 128
BLOCKS = 64
GROUP = 4


def tables():
    size = 2 * BLOCKS * LANES
    half = np.arange(BLOCKS) + 0.5
    n = np.arange(BLOCKS)
    m = np.arange(LANES)
    theta = 2 * np.pi * half[:, None] * n[None, :] / LANES
    phi = 2 * np.pi * half[:, None] * m[None, :] / size
    psi = 2 * np.pi * (m[:, None] * m[None, :] % LANES) / LANES
    first = np.concatenate([np.cos(theta), -np.sin(theta)], axis=0)
    second = np.block([[np.cos(psi), -np.sin(psi)], [np.sin(psi), np.cos(psi)]])
    second_back = np.block([[np.cos(psi), np.sin(psi)], [-np.sin(psi), np.cos(psi)]])
    first_back = np.concatenate([np.cos(theta).T, -np.sin(theta).T], axis=1)
    low = lambda value: jnp.asarray(value, jnp.bfloat16)
    turn = jnp.asarray(np.stack([np.cos(phi), np.sin(phi)]), jnp.float32)
    return low(first), low(second), low(second_back), low(first_back), turn


def turned(mixed, count, cos, sin):
    result = []
    for index in range(count):
        at = slice(index * LANES, (index + 1) * LANES)
        re, im = mixed[:BLOCKS, at], mixed[BLOCKS:, at]
        both = jnp.concatenate([re * cos + im * sin, im * cos - re * sin], axis=1)
        result.append(both.astype(jnp.bfloat16))
    return jnp.concatenate(result, axis=0)


def unturned(back, count, cos, sin):
    size = 2 * BLOCKS * LANES
    cos, sin = cos * (2.0 / size), sin * (2.0 / size)
    result = []
    for index in range(count):
        rows = slice(index * BLOCKS, (index + 1) * BLOCKS)
        re, im = back[rows, :LANES], back[rows, LANES:]
        both = jnp.concatenate([re * cos - im * sin, im * cos + re * sin], axis=0)
        result.append(both.astype(jnp.bfloat16))
    return jnp.concatenate(result, axis=1)


def places():
    me, b = lax.axis_index("ctx"), lax.axis_index("tp")
    core, xh, y = lax.rem(me, 2), lax.rem(me // 2, 2), me // 4
    z, xl = lax.rem(b, 4), b // 4
    ctx_of = lambda y, xh: (y * 2 + xh) * 2 + core
    return dict(
        core=core,
        xh=xh,
        y=y,
        z=z,
        xl=xl,
        twin={"ctx": me + 1 - 2 * core},
        up={"ctx": ctx_of(lax.rem(y + 1, 4), xh)},
        down={"ctx": ctx_of(lax.rem(y + 3, 4), xh)},
        near={"ctx": me, "tp": (1 - xl) * 4 + z},
        far={"ctx": ctx_of(y, 1 - xh), "tp": (1 - xl) * 4 + z},
        above={"tp": xl * 4 + lax.rem(z + 1, 4)},
        below={"tp": xl * 4 + lax.rem(z + 3, 4)},
    )


def greet(peers):
    barrier = pltpu.get_barrier_semaphore()
    for peer in peers:
        pl.semaphore_signal(barrier, inc=1, device_id=peer, device_id_type=MESH)
    pl.semaphore_wait(barrier, len(peers))


def rows_of(ref, index, group):
    first = pl.multiple_of(index * 32 + group * 16, 16)
    return ref.at[:, pl.ds(first, 16), :]


def positions_of(ref, index, group):
    return ref.at[:, pl.ds(group * 16, 16), pl.ds(pl.multiple_of(index * 512, 512), 512)]


def mixer_kernel(
    tokens, weight, cotangent_in, taps_in, filters_in, bias_in, first_in, second_in,
    second_back_in, first_back_in, turn_in, ig_out, wg_out, grad,
    tok, oth, wall, cotangent, taps, coltaps, filters, bias, gains, first, second, second_back, first_back,
    turn, keys, values, out, arr, held, fgs, ret, cgx, hout, hin, pgc, pgt, pgo, ig, acc, part,
    xin, r2, rf, xr, z2, zf, xz, send, recv, load,
):
    f32, bf16 = jnp.float32, jnp.bfloat16
    at = places()
    core, xh, y, z, xl = at["core"], at["xh"], at["y"], at["z"], at["xl"]
    me = lax.axis_index("ctx")
    at["across"] = {"ctx": (y * 2 + 1 - xh) * 2 + core}
    at["next"] = {"ctx": lax.rem(me + 1, N_CTX)}
    steps = [(s, i) for s in range(4) for i in range(4)][1:]
    fourth = lax.rem(me, 4)

    def peer_of(s, i):
        return lax.rem(y + s, 4) * 4 + lax.rem(fourth + i, 4)

    for step in steps:
        at[step] = {"ctx": peer_of(*step)}
    at["last"] = {"ctx": lax.rem(me + N_CTX - 1, N_CTX)}
    fetched = [
        (tokens, tok.at[pl.ds(16, 512)]),
        (cotangent_in, cotangent),
        (taps_in, taps),
        (filters_in, filters),
        (bias_in, bias),
        (first_in, first),
        (second_in, second),
        (second_back_in, second_back),
        (first_back_in, first_back),
        (turn_in, turn),
    ]
    loads = [
        pltpu.make_async_copy(src, dst, load.at[index]) for index, (src, dst) in enumerate(fetched)
    ]
    own_weight = [
        pltpu.make_async_copy(
            weight.at[p], wall.at[me, :, pl.ds(p * 512, 512)], load.at[15 + p]
        )
        for p in range(3)
    ]
    for one in (*own_weight, *loads):
        one.start()
    greet([at[name] for name in (*steps, "near", "above", "below")])
    sent = {}

    def start(name, src, dst, peer):
        index = len(sent)
        copy = pltpu.make_async_remote_copy(
            src_ref=src,
            dst_ref=dst,
            send_sem=send.at[index],
            recv_sem=recv.at[index],
            device_id=at[peer],
            device_id_type=MESH,
        )
        copy.start()
        sent[name] = copy

    def arrived(*names):
        for name in names:
            sent[name].wait_recv()

    halves = (pl.ds(0, 128), pl.ds(128, 128))

    def half_of(index, half):
        return wall.at[index, halves[half]]

    def pass_on(name, index, half, peer):
        start(name, half_of(index, half), half_of(index, half), peer)

    def hand_over(name, index):
        start(name, wall.at[index], wall.at[index], "twin")

    def multiply(index, fresh=False):
        pair = index // 2
        columns = pl.ds(pl.multiple_of(pair * 512, 512), 512)

        def tile(step, carry):
            place = pl.ds(pl.multiple_of(step * 512, 512), 512)
            value = jnp.dot(
                tok[:, columns],
                wall[pl.ds(pair * 2, 2), :, place].reshape(512, 512),
                preferred_element_type=f32,
            )
            for half in range(2):
                rows = pl.ds(pl.multiple_of(step * 1056 + half * 528, 16), 528)
                piece = value[:, half * 256 : half * 256 + 256]
                acc[rows, :] = piece if fresh else acc[rows, :] + piece
            return carry

        lax.fori_loop(0, 3, tile, 0)

    def ctx_of(y, xh):
        return (lax.rem(y, 4) * 2 + xh) * 2 + core

    below, above, beyond = ctx_of(y + 3, xh), ctx_of(y + 1, xh), ctx_of(y + 2, xh)
    side = ctx_of(y, 1 - xh)
    side_below, side_above = ctx_of(y + 3, 1 - xh), ctx_of(y + 1, 1 - xh)
    side_beyond = ctx_of(y + 2, 1 - xh)

    for one in own_weight:
        one.wait()
    pass_on("w_up0", me, 0, "up")
    pass_on("w_down1", me, 1, "down")
    start("w_across", wall.at[me], wall.at[me], "across")
    hand_over("w_twin", me)
    start("w_halo", tokens.at[pl.ds(496, 16)], tok.at[pl.ds(0, 16)], "next")
    for j in range(8):
        columns = pl.ds(pl.multiple_of((2 * j + 1 - core) * 256, 256), 256)
        start(("swap", j), tokens.at[:, columns], oth.at[:, pl.ds(j * 256, 256)], "twin")
    arrived("w_up0")
    pass_on("w_on0", below, 0, "up")
    arrived("w_down1")
    pass_on("w_on1", above, 1, "down")
    pass_on("w_up1", me, 1, "up")
    pass_on("w_down0", me, 0, "down")
    for one in loads:
        one.wait()
    arrived("w_halo", "w_twin")
    multiply(me, fresh=True)
    arrived("w_across")
    hand_over("w_twin_side", side)
    arrived("w_on0", "w_on1")
    start("w_across_beyond", wall.at[beyond], wall.at[beyond], "across")
    pass_on("w_side_up0", side, 0, "up")
    pass_on("w_side_down1", side, 1, "down")
    pass_on("w_side_up1", side, 1, "up")
    pass_on("w_side_down0", side, 0, "down")
    hand_over("w_twin_beyond", beyond)
    arrived("w_twin_side")
    multiply(side)
    arrived("w_twin_beyond")
    multiply(beyond)
    arrived("w_up1")
    hand_over("w_twin_below", below)
    arrived("w_down0")
    hand_over("w_twin_above", above)
    arrived("w_twin_below")
    multiply(below)
    arrived("w_twin_above")
    multiply(above)
    arrived("w_side_up0")
    pass_on("w_twin_sb0", side_below, 0, "twin")
    arrived("w_side_down1")
    pass_on("w_twin_sa1", side_above, 1, "twin")
    arrived("w_across_beyond")
    hand_over("w_twin_across", side_beyond)
    arrived("w_twin_across")
    multiply(side_beyond)
    arrived("w_side_up1")
    pass_on("w_twin_sb1", side_below, 1, "twin")
    arrived("w_side_down0")
    pass_on("w_twin_sa0", side_above, 0, "twin")
    arrived("w_twin_sb0", "w_twin_sb1")
    multiply(side_below)
    arrived("w_twin_sa0", "w_twin_sa1")
    multiply(side_above)

    for j in range(8):
        arrived(("swap", j))
    columns = jnp.concatenate([taps[0], taps[1], taps[2], jnp.zeros((7, 512), f32)], axis=0).T
    for group in range(2):
        pieces = [columns[i * 32 + group * 16 : i * 32 + group * 16 + 16] for i in range(N_CTX)]
        coltaps[group] = jnp.concatenate(pieces, axis=0)
    diagonal = lax.broadcasted_iota(jnp.int32, (32, 32), 0) == lax.broadcasted_iota(
        jnp.int32, (32, 32), 1
    )
    gain = jnp.where(diagonal, jnp.broadcast_to(bias[...], (32, 32)), 0.0)
    gains[...] = jnp.broadcast_to(jnp.sum(gain, axis=1, keepdims=True), (32, LANES))

    def head(x):
        edge = x[0:16]
        return jnp.concatenate([jnp.where(me == 0, jnp.zeros_like(edge), edge), x[16:]], axis=0)

    def filtered(p, chunk):
        rows = pl.ds(pl.multiple_of((p * 2 + chunk // 2) * 528, 16), 528)
        columns = pl.ds(pl.multiple_of(lax.rem(chunk, 2) * 128, 128), 128)
        own = pl.ds(pl.multiple_of(chunk * 128, 128), 128)
        x = head(acc[rows, columns].astype(bf16).astype(f32))
        total = taps[0, p : p + 1, own] * x
        for j in (1, 2):
            total = total + taps[j, p : p + 1, own] * pltpu.roll(x, j, 0)
        return total[16:].astype(bf16).T

    def start_out(step, group):
        peer = peer_of(*step)
        start(("out", step, group), rows_of(out, peer, group), positions_of(arr, me, group), step)

    for s in range(4):
        chunk = lax.rem(y + s, 4)
        rows = pl.ds(pl.multiple_of(chunk * 128, 128), 128)
        query, key, value = (filtered(p, chunk) for p in range(3))
        for group in range(2):
            compact = pl.ds(pl.multiple_of(chunk * 64, 16), 64)
            for dst, src in ((keys, key), (values, value)):
                pieces = [src[i * 32 + group * 16 : i * 32 + group * 16 + 16] for i in range(4)]
                dst[group, compact, :] = jnp.concatenate(pieces, axis=0)
        out[0, rows, :] = (key.astype(f32) * value.astype(f32)).astype(bf16)
        out[1, rows, :] = (cotangent[rows, :].astype(f32) * query.astype(f32)).astype(bf16)
        for step in steps:
            if step[0] == s:
                start_out(step, 0)
    kept = []
    for group in range(2):
        copy = pltpu.make_async_copy(
            rows_of(out, me, group), positions_of(arr, me, group), load.at[11 + group]
        )
        copy.start()
        kept.append(copy)

    def dot(a, b):
        return jnp.dot(a, b, preferred_element_type=f32)

    def channel(index):
        return pl.ds(index, BLOCKS, stride=32)

    def block(n):
        return slice(n * LANES, (n + 1) * LANES)

    for n in range(BLOCKS):
        held[2, n * 32 : (n + 1) * 32, :] = filters[:, block(n)]

    def filter_spectra(step, carry):
        signals = [held[2, channel(step * 8 + j), :].astype(bf16) for j in range(8)]
        mixed = dot(first[...], jnp.concatenate(signals, axis=1))
        rows = pl.ds(pl.multiple_of(step * 512, 512), 512)
        acc[rows, :] = dot(turned(mixed, 8, turn[0], turn[1]), second[...])
        return carry

    lax.fori_loop(0, 4, filter_spectra, 0)
    for step in steps:
        start_out(step, 1)

    def both_ways(start_at, step, carry):
        index = start_at + step * 4
        signals = [held[s, channel(index + j), :].astype(bf16) for j in range(4) for s in range(2)]
        mixed = dot(first[...], jnp.concatenate(signals, axis=1))
        spectra = dot(turned(mixed, 8, turn[0], turn[1]), second[...])
        rows = pl.ds(pl.multiple_of(index * 64, 256), 256)
        filt = acc[rows, :]
        joined, kept = [], []
        for j in range(4):
            parts = []
            for value in (
                spectra[j * 128 : j * 128 + 64],
                spectra[j * 128 + 64 : j * 128 + 128],
                filt[j * 64 : j * 64 + 64],
            ):
                parts.append((value[:, :LANES], value[:, LANES:]))
            (pr, pi), (wr, wi), (hr, hi) = parts
            joined.append(jnp.concatenate([pr * hr - pi * hi, pr * hi + pi * hr], axis=1))
            joined.append(jnp.concatenate([hr * wr + hi * wi, hr * wi - hi * wr], axis=1))
            kept.append(jnp.concatenate([pr * wr + pi * wi, pr * wi - pi * wr], axis=1))
        fgs[rows, :] = jnp.concatenate(kept, axis=0).astype(bf16)
        back = dot(jnp.concatenate(joined, axis=0).astype(bf16), second_back[...])
        final = dot(first_back[...], unturned(back, 8, turn[0], turn[1]))
        for j in range(4):
            for s in range(2):
                held[s, channel(index + j), :] = final[:, block(2 * j + s)]
        return carry

    def compact_of(group):
        return ret.at[group, :, pl.ds(pl.multiple_of(me * 16, 16), 16), :]

    for group in range(2):
        arrived(*(("out", step, group) for step in steps))
        kept[group].wait()
        own = slice(group * 16, group * 16 + 16)
        for n in range(BLOCKS):
            for s in range(2):
                rows = slice(n * 32 + group * 16, n * 32 + group * 16 + 16)
                held[s, rows, :] = arr[s, own, block(n)].astype(f32)
        lax.fori_loop(0, 4, functools.partial(both_ways, group * 16), 0)
        gain = gains[own, :]
        for n in range(BLOCKS):
            for s in range(2):
                rows = slice(n * 32 + group * 16, n * 32 + group * 16 + 16)
                direct = gain * arr[s, own, block(n)].astype(f32)
                arr[s, own, block(n)] = (held[s, rows, :] + direct).astype(bf16)
        for step in steps:
            src = positions_of(arr, peer_of(*step), group)
            start(("back", step, group), src, compact_of(group), step)
        copy = pltpu.make_async_copy(
            positions_of(arr, me, group), compact_of(group), load.at[13 + group]
        )
        copy.start()
        kept.append(copy)

    def filter_grads(step, carry):
        rows = pl.ds(pl.multiple_of(step * 512, 512), 512)
        back = dot(fgs[rows, :], second_back[...])
        final = dot(first_back[...], unturned(back, 8, turn[0], turn[1]))
        for j in range(8):
            held[2, channel(step * 8 + j), :] = final[:, block(j)]
        return carry

    def stream_grads(group, chunk, carry):
        rows = pl.ds(pl.multiple_of(chunk * 128, 128), 128)
        one, two = ret[group, 0, rows, :].astype(f32), ret[group, 1, rows, :].astype(f32)
        owners = [
            cotangent[pl.ds(pl.multiple_of((chunk * 8 + i) * 32 + group * 16, 16), 16), :]
            for i in range(8)
        ]
        factors = (
            (one, jnp.concatenate(owners, axis=0)),
            (two, values[group, rows, :]),
            (two, keys[group, rows, :]),
        )
        for p, (value, factor) in enumerate(factors):
            grads = (value * factor.astype(f32)).astype(bf16)
            cgx[group * 3 + p, rows, 0:512] = grads
            columns = pl.ds(pl.multiple_of(p * 256 + chunk * 128, 128), 128)
            hout[group, :, columns] = grads[:, 0:128].T[0:16, :]
        return carry

    def tapped(group, p, rows, first, width, kept):
        x = cgx[group * 3 + p, rows, first : first + width].astype(f32)
        total = coltaps[group, rows, p : p + 1] * x
        for j in (1, 2):
            tap = coltaps[group, rows, 3 * j + p : 3 * j + p + 1]
            total = total + tap * pltpu.roll(x, width - j, 1)
        return total[:, :kept].astype(bf16)

    def grad_rows(group, p, chunk):
        return pl.ds(pl.multiple_of(group * 768 + p * 256 + chunk * 128, 128), 128)

    def front(group, chunk, carry):
        rows = pl.ds(pl.multiple_of(chunk * 128, 128), 128)
        for p in range(3):
            pgc[grad_rows(group, p, chunk), 0:384] = tapped(group, p, rows, 0, 512, 384)
        return carry

    def rest(group, chunk, carry):
        rows = pl.ds(pl.multiple_of(chunk * 128, 128), 128)
        for p in range(3):
            columns = pl.ds(pl.multiple_of(p * 256 + chunk * 128, 128), 128)
            edge = hin[group, :, columns].astype(f32)
            edge = jnp.where(me == N_CTX - 1, jnp.zeros_like(edge), edge)
            edge = jnp.concatenate([edge, jnp.zeros((112, 128), f32)], axis=0)
            cgx[group * 3 + p, rows, 512:640] = edge.T.astype(bf16)
            pgc[grad_rows(group, p, chunk), 384:512] = tapped(group, p, rows, 384, 256, 128)
        return carry

    def swap(group, part, first, count):
        places = (pl.ds(group * 768, 768), pl.ds(first, count))
        start(("grads", group, part), pgc.at[places], pgo.at[places], "twin")

    def begin_grads(group):
        arrived(*(("back", step, group) for step in steps))
        kept[2 + group].wait()
        lax.fori_loop(0, 2, functools.partial(stream_grads, group), 0)
        start(("halo", group), hout.at[group], hin.at[group], "last")

    def most_grads(group):
        lax.fori_loop(0, 2, functools.partial(front, group), 0)
        swap(group, 0, 0, 384)

    def last_grads(group):
        arrived(("halo", group))
        lax.fori_loop(0, 2, functools.partial(rest, group), 0)
        swap(group, 1, 384, 128)

    def whole_filter_grads():
        lax.fori_loop(0, 4, filter_grads, 0)
        for n in range(BLOCKS):
            grad[:, block(n)] = held[2, n * 32 : (n + 1) * 32, :]

    def by_position(chunk, carry):
        for p in range(3):
            pieces = []
            for i in range(4):
                for group in range(2):
                    first = group * 768 + p * 256 + chunk * 64 + i * 16
                    pieces.append(pgc[pl.ds(pl.multiple_of(first, 16), 16), :])
            columns = pl.ds(pl.multiple_of(p * 512 + chunk * 128, 128), 128)
            pgt[:, columns] = jnp.concatenate(pieces, axis=0).T
        return carry

    def input_tiles(first):
        def tile(step, carry):
            rows = pl.ds(pl.multiple_of((first + step) * 512, 512), 512)
            ig[:, rows] = lax.dot_general(
                pgt[...],
                wall[pl.ds((first + step) * 2, 2)].reshape(512, 1536),
                (((1,), (1,)), ((), ())),
                preferred_element_type=f32,
            ).astype(bf16)
            return carry

        lax.fori_loop(0, 4, tile, 0)

    def acc_rows(slot, row, count):
        return pl.ds(pl.multiple_of(slot * 768 + row, 16), count)

    def weight_part(slot, group, block, own=True, theirs=True):
        mine = pl.ds(pl.multiple_of((2 * block + core) * 256, 256), 256)
        columns = pl.ds(pl.multiple_of(block * 256, 256), 256)
        rows, kept = slice(group * 768, group * 768 + 768), acc_rows(slot, 0, 768)
        value = dot(pgc[rows, :], tok[16:528, mine]) if own else acc[kept, :]
        if theirs:
            value = value + dot(pgo[rows, :], oth[:, columns])
        acc[kept, :] = value

    def fold(dst, slot, first, last, *terms):
        def chunk(step, carry):
            rows = pl.ds(pl.multiple_of(step * 128, 128), 128)
            total = acc[acc_rows(slot, step * 128, 128), :]
            for term, offset in terms:
                part_rows = pl.ds(pl.multiple_of(step * 128 - offset, 128), 128)
                total = total + term[part_rows, :].astype(f32)
            dst[rows, :] = total.astype(bf16)
            return carry

        lax.fori_loop(first // 128, last // 128, chunk, 0)

    def block_of(y, xh):
        return y * 2 + xh

    y2, yp, ym = lax.rem(y + 2, 4), lax.rem(y + 1, 4), lax.rem(y + 3, 4)
    ztwo, zp, zm = lax.rem(z + 2, 4), lax.rem(z + 1, 4), lax.rem(z + 3, 4)
    xo = 1 - xh
    sides = (1 - xl, xl)
    low, high = pl.ds(0, 384), pl.ds(384, 384)
    parts = (slice(0, 2048), slice(2048, 4096))

    def ig_rows(side, z, first, count):
        return pl.ds(pl.multiple_of((side * 4 + z) * 64 + first, 32), count)

    def ig_add(rows, h, *terms):
        total = ig[rows, parts[h]].astype(f32)
        for term in terms:
            total = total + term[...].astype(f32)
        return total.astype(bf16)

    def z_first(h):
        for k in range(2):
            src = ig.at[ig_rows(sides[k], ztwo, 0, 32), parts[h]]
            start(("z2p", h, k), src, z2.at[h, k, 0], "above")
            src = ig.at[ig_rows(sides[k], ztwo, 32, 32), parts[h]]
            start(("z2m", h, k), src, z2.at[h, k, 1], "below")

    def z_second(h):
        for k in range(2):
            arrived(("z2p", h, k))
            rows = ig_rows(sides[k], zp, 0, 32)
            ig[rows, parts[h]] = ig_add(rows, h, z2.at[h, k, 0])
            src = ig.at[ig_rows(sides[k], zp, 0, 64), parts[h]]
            start(("zfp", h, k), src, zf.at[h, k, 0], "above")
            arrived(("z2m", h, k))
            rows = ig_rows(sides[k], zm, 32, 32)
            ig[rows, parts[h]] = ig_add(rows, h, z2.at[h, k, 1])
            src = ig.at[ig_rows(sides[k], zm, 0, 64), parts[h]]
            start(("zfm", h, k), src, zf.at[h, k, 1], "below")

    def z_across(h):
        arrived(("zfp", h, 0), ("zfm", h, 0))
        rows = ig_rows(sides[0], z, 0, 64)
        ig[rows, parts[h]] = ig_add(rows, h, zf.at[h, 0, 0], zf.at[h, 0, 1])
        start(("xz", h), ig.at[rows, parts[h]], xz.at[h], "near")

    def z_last(h):
        arrived(("zfp", h, 1), ("zfm", h, 1), ("xz", h))
        rows = ig_rows(sides[1], z, 0, 64)
        ig_out[:, parts[h]] = ig_add(rows, h, zf.at[h, 1, 0], zf.at[h, 1, 1], xz.at[h])

    early = ((y2, xo), (yp, xo), (ym, xo))

    def own_halves(group):
        for n, place in enumerate(early):
            weight_part(3 * group + n, group, block_of(*place), theirs=False)

    def first_blocks(group):
        arrived(("grads", group, 0), ("grads", group, 1))
        for n, place in enumerate(early):
            slot = 3 * group + n
            weight_part(slot, group, block_of(*place), own=False)
            fold(part.at[group, n], slot, 0, 768)
            dst = (xin.at[group], rf.at[group, 0, 0], rf.at[group, 0, 1])[n]
            peer = ("across", "up", "down")[n]
            start((peer, 0, group), part.at[group, n], dst, peer)

    def second_blocks(group):
        weight_part(0, group, block_of(y2, xh))
        arrived(("across", 0, group))
        fold(part.at[group, 3], 0, 0, 768, (xin.at[group], 0))
        start(("up", 2, group), part.at[group, 3, low], r2.at[group, 0], "up")
        start(("down", 2, group), part.at[group, 3, high], r2.at[group, 1], "down")

    def free_halves(group):
        weight_part(2 * group, group, block_of(yp, xh))
        fold(part.at[group, 4], 2 * group, 384, 768)
        start(("upb", 1, group), part.at[group, 4, high], rf.at[group, 1, 0, high], "up")
        weight_part(2 * group + 1, group, block_of(ym, xh))
        fold(part.at[group, 5], 2 * group + 1, 0, 384)
        start(("downa", 1, group), part.at[group, 5, low], rf.at[group, 1, 1, low], "down")

    def side_blocks(group):
        weight_part(4, group, block_of(y, xo))
        arrived(("up", 0, group), ("down", 0, group))
        sent[("across", 0, group)].wait_send()
        terms = ((rf.at[group, 0, 0], 0), (rf.at[group, 0, 1], 0))
        fold(part.at[group, 0], 4, 0, 768, *terms)
        start(("across", 1, group), part.at[group, 0], xr.at[group], "across")

    def bound_halves(group):
        arrived(("up", 2, group))
        fold(part.at[group, 4], 2 * group, 0, 384, (r2.at[group, 0], 0))
        start(("upa", 1, group), part.at[group, 4, low], rf.at[group, 1, 0, low], "up")
        arrived(("down", 2, group))
        fold(part.at[group, 5], 2 * group + 1, 384, 768, (r2.at[group, 1], 384))
        start(("downb", 1, group), part.at[group, 5, high], rf.at[group, 1, 1, high], "down")

    def own_blocks(group):
        names = (("across", 1), ("upa", 1), ("upb", 1), ("downa", 1), ("downb", 1))
        arrived(*((*name, group) for name in names))

        def chunk(step, carry):
            rows = pl.ds(pl.multiple_of(step * 128, 128), 128)
            place = acc_rows(4 + group, step * 128, 128)
            total = acc[place, :]
            for term in (rf.at[group, 1, 0], rf.at[group, 1, 1], xr.at[group]):
                total = total + term[rows, :].astype(f32)
            acc[place, :] = total
            return carry

        lax.fori_loop(0, 6, chunk, 0)

    def last_fold(step, carry):
        p, chunk = step // 4, lax.rem(step, 4)
        pieces = []
        for i in range(4):
            for group in range(2):
                pieces.append(acc[acc_rows(4 + group, p * 256 + chunk * 64 + i * 16, 16), :])
        columns = pl.ds(pl.multiple_of(chunk * 128, 128), 128)
        wg_out[p, :, columns] = jnp.concatenate(pieces, axis=0).T.astype(bf16)
        return carry

    begin_grads(0)
    most_grads(0)
    whole_filter_grads()
    last_grads(0)
    own_halves(0)
    begin_grads(1)
    first_blocks(0)
    most_grads(1)
    last_grads(1)
    lax.fori_loop(0, 4, by_position, 0)
    input_tiles(0)
    z_first(0)
    own_halves(1)
    first_blocks(1)
    second_blocks(0)
    input_tiles(4)
    z_first(1)
    z_second(0)
    side_blocks(0)
    second_blocks(1)
    z_second(1)
    free_halves(0)
    free_halves(1)
    side_blocks(1)
    bound_halves(0)
    z_across(0)
    bound_halves(1)
    for group in range(2):
        weight_part(4 + group, group, block_of(y, xh))
    z_across(1)
    own_blocks(0)
    z_last(0)
    z_last(1)
    own_blocks(1)
    lax.fori_loop(0, 12, last_fold, 0)
    for name, copy in sent.items():
        if name[:2] != ("across", 0):
            copy.wait_send()


def mixer(tokens, weight, out_grad, short_taps, long_filter, skip_bias):
    bf16, f32 = jnp.bfloat16, jnp.float32
    vmem = lambda *shape: pltpu.VMEM(shape, bf16)
    wide = lambda *shape: pltpu.VMEM(shape, f32)
    return pl.pallas_call(
        mixer_kernel,
        out_shape=(
            jax.ShapeDtypeStruct((64, 4096), bf16),
            jax.ShapeDtypeStruct((3, 256, 512), bf16),
            jax.ShapeDtypeStruct((32, BLOCKS * LANES), f32),
        ),
        in_specs=[ANY] * 11,
        out_specs=(IN_VMEM,) * 3,
        scratch_shapes=[
            vmem(528, 4096),
            vmem(512, 2048),
            vmem(N_CTX, 256, 1536),
            vmem(512, 512),
            wide(3, 3, 512),
            wide(2, 256, 16),
            wide(32, BLOCKS * LANES),
            wide(1, 32),
            wide(32, LANES),
            vmem(128, 64),
            vmem(256, 256),
            vmem(256, 256),
            vmem(64, 128),
            wide(2, 64, LANES),
            vmem(2, 256, 512),
            vmem(2, 256, 512),
            vmem(2, 512, 512),
            vmem(2, 32, BLOCKS * LANES),
            wide(3, 32 * BLOCKS, LANES),
            vmem(32 * BLOCKS, 2 * LANES),
            vmem(2, 2, 256, 512),
            vmem(6, 256, 640),
            vmem(2, 16, 768),
            vmem(2, 16, 768),
            vmem(1536, 512),
            vmem(512, 1536),
            vmem(1536, 512),
            vmem(512, 4096),
            wide(4608, 256),
            vmem(2, 6, 768, 256),
            vmem(2, 768, 256),
            vmem(2, 2, 384, 256),
            vmem(2, 2, 2, 768, 256),
            vmem(2, 768, 256),
            vmem(2, 2, 2, 32, 2048),
            vmem(2, 2, 2, 64, 2048),
            vmem(2, 64, 2048),
            pltpu.SemaphoreType.DMA((136,)),
            pltpu.SemaphoreType.DMA((136,)),
            pltpu.SemaphoreType.DMA((18,)),
        ],
        compiler_params=pltpu.CompilerParams(
            collective_id=1, has_side_effects=True, vmem_limit_bytes=63 * 1024 * 1024
        ),
    )(
        tokens, weight, out_grad, short_taps, long_filter, skip_bias.reshape(1, 32), *tables()
    )


def hand_out_kernel(*refs):
    count = (len(refs) - 1) // 3
    given, results, held, sem = refs[:count], refs[count : 2 * count], refs[2 * count : -1], refs[-1]
    inward = [pltpu.make_async_copy(given[n], held[n], sem.at[n]) for n in range(count)]
    outward = [pltpu.make_async_copy(held[n], results[n], sem.at[count + n]) for n in range(count)]
    for copy in inward:
        copy.start()
    for first, then in zip(inward, outward):
        first.wait()
        then.start()
    for copy in outward:
        copy.wait()


def hand_out(results):
    count = len(results)
    return pl.pallas_call(
        hand_out_kernel,
        out_shape=[jax.ShapeDtypeStruct(value.shape, value.dtype) for value in results],
        in_specs=[ANY] * count,
        out_specs=[ANY] * count,
        scratch_shapes=[pltpu.VMEM(value.shape, value.dtype) for value in results]
        + [pltpu.SemaphoreType.DMA((2 * count,))],
        compiler_params=pltpu.CompilerParams(vmem_limit_bytes=63 * 1024 * 1024),
    )(*results)


def on_device(tokens, in_weight, short_taps, long_filter, skip_bias, out_grad):
    weight = jnp.transpose(in_weight, (1, 0, 2))
    results = mixer(tokens, weight, out_grad, short_taps, long_filter, skip_bias)
    input_grad, weight_grad, filter_grad = hand_out(results)
    return input_grad, jnp.transpose(weight_grad, (1, 0, 2)), filter_grad


def solution(mesh):
    in_specs = (
        P("ctx", None),
        P("ctx", None, "tp"),
        P(None, None, "tp"),
        P(("tp", "ctx"), None),
        P(("tp", "ctx")),
        P("tp", "ctx"),
    )
    out_specs = (P(("ctx", "tp"), None), P("ctx", None, "tp"), P(("tp", "ctx"), None))
    return jax.shard_map(
        on_device, mesh=mesh, in_specs=in_specs, out_specs=out_specs, check_vma=False
    )
```

```python
import functools
import math

import jax
import jax.numpy as jnp
import numpy as np
from jax import lax
from jax.experimental import pallas as pl
from jax.experimental.pallas import tpu as pltpu
from jax.sharding import PartitionSpec as P

MESH = pl.DeviceIdType.MESH
ANY = pl.BlockSpec(memory_space=pl.ANY)
IN_VMEM = pl.BlockSpec(memory_space=pltpu.VMEM)
N_CTX = 16
LANES = 128
BLOCKS = 64
GROUP = 4


def tables():
    size = 2 * BLOCKS * LANES
    half = np.arange(BLOCKS) + 0.5
    n = np.arange(BLOCKS)
    m = np.arange(LANES)
    theta = 2 * np.pi * half[:, None] * n[None, :] / LANES
    phi = 2 * np.pi * half[:, None] * m[None, :] / size
    psi = 2 * np.pi * (m[:, None] * m[None, :] % LANES) / LANES
    first = np.concatenate([np.cos(theta), -np.sin(theta)], axis=0)
    second = np.block([[np.cos(psi), -np.sin(psi)], [np.sin(psi), np.cos(psi)]])
    second_back = np.block([[np.cos(psi), np.sin(psi)], [-np.sin(psi), np.cos(psi)]])
    first_back = np.concatenate([np.cos(theta).T, -np.sin(theta).T], axis=1)
    low = lambda value: jnp.asarray(value, jnp.bfloat16)
    turn = jnp.asarray(np.stack([np.cos(phi), np.sin(phi)]), jnp.float32)
    return low(first), low(second), low(second_back), low(first_back), turn


def turned(mixed, count, cos, sin):
    result = []
    for index in range(count):
        at = slice(index * LANES, (index + 1) * LANES)
        re, im = mixed[:BLOCKS, at], mixed[BLOCKS:, at]
        both = jnp.concatenate([re * cos + im * sin, im * cos - re * sin], axis=1)
        result.append(both.astype(jnp.bfloat16))
    return jnp.concatenate(result, axis=0)


def unturned(back, count, cos, sin):
    size = 2 * BLOCKS * LANES
    cos, sin = cos * (2.0 / size), sin * (2.0 / size)
    result = []
    for index in range(count):
        rows = slice(index * BLOCKS, (index + 1) * BLOCKS)
        re, im = back[rows, :LANES], back[rows, LANES:]
        both = jnp.concatenate([re * cos - im * sin, im * cos + re * sin], axis=0)
        result.append(both.astype(jnp.bfloat16))
    return jnp.concatenate(result, axis=1)


def places():
    me, b = lax.axis_index("ctx"), lax.axis_index("tp")
    core, xh, y = lax.rem(me, 2), lax.rem(me // 2, 2), me // 4
    z, xl = lax.rem(b, 4), b // 4
    ctx_of = lambda y, xh: (y * 2 + xh) * 2 + core
    return dict(
        core=core,
        xh=xh,
        y=y,
        z=z,
        xl=xl,
        twin={"ctx": me + 1 - 2 * core},
        up={"ctx": ctx_of(lax.rem(y + 1, 4), xh)},
        down={"ctx": ctx_of(lax.rem(y + 3, 4), xh)},
        near={"ctx": me, "tp": (1 - xl) * 4 + z},
        far={"ctx": ctx_of(y, 1 - xh), "tp": (1 - xl) * 4 + z},
        above={"tp": xl * 4 + lax.rem(z + 1, 4)},
        below={"tp": xl * 4 + lax.rem(z + 3, 4)},
    )


def greet(peers):
    barrier = pltpu.get_barrier_semaphore()
    for peer in peers:
        pl.semaphore_signal(barrier, inc=1, device_id=peer, device_id_type=MESH)
    pl.semaphore_wait(barrier, len(peers))


def rows_of(ref, index, group):
    first = pl.multiple_of(index * 32 + group * 16, 16)
    return ref.at[:, pl.ds(first, 16), :]


def positions_of(ref, index, group):
    return ref.at[:, pl.ds(group * 16, 16), pl.ds(pl.multiple_of(index * 512, 512), 512)]


def mixer_kernel(
    tokens, weight, cotangent_in, taps_in, filters_in, bias_in, first_in, second_in,
    second_back_in, first_back_in, turn_in, ig_out, wg_out, grad,
    tok, oth, wall, cotangent, taps, coltaps, filters, bias, gains, first, second, second_back, first_back,
    turn, keys, values, out, arr, held, fgs, ret, cgx, hout, hin, pgc, pgt, pgo, ig, acc, part,
    xin, r2, rf, xr, z2, zf, xz, send, recv, load,
):
    f32, bf16 = jnp.float32, jnp.bfloat16
    at = places()
    core, xh, y, z, xl = at["core"], at["xh"], at["y"], at["z"], at["xl"]
    me = lax.axis_index("ctx")
    at["across"] = {"ctx": (y * 2 + 1 - xh) * 2 + core}
    at["next"] = {"ctx": lax.rem(me + 1, N_CTX)}
    steps = [(s, i) for s in range(4) for i in range(4)][1:]
    fourth = lax.rem(me, 4)

    def peer_of(s, i):
        return lax.rem(y + s, 4) * 4 + lax.rem(fourth + i, 4)

    for step in steps:
        at[step] = {"ctx": peer_of(*step)}
    at["last"] = {"ctx": lax.rem(me + N_CTX - 1, N_CTX)}
    fetched = [
        (tokens, tok.at[pl.ds(16, 512)]),
        (cotangent_in, cotangent),
        (taps_in, taps),
        (filters_in, filters),
        (bias_in, bias),
        (first_in, first),
        (second_in, second),
        (second_back_in, second_back),
        (first_back_in, first_back),
        (turn_in, turn),
    ]
    loads = [
        pltpu.make_async_copy(src, dst, load.at[index]) for index, (src, dst) in enumerate(fetched)
    ]
    own_weight = [
        pltpu.make_async_copy(
            weight.at[p], wall.at[me, :, pl.ds(p * 512, 512)], load.at[15 + p]
        )
        for p in range(3)
    ]
    for one in (*own_weight, *loads):
        one.start()
    greet([at[name] for name in (*steps, "near", "above", "below")])
    sent = {}

    def start(name, src, dst, peer):
        index = len(sent)
        copy = pltpu.make_async_remote_copy(
            src_ref=src,
            dst_ref=dst,
            send_sem=send.at[index],
            recv_sem=recv.at[index],
            device_id=at[peer],
            device_id_type=MESH,
        )
        copy.start()
        sent[name] = copy

    def arrived(*names):
        for name in names:
            sent[name].wait_recv()

    halves = (pl.ds(0, 128), pl.ds(128, 128))

    def half_of(index, half):
        return wall.at[index, halves[half]]

    def pass_on(name, index, half, peer):
        start(name, half_of(index, half), half_of(index, half), peer)

    def hand_over(name, index):
        start(name, wall.at[index], wall.at[index], "twin")

    def multiply(index, fresh=False):
        pair = index // 2
        columns = pl.ds(pl.multiple_of(pair * 512, 512), 512)

        def tile(step, carry):
            place = pl.ds(pl.multiple_of(step * 512, 512), 512)
            value = jnp.dot(
                tok[:, columns],
                wall[pl.ds(pair * 2, 2), :, place].reshape(512, 512),
                preferred_element_type=f32,
            )
            for half in range(2):
                rows = pl.ds(pl.multiple_of(step * 1056 + half * 528, 16), 528)
                piece = value[:, half * 256 : half * 256 + 256]
                acc[rows, :] = piece if fresh else acc[rows, :] + piece
            return carry

        lax.fori_loop(0, 3, tile, 0)

    def ctx_of(y, xh):
        return (lax.rem(y, 4) * 2 + xh) * 2 + core

    below, above, beyond = ctx_of(y + 3, xh), ctx_of(y + 1, xh), ctx_of(y + 2, xh)
    side = ctx_of(y, 1 - xh)
    side_below, side_above = ctx_of(y + 3, 1 - xh), ctx_of(y + 1, 1 - xh)
    side_beyond = ctx_of(y + 2, 1 - xh)

    for one in own_weight:
        one.wait()
    pass_on("w_up0", me, 0, "up")
    pass_on("w_down1", me, 1, "down")
    start("w_across", wall.at[me], wall.at[me], "across")
    hand_over("w_twin", me)
    start("w_halo", tokens.at[pl.ds(496, 16)], tok.at[pl.ds(0, 16)], "next")
    for j in range(8):
        columns = pl.ds(pl.multiple_of((2 * j + 1 - core) * 256, 256), 256)
        start(("swap", j), tokens.at[:, columns], oth.at[:, pl.ds(j * 256, 256)], "twin")
    arrived("w_up0")
    pass_on("w_on0", below, 0, "up")
    arrived("w_down1")
    pass_on("w_on1", above, 1, "down")
    pass_on("w_up1", me, 1, "up")
    pass_on("w_down0", me, 0, "down")
    for one in loads:
        one.wait()
    arrived("w_halo", "w_twin")
    multiply(me, fresh=True)
    arrived("w_across")
    hand_over("w_twin_side", side)
    arrived("w_on0", "w_on1")
    start("w_across_beyond", wall.at[beyond], wall.at[beyond], "across")
    pass_on("w_side_up0", side, 0, "up")
    pass_on("w_side_down1", side, 1, "down")
    pass_on("w_side_up1", side, 1, "up")
    pass_on("w_side_down0", side, 0, "down")
    hand_over("w_twin_beyond", beyond)
    arrived("w_twin_side")
    multiply(side)
    arrived("w_twin_beyond")
    multiply(beyond)
    arrived("w_up1")
    hand_over("w_twin_below", below)
    arrived("w_down0")
    hand_over("w_twin_above", above)
    arrived("w_twin_below")
    multiply(below)
    arrived("w_twin_above")
    multiply(above)
    arrived("w_side_up0")
    pass_on("w_twin_sb0", side_below, 0, "twin")
    arrived("w_side_down1")
    pass_on("w_twin_sa1", side_above, 1, "twin")
    arrived("w_across_beyond")
    hand_over("w_twin_across", side_beyond)
    arrived("w_side_up1")
    pass_on("w_twin_sb1", side_below, 1, "twin")
    arrived("w_side_down0")
    pass_on("w_twin_sa0", side_above, 0, "twin")
    arrived("w_twin_across")
    multiply(side_beyond)
    arrived("w_twin_sb0", "w_twin_sb1")
    multiply(side_below)
    arrived("w_twin_sa0", "w_twin_sa1")
    multiply(side_above)

    for j in range(8):
        arrived(("swap", j))
    columns = jnp.concatenate([taps[0], taps[1], taps[2], jnp.zeros((7, 512), f32)], axis=0).T
    for group in range(2):
        pieces = [columns[i * 32 + group * 16 : i * 32 + group * 16 + 16] for i in range(N_CTX)]
        coltaps[group] = jnp.concatenate(pieces, axis=0)
    diagonal = lax.broadcasted_iota(jnp.int32, (32, 32), 0) == lax.broadcasted_iota(
        jnp.int32, (32, 32), 1
    )
    gain = jnp.where(diagonal, jnp.broadcast_to(bias[...], (32, 32)), 0.0)
    gains[...] = jnp.broadcast_to(jnp.sum(gain, axis=1, keepdims=True), (32, LANES))

    def head(x):
        edge = x[0:16]
        return jnp.concatenate([jnp.where(me == 0, jnp.zeros_like(edge), edge), x[16:]], axis=0)

    def filtered(p, chunk):
        rows = pl.ds(pl.multiple_of((p * 2 + chunk // 2) * 528, 16), 528)
        columns = pl.ds(pl.multiple_of(lax.rem(chunk, 2) * 128, 128), 128)
        own = pl.ds(pl.multiple_of(chunk * 128, 128), 128)
        x = head(acc[rows, columns].astype(bf16).astype(f32))
        total = taps[0, p : p + 1, own] * x
        for j in (1, 2):
            total = total + taps[j, p : p + 1, own] * pltpu.roll(x, j, 0)
        return total[16:].astype(bf16).T

    def start_out(step, group):
        peer = peer_of(*step)
        start(("out", step, group), rows_of(out, peer, group), positions_of(arr, me, group), step)

    for s in range(4):
        chunk = lax.rem(y + s, 4)
        rows = pl.ds(pl.multiple_of(chunk * 128, 128), 128)
        query, key, value = (filtered(p, chunk) for p in range(3))
        for group in range(2):
            compact = pl.ds(pl.multiple_of(chunk * 64, 16), 64)
            for dst, src in ((keys, key), (values, value)):
                pieces = [src[i * 32 + group * 16 : i * 32 + group * 16 + 16] for i in range(4)]
                dst[group, compact, :] = jnp.concatenate(pieces, axis=0)
        out[0, rows, :] = (key.astype(f32) * value.astype(f32)).astype(bf16)
        out[1, rows, :] = (cotangent[rows, :].astype(f32) * query.astype(f32)).astype(bf16)
        for step in steps:
            if step[0] == s:
                start_out(step, 0)
    kept = []
    for group in range(2):
        copy = pltpu.make_async_copy(
            rows_of(out, me, group), positions_of(arr, me, group), load.at[11 + group]
        )
        copy.start()
        kept.append(copy)

    def dot(a, b):
        return jnp.dot(a, b, preferred_element_type=f32)

    def channel(index):
        return pl.ds(index, BLOCKS, stride=32)

    def block(n):
        return slice(n * LANES, (n + 1) * LANES)

    for n in range(BLOCKS):
        held[2, n * 32 : (n + 1) * 32, :] = filters[:, block(n)]

    def filter_spectra(step, carry):
        signals = [held[2, channel(step * 8 + j), :].astype(bf16) for j in range(8)]
        mixed = dot(first[...], jnp.concatenate(signals, axis=1))
        rows = pl.ds(pl.multiple_of(step * 512, 512), 512)
        acc[rows, :] = dot(turned(mixed, 8, turn[0], turn[1]), second[...])
        return carry

    lax.fori_loop(0, 4, filter_spectra, 0)
    for step in steps:
        start_out(step, 1)

    def both_ways(start_at, step, carry):
        index = start_at + step * 4
        signals = [held[s, channel(index + j), :].astype(bf16) for j in range(4) for s in range(2)]
        mixed = dot(first[...], jnp.concatenate(signals, axis=1))
        spectra = dot(turned(mixed, 8, turn[0], turn[1]), second[...])
        rows = pl.ds(pl.multiple_of(index * 64, 256), 256)
        filt = acc[rows, :]
        joined, kept = [], []
        for j in range(4):
            parts = []
            for value in (
                spectra[j * 128 : j * 128 + 64],
                spectra[j * 128 + 64 : j * 128 + 128],
                filt[j * 64 : j * 64 + 64],
            ):
                parts.append((value[:, :LANES], value[:, LANES:]))
            (pr, pi), (wr, wi), (hr, hi) = parts
            joined.append(jnp.concatenate([pr * hr - pi * hi, pr * hi + pi * hr], axis=1))
            joined.append(jnp.concatenate([hr * wr + hi * wi, hr * wi - hi * wr], axis=1))
            kept.append(jnp.concatenate([pr * wr + pi * wi, pr * wi - pi * wr], axis=1))
        fgs[rows, :] = jnp.concatenate(kept, axis=0).astype(bf16)
        back = dot(jnp.concatenate(joined, axis=0).astype(bf16), second_back[...])
        final = dot(first_back[...], unturned(back, 8, turn[0], turn[1]))
        for j in range(4):
            for s in range(2):
                held[s, channel(index + j), :] = final[:, block(2 * j + s)]
        return carry

    def compact_of(group):
        return ret.at[group, :, pl.ds(pl.multiple_of(me * 16, 16), 16), :]

    for group in range(2):
        arrived(*(("out", step, group) for step in steps))
        kept[group].wait()
        own = slice(group * 16, group * 16 + 16)
        for n in range(BLOCKS):
            for s in range(2):
                rows = slice(n * 32 + group * 16, n * 32 + group * 16 + 16)
                held[s, rows, :] = arr[s, own, block(n)].astype(f32)
        lax.fori_loop(0, 4, functools.partial(both_ways, group * 16), 0)
        gain = gains[own, :]
        for n in range(BLOCKS):
            for s in range(2):
                rows = slice(n * 32 + group * 16, n * 32 + group * 16 + 16)
                direct = gain * arr[s, own, block(n)].astype(f32)
                arr[s, own, block(n)] = (held[s, rows, :] + direct).astype(bf16)
        for step in steps:
            src = positions_of(arr, peer_of(*step), group)
            start(("back", step, group), src, compact_of(group), step)
        copy = pltpu.make_async_copy(
            positions_of(arr, me, group), compact_of(group), load.at[13 + group]
        )
        copy.start()
        kept.append(copy)

    def filter_grads(step, carry):
        rows = pl.ds(pl.multiple_of(step * 512, 512), 512)
        back = dot(fgs[rows, :], second_back[...])
        final = dot(first_back[...], unturned(back, 8, turn[0], turn[1]))
        for j in range(8):
            held[2, channel(step * 8 + j), :] = final[:, block(j)]
        return carry

    def stream_grads(group, chunk, carry):
        rows = pl.ds(pl.multiple_of(chunk * 128, 128), 128)
        one, two = ret[group, 0, rows, :].astype(f32), ret[group, 1, rows, :].astype(f32)
        owners = [
            cotangent[pl.ds(pl.multiple_of((chunk * 8 + i) * 32 + group * 16, 16), 16), :]
            for i in range(8)
        ]
        factors = (
            (one, jnp.concatenate(owners, axis=0)),
            (two, values[group, rows, :]),
            (two, keys[group, rows, :]),
        )
        for p, (value, factor) in enumerate(factors):
            grads = (value * factor.astype(f32)).astype(bf16)
            cgx[group * 3 + p, rows, 0:512] = grads
            columns = pl.ds(pl.multiple_of(p * 256 + chunk * 128, 128), 128)
            hout[group, :, columns] = grads[:, 0:128].T[0:16, :]
        return carry

    def tapped(group, p, rows, first, width, kept):
        x = cgx[group * 3 + p, rows, first : first + width].astype(f32)
        total = coltaps[group, rows, p : p + 1] * x
        for j in (1, 2):
            tap = coltaps[group, rows, 3 * j + p : 3 * j + p + 1]
            total = total + tap * pltpu.roll(x, width - j, 1)
        return total[:, :kept].astype(bf16)

    def grad_rows(group, p, chunk):
        return pl.ds(pl.multiple_of(group * 768 + p * 256 + chunk * 128, 128), 128)

    def front(group, chunk, carry):
        rows = pl.ds(pl.multiple_of(chunk * 128, 128), 128)
        for p in range(3):
            pgc[grad_rows(group, p, chunk), 0:384] = tapped(group, p, rows, 0, 512, 384)
        return carry

    def rest(group, chunk, carry):
        rows = pl.ds(pl.multiple_of(chunk * 128, 128), 128)
        for p in range(3):
            columns = pl.ds(pl.multiple_of(p * 256 + chunk * 128, 128), 128)
            edge = hin[group, :, columns].astype(f32)
            edge = jnp.where(me == N_CTX - 1, jnp.zeros_like(edge), edge)
            edge = jnp.concatenate([edge, jnp.zeros((112, 128), f32)], axis=0)
            cgx[group * 3 + p, rows, 512:640] = edge.T.astype(bf16)
            pgc[grad_rows(group, p, chunk), 384:512] = tapped(group, p, rows, 384, 256, 128)
        return carry

    def swap(group, part, first, count):
        places = (pl.ds(group * 768, 768), pl.ds(first, count))
        start(("grads", group, part), pgc.at[places], pgo.at[places], "twin")

    def begin_grads(group):
        arrived(*(("back", step, group) for step in steps))
        kept[2 + group].wait()
        lax.fori_loop(0, 2, functools.partial(stream_grads, group), 0)
        start(("halo", group), hout.at[group], hin.at[group], "last")

    def most_grads(group):
        lax.fori_loop(0, 2, functools.partial(front, group), 0)
        swap(group, 0, 0, 384)

    def last_grads(group):
        arrived(("halo", group))
        lax.fori_loop(0, 2, functools.partial(rest, group), 0)
        swap(group, 1, 384, 128)

    def whole_filter_grads():
        lax.fori_loop(0, 4, filter_grads, 0)
        for n in range(BLOCKS):
            grad[:, block(n)] = held[2, n * 32 : (n + 1) * 32, :]

    def by_position(chunk, carry):
        for p in range(3):
            pieces = []
            for i in range(4):
                for group in range(2):
                    first = group * 768 + p * 256 + chunk * 64 + i * 16
                    pieces.append(pgc[pl.ds(pl.multiple_of(first, 16), 16), :])
            columns = pl.ds(pl.multiple_of(p * 512 + chunk * 128, 128), 128)
            pgt[:, columns] = jnp.concatenate(pieces, axis=0).T
        return carry

    def input_tiles(first):
        def tile(step, carry):
            rows = pl.ds(pl.multiple_of((first + step) * 512, 512), 512)
            ig[:, rows] = lax.dot_general(
                pgt[...],
                wall[pl.ds((first + step) * 2, 2)].reshape(512, 1536),
                (((1,), (1,)), ((), ())),
                preferred_element_type=f32,
            ).astype(bf16)
            return carry

        lax.fori_loop(0, 4, tile, 0)

    def acc_rows(slot, row, count):
        return pl.ds(pl.multiple_of(slot * 768 + row, 16), count)

    def weight_part(slot, group, block, own=True, theirs=True):
        mine = pl.ds(pl.multiple_of((2 * block + core) * 256, 256), 256)
        columns = pl.ds(pl.multiple_of(block * 256, 256), 256)
        rows, kept = slice(group * 768, group * 768 + 768), acc_rows(slot, 0, 768)
        value = dot(pgc[rows, :], tok[16:528, mine]) if own else acc[kept, :]
        if theirs:
            value = value + dot(pgo[rows, :], oth[:, columns])
        acc[kept, :] = value

    def fold(dst, slot, first, last, *terms):
        def chunk(step, carry):
            rows = pl.ds(pl.multiple_of(step * 128, 128), 128)
            total = acc[acc_rows(slot, step * 128, 128), :]
            for term, offset in terms:
                part_rows = pl.ds(pl.multiple_of(step * 128 - offset, 128), 128)
                total = total + term[part_rows, :].astype(f32)
            dst[rows, :] = total.astype(bf16)
            return carry

        lax.fori_loop(first // 128, last // 128, chunk, 0)

    def block_of(y, xh):
        return y * 2 + xh

    y2, yp, ym = lax.rem(y + 2, 4), lax.rem(y + 1, 4), lax.rem(y + 3, 4)
    ztwo, zp, zm = lax.rem(z + 2, 4), lax.rem(z + 1, 4), lax.rem(z + 3, 4)
    xo = 1 - xh
    sides = (1 - xl, xl)
    low, high = pl.ds(0, 384), pl.ds(384, 384)
    parts = (slice(0, 2048), slice(2048, 4096))

    def ig_rows(side, z, first, count):
        return pl.ds(pl.multiple_of((side * 4 + z) * 64 + first, 32), count)

    def ig_add(rows, h, *terms):
        total = ig[rows, parts[h]].astype(f32)
        for term in terms:
            total = total + term[...].astype(f32)
        return total.astype(bf16)

    def z_first(h):
        for k in range(2):
            src = ig.at[ig_rows(sides[k], ztwo, 0, 32), parts[h]]
            start(("z2p", h, k), src, z2.at[h, k, 0], "above")
            src = ig.at[ig_rows(sides[k], ztwo, 32, 32), parts[h]]
            start(("z2m", h, k), src, z2.at[h, k, 1], "below")

    def z_second(h, k):
        arrived(("z2p", h, k))
        rows = ig_rows(sides[k], zp, 0, 32)
        ig[rows, parts[h]] = ig_add(rows, h, z2.at[h, k, 0])
        src = ig.at[ig_rows(sides[k], zp, 0, 64), parts[h]]
        start(("zfp", h, k), src, zf.at[h, k, 0], "above")
        arrived(("z2m", h, k))
        rows = ig_rows(sides[k], zm, 32, 32)
        ig[rows, parts[h]] = ig_add(rows, h, z2.at[h, k, 1])
        src = ig.at[ig_rows(sides[k], zm, 0, 64), parts[h]]
        start(("zfm", h, k), src, zf.at[h, k, 1], "below")

    def z_across(h):
        arrived(("zfp", h, 0), ("zfm", h, 0))
        rows = ig_rows(sides[0], z, 0, 64)
        ig[rows, parts[h]] = ig_add(rows, h, zf.at[h, 0, 0], zf.at[h, 0, 1])
        start(("xz", h), ig.at[rows, parts[h]], xz.at[h], "near")

    def z_last(h):
        arrived(("zfp", h, 1), ("zfm", h, 1), ("xz", h))
        rows = ig_rows(sides[1], z, 0, 64)
        ig_out[:, parts[h]] = ig_add(rows, h, zf.at[h, 1, 0], zf.at[h, 1, 1], xz.at[h])

    early = ((y2, xo), (yp, xo), (ym, xo))

    def own_halves(group):
        for n, place in enumerate(early):
            weight_part(3 * group + n, group, block_of(*place), theirs=False)

    def first_blocks(group):
        arrived(("grads", group, 0), ("grads", group, 1))
        for n, place in enumerate(early):
            slot = 3 * group + n
            weight_part(slot, group, block_of(*place), own=False)
            fold(part.at[group, n], slot, 0, 768)
            dst = (xin.at[group], rf.at[group, 0, 0], rf.at[group, 0, 1])[n]
            peer = ("across", "up", "down")[n]
            start((peer, 0, group), part.at[group, n], dst, peer)

    def second_blocks(group):
        weight_part(0, group, block_of(y2, xh))
        arrived(("across", 0, group))
        fold(part.at[group, 3], 0, 0, 768, (xin.at[group], 0))
        start(("up", 2, group), part.at[group, 3, low], r2.at[group, 0], "up")
        start(("down", 2, group), part.at[group, 3, high], r2.at[group, 1], "down")

    def free_halves(group):
        weight_part(2 * group, group, block_of(yp, xh))
        fold(part.at[group, 4], 2 * group, 384, 768)
        start(("upb", 1, group), part.at[group, 4, high], rf.at[group, 1, 0, high], "up")
        weight_part(2 * group + 1, group, block_of(ym, xh))
        fold(part.at[group, 5], 2 * group + 1, 0, 384)
        start(("downa", 1, group), part.at[group, 5, low], rf.at[group, 1, 1, low], "down")

    def side_blocks(group):
        weight_part(4, group, block_of(y, xo))
        arrived(("up", 0, group), ("down", 0, group))
        sent[("across", 0, group)].wait_send()
        terms = ((rf.at[group, 0, 0], 0), (rf.at[group, 0, 1], 0))
        fold(part.at[group, 0], 4, 0, 768, *terms)
        start(("across", 1, group), part.at[group, 0], xr.at[group], "across")

    def bound_halves(group):
        arrived(("up", 2, group))
        fold(part.at[group, 4], 2 * group, 0, 384, (r2.at[group, 0], 0))
        start(("upa", 1, group), part.at[group, 4, low], rf.at[group, 1, 0, low], "up")
        arrived(("down", 2, group))
        fold(part.at[group, 5], 2 * group + 1, 384, 768, (r2.at[group, 1], 384))
        start(("downb", 1, group), part.at[group, 5, high], rf.at[group, 1, 1, high], "down")

    def own_blocks(group):
        names = (("across", 1), ("upa", 1), ("upb", 1), ("downa", 1), ("downb", 1))
        arrived(*((*name, group) for name in names))

        def chunk(step, carry):
            rows = pl.ds(pl.multiple_of(step * 128, 128), 128)
            place = acc_rows(4 + group, step * 128, 128)
            total = acc[place, :]
            for term in (rf.at[group, 1, 0], rf.at[group, 1, 1], xr.at[group]):
                total = total + term[rows, :].astype(f32)
            acc[place, :] = total
            return carry

        lax.fori_loop(0, 6, chunk, 0)

    def last_fold(step, carry):
        p, chunk = step // 4, lax.rem(step, 4)
        pieces = []
        for i in range(4):
            for group in range(2):
                pieces.append(acc[acc_rows(4 + group, p * 256 + chunk * 64 + i * 16, 16), :])
        columns = pl.ds(pl.multiple_of(chunk * 128, 128), 128)
        wg_out[p, :, columns] = jnp.concatenate(pieces, axis=0).T.astype(bf16)
        return carry

    begin_grads(0)
    most_grads(0)
    whole_filter_grads()
    last_grads(0)
    own_halves(0)
    begin_grads(1)
    first_blocks(0)
    most_grads(1)
    last_grads(1)
    lax.fori_loop(0, 4, by_position, 0)
    input_tiles(0)
    z_first(0)
    own_halves(1)
    first_blocks(1)
    second_blocks(0)
    input_tiles(4)
    z_first(1)
    z_second(0, 0)
    side_blocks(0)
    second_blocks(1)
    z_second(1, 0)
    free_halves(0)
    z_second(0, 1)
    free_halves(1)
    side_blocks(1)
    bound_halves(0)
    z_second(1, 1)
    z_across(0)
    bound_halves(1)
    z_across(1)
    for group in range(2):
        weight_part(4 + group, group, block_of(y, xh))
    own_blocks(0)
    z_last(0)
    z_last(1)
    own_blocks(1)
    lax.fori_loop(0, 12, last_fold, 0)
    for name, copy in sent.items():
        if name[:2] != ("across", 0):
            copy.wait_send()


def mixer(tokens, weight, out_grad, short_taps, long_filter, skip_bias):
    bf16, f32 = jnp.bfloat16, jnp.float32
    vmem = lambda *shape: pltpu.VMEM(shape, bf16)
    wide = lambda *shape: pltpu.VMEM(shape, f32)
    return pl.pallas_call(
        mixer_kernel,
        out_shape=(
            jax.ShapeDtypeStruct((64, 4096), bf16),
            jax.ShapeDtypeStruct((3, 256, 512), bf16),
            jax.ShapeDtypeStruct((32, BLOCKS * LANES), f32),
        ),
        in_specs=[ANY] * 11,
        out_specs=(IN_VMEM,) * 3,
        scratch_shapes=[
            vmem(528, 4096),
            vmem(512, 2048),
            vmem(N_CTX, 256, 1536),
            vmem(512, 512),
            wide(3, 3, 512),
            wide(2, 256, 16),
            wide(32, BLOCKS * LANES),
            wide(1, 32),
            wide(32, LANES),
            vmem(128, 64),
            vmem(256, 256),
            vmem(256, 256),
            vmem(64, 128),
            wide(2, 64, LANES),
            vmem(2, 256, 512),
            vmem(2, 256, 512),
            vmem(2, 512, 512),
            vmem(2, 32, BLOCKS * LANES),
            wide(3, 32 * BLOCKS, LANES),
            vmem(32 * BLOCKS, 2 * LANES),
            vmem(2, 2, 256, 512),
            vmem(6, 256, 640),
            vmem(2, 16, 768),
            vmem(2, 16, 768),
            vmem(1536, 512),
            vmem(512, 1536),
            vmem(1536, 512),
            vmem(512, 4096),
            wide(4608, 256),
            vmem(2, 6, 768, 256),
            vmem(2, 768, 256),
            vmem(2, 2, 384, 256),
            vmem(2, 2, 2, 768, 256),
            vmem(2, 768, 256),
            vmem(2, 2, 2, 32, 2048),
            vmem(2, 2, 2, 64, 2048),
            vmem(2, 64, 2048),
            pltpu.SemaphoreType.DMA((136,)),
            pltpu.SemaphoreType.DMA((136,)),
            pltpu.SemaphoreType.DMA((18,)),
        ],
        compiler_params=pltpu.CompilerParams(
            collective_id=1, has_side_effects=True, vmem_limit_bytes=63 * 1024 * 1024
        ),
    )(
        tokens, weight, out_grad, short_taps, long_filter, skip_bias.reshape(1, 32), *tables()
    )


def hand_out_kernel(*refs):
    count = (len(refs) - 1) // 3
    given, results, held, sem = refs[:count], refs[count : 2 * count], refs[2 * count : -1], refs[-1]
    inward = [pltpu.make_async_copy(given[n], held[n], sem.at[n]) for n in range(count)]
    outward = [pltpu.make_async_copy(held[n], results[n], sem.at[count + n]) for n in range(count)]
    for copy in inward:
        copy.start()
    for first, then in zip(inward, outward):
        first.wait()
        then.start()
    for copy in outward:
        copy.wait()


def hand_out(results):
    count = len(results)
    return pl.pallas_call(
        hand_out_kernel,
        out_shape=[jax.ShapeDtypeStruct(value.shape, value.dtype) for value in results],
        in_specs=[ANY] * count,
        out_specs=[ANY] * count,
        scratch_shapes=[pltpu.VMEM(value.shape, value.dtype) for value in results]
        + [pltpu.SemaphoreType.DMA((2 * count,))],
        compiler_params=pltpu.CompilerParams(vmem_limit_bytes=63 * 1024 * 1024),
    )(*results)


def on_device(tokens, in_weight, short_taps, long_filter, skip_bias, out_grad):
    weight = jnp.transpose(in_weight, (1, 0, 2))
    results = mixer(tokens, weight, out_grad, short_taps, long_filter, skip_bias)
    input_grad, weight_grad, filter_grad = hand_out(results)
    return input_grad, jnp.transpose(weight_grad, (1, 0, 2)), filter_grad


def solution(mesh):
    in_specs = (
        P("ctx", None),
        P("ctx", None, "tp"),
        P(None, None, "tp"),
        P(("tp", "ctx"), None),
        P(("tp", "ctx")),
        P("tp", "ctx"),
    )
    out_specs = (P(("ctx", "tp"), None), P("ctx", None, "tp"), P(("tp", "ctx"), None))
    return jax.shard_map(
        on_device, mesh=mesh, in_specs=in_specs, out_specs=out_specs, check_vma=False
    )
```

```python
import functools
import math

import jax
import jax.numpy as jnp
import numpy as np
from jax import lax
from jax.experimental import pallas as pl
from jax.experimental.pallas import tpu as pltpu
from jax.sharding import PartitionSpec as P

MESH = pl.DeviceIdType.MESH
ANY = pl.BlockSpec(memory_space=pl.ANY)
IN_VMEM = pl.BlockSpec(memory_space=pltpu.VMEM)
N_CTX = 16
LANES = 128
BLOCKS = 64
GROUP = 4


def tables():
    size = 2 * BLOCKS * LANES
    half = np.arange(BLOCKS) + 0.5
    n = np.arange(BLOCKS)
    m = np.arange(LANES)
    theta = 2 * np.pi * half[:, None] * n[None, :] / LANES
    phi = 2 * np.pi * half[:, None] * m[None, :] / size
    psi = 2 * np.pi * (m[:, None] * m[None, :] % LANES) / LANES
    first = np.concatenate([np.cos(theta), -np.sin(theta)], axis=0)
    second = np.block([[np.cos(psi), -np.sin(psi)], [np.sin(psi), np.cos(psi)]])
    second_back = np.block([[np.cos(psi), np.sin(psi)], [-np.sin(psi), np.cos(psi)]])
    first_back = np.concatenate([np.cos(theta).T, -np.sin(theta).T], axis=1)
    low = lambda value: jnp.asarray(value, jnp.bfloat16)
    turn = jnp.asarray(np.stack([np.cos(phi), np.sin(phi)]), jnp.float32)
    return low(first), low(second), low(second_back), low(first_back), turn


def turned(mixed, count, cos, sin):
    result = []
    for index in range(count):
        at = slice(index * LANES, (index + 1) * LANES)
        re, im = mixed[:BLOCKS, at], mixed[BLOCKS:, at]
        both = jnp.concatenate([re * cos + im * sin, im * cos - re * sin], axis=1)
        result.append(both.astype(jnp.bfloat16))
    return jnp.concatenate(result, axis=0)


def unturned(back, count, cos, sin):
    size = 2 * BLOCKS * LANES
    cos, sin = cos * (2.0 / size), sin * (2.0 / size)
    result = []
    for index in range(count):
        rows = slice(index * BLOCKS, (index + 1) * BLOCKS)
        re, im = back[rows, :LANES], back[rows, LANES:]
        both = jnp.concatenate([re * cos - im * sin, im * cos + re * sin], axis=0)
        result.append(both.astype(jnp.bfloat16))
    return jnp.concatenate(result, axis=1)


def places():
    me, b = lax.axis_index("ctx"), lax.axis_index("tp")
    core, xh, y = lax.rem(me, 2), lax.rem(me // 2, 2), me // 4
    z, xl = lax.rem(b, 4), b // 4
    ctx_of = lambda y, xh: (y * 2 + xh) * 2 + core
    return dict(
        core=core,
        xh=xh,
        y=y,
        z=z,
        xl=xl,
        twin={"ctx": me + 1 - 2 * core},
        up={"ctx": ctx_of(lax.rem(y + 1, 4), xh)},
        down={"ctx": ctx_of(lax.rem(y + 3, 4), xh)},
        near={"ctx": me, "tp": (1 - xl) * 4 + z},
        far={"ctx": ctx_of(y, 1 - xh), "tp": (1 - xl) * 4 + z},
        above={"tp": xl * 4 + lax.rem(z + 1, 4)},
        below={"tp": xl * 4 + lax.rem(z + 3, 4)},
    )


def greet(peers):
    barrier = pltpu.get_barrier_semaphore()
    for peer in peers:
        pl.semaphore_signal(barrier, inc=1, device_id=peer, device_id_type=MESH)
    pl.semaphore_wait(barrier, len(peers))


def rows_of(ref, index, group):
    first = pl.multiple_of(index * 32 + group * 16, 16)
    return ref.at[:, pl.ds(first, 16), :]


def positions_of(ref, index, group):
    return ref.at[:, pl.ds(group * 16, 16), pl.ds(pl.multiple_of(index * 512, 512), 512)]


def mixer_kernel(
    tokens, weight, cotangent_in, taps_in, filters_in, bias_in, first_in, second_in,
    second_back_in, first_back_in, turn_in, ig_out, wg_out, grad,
    tok, oth, wall, cotangent, taps, coltaps, filters, bias, gains, first, second, second_back, first_back,
    turn, keys, values, out, arr, held, fgs, ret, cgx, hout, hin, pgc, pgt, pgo, ig, acc, part,
    xin, r2, rf, xr, z2, zf, xz, send, recv, load,
):
    f32, bf16 = jnp.float32, jnp.bfloat16
    at = places()
    core, xh, y, z, xl = at["core"], at["xh"], at["y"], at["z"], at["xl"]
    me = lax.axis_index("ctx")
    at["across"] = {"ctx": (y * 2 + 1 - xh) * 2 + core}
    at["next"] = {"ctx": lax.rem(me + 1, N_CTX)}
    steps = [(s, i) for s in range(4) for i in range(4)][1:]
    fourth = lax.rem(me, 4)

    def peer_of(s, i):
        return lax.rem(y + s, 4) * 4 + lax.rem(fourth + i, 4)

    for step in steps:
        at[step] = {"ctx": peer_of(*step)}
    at["last"] = {"ctx": lax.rem(me + N_CTX - 1, N_CTX)}
    fetched = [
        (tokens, tok.at[pl.ds(16, 512)]),
        (cotangent_in, cotangent),
        (taps_in, taps),
        (filters_in, filters),
        (bias_in, bias),
        (first_in, first),
        (second_in, second),
        (second_back_in, second_back),
        (first_back_in, first_back),
        (turn_in, turn),
    ]
    loads = [
        pltpu.make_async_copy(src, dst, load.at[index]) for index, (src, dst) in enumerate(fetched)
    ]
    own_weight = [
        pltpu.make_async_copy(
            weight.at[p], wall.at[me, :, pl.ds(p * 512, 512)], load.at[15 + p]
        )
        for p in range(3)
    ]
    for one in (*own_weight, *loads):
        one.start()
    greet([at[name] for name in (*steps, "near", "above", "below")])
    sent = {}

    def start(name, src, dst, peer):
        index = len(sent)
        copy = pltpu.make_async_remote_copy(
            src_ref=src,
            dst_ref=dst,
            send_sem=send.at[index],
            recv_sem=recv.at[index],
            device_id=at[peer],
            device_id_type=MESH,
        )
        copy.start()
        sent[name] = copy

    def arrived(*names):
        for name in names:
            sent[name].wait_recv()

    halves = (pl.ds(0, 128), pl.ds(128, 128))

    def half_of(index, half):
        return wall.at[index, halves[half]]

    def pass_on(name, index, half, peer):
        start(name, half_of(index, half), half_of(index, half), peer)

    def hand_over(name, index):
        start(name, wall.at[index], wall.at[index], "twin")

    def multiply(index, fresh=False):
        pair = index // 2
        columns = pl.ds(pl.multiple_of(pair * 512, 512), 512)

        def tile(step, carry):
            place = pl.ds(pl.multiple_of(step * 512, 512), 512)
            value = jnp.dot(
                tok[:, columns],
                wall[pl.ds(pair * 2, 2), :, place].reshape(512, 512),
                preferred_element_type=f32,
            )
            for half in range(2):
                rows = pl.ds(pl.multiple_of(step * 1056 + half * 528, 16), 528)
                piece = value[:, half * 256 : half * 256 + 256]
                acc[rows, :] = piece if fresh else acc[rows, :] + piece
            return carry

        lax.fori_loop(0, 3, tile, 0)

    def ctx_of(y, xh):
        return (lax.rem(y, 4) * 2 + xh) * 2 + core

    below, above, beyond = ctx_of(y + 3, xh), ctx_of(y + 1, xh), ctx_of(y + 2, xh)
    side = ctx_of(y, 1 - xh)
    side_below, side_above = ctx_of(y + 3, 1 - xh), ctx_of(y + 1, 1 - xh)
    side_beyond = ctx_of(y + 2, 1 - xh)

    for one in own_weight:
        one.wait()
    pass_on("w_up0", me, 0, "up")
    pass_on("w_down1", me, 1, "down")
    start("w_across", wall.at[me], wall.at[me], "across")
    hand_over("w_twin", me)
    start("w_halo", tokens.at[pl.ds(496, 16)], tok.at[pl.ds(0, 16)], "next")
    for j in range(8):
        columns = pl.ds(pl.multiple_of((2 * j + 1 - core) * 256, 256), 256)
        start(("swap", j), tokens.at[:, columns], oth.at[:, pl.ds(j * 256, 256)], "twin")
    arrived("w_up0")
    pass_on("w_on0", below, 0, "up")
    arrived("w_down1")
    pass_on("w_on1", above, 1, "down")
    for one in loads:
        one.wait()
    arrived("w_halo", "w_twin")
    multiply(me, fresh=True)
    pass_on("w_up1", me, 1, "up")
    pass_on("w_down0", me, 0, "down")
    arrived("w_across")
    hand_over("w_twin_side", side)
    arrived("w_on0", "w_on1")
    start("w_across_beyond", wall.at[beyond], wall.at[beyond], "across")
    pass_on("w_side_up0", side, 0, "up")
    pass_on("w_side_down1", side, 1, "down")
    hand_over("w_twin_beyond", beyond)
    arrived("w_twin_side")
    multiply(side)
    pass_on("w_side_up1", side, 1, "up")
    pass_on("w_side_down0", side, 0, "down")
    arrived("w_twin_beyond")
    multiply(beyond)
    arrived("w_up1")
    hand_over("w_twin_below", below)
    arrived("w_down0")
    hand_over("w_twin_above", above)
    arrived("w_twin_below")
    multiply(below)
    arrived("w_twin_above")
    multiply(above)
    arrived("w_side_up0")
    pass_on("w_twin_sb0", side_below, 0, "twin")
    arrived("w_side_down1")
    pass_on("w_twin_sa1", side_above, 1, "twin")
    arrived("w_across_beyond")
    hand_over("w_twin_across", side_beyond)
    arrived("w_side_up1")
    pass_on("w_twin_sb1", side_below, 1, "twin")
    arrived("w_side_down0")
    pass_on("w_twin_sa0", side_above, 0, "twin")
    arrived("w_twin_across")
    multiply(side_beyond)
    arrived("w_twin_sb0", "w_twin_sb1")
    multiply(side_below)
    arrived("w_twin_sa0", "w_twin_sa1")
    multiply(side_above)

    for j in range(8):
        arrived(("swap", j))
    columns = jnp.concatenate([taps[0], taps[1], taps[2], jnp.zeros((7, 512), f32)], axis=0).T
    for group in range(2):
        pieces = [columns[i * 32 + group * 16 : i * 32 + group * 16 + 16] for i in range(N_CTX)]
        coltaps[group] = jnp.concatenate(pieces, axis=0)
    diagonal = lax.broadcasted_iota(jnp.int32, (32, 32), 0) == lax.broadcasted_iota(
        jnp.int32, (32, 32), 1
    )
    gain = jnp.where(diagonal, jnp.broadcast_to(bias[...], (32, 32)), 0.0)
    gains[...] = jnp.broadcast_to(jnp.sum(gain, axis=1, keepdims=True), (32, LANES))

    def head(x):
        edge = x[0:16]
        return jnp.concatenate([jnp.where(me == 0, jnp.zeros_like(edge), edge), x[16:]], axis=0)

    def filtered(p, chunk):
        rows = pl.ds(pl.multiple_of((p * 2 + chunk // 2) * 528, 16), 528)
        columns = pl.ds(pl.multiple_of(lax.rem(chunk, 2) * 128, 128), 128)
        own = pl.ds(pl.multiple_of(chunk * 128, 128), 128)
        x = head(acc[rows, columns].astype(bf16).astype(f32))
        total = taps[0, p : p + 1, own] * x
        for j in (1, 2):
            total = total + taps[j, p : p + 1, own] * pltpu.roll(x, j, 0)
        return total[16:].astype(bf16).T

    def start_out(step, group):
        peer = peer_of(*step)
        start(("out", step, group), rows_of(out, peer, group), positions_of(arr, me, group), step)

    for s in range(4):
        chunk = lax.rem(y + s, 4)
        rows = pl.ds(pl.multiple_of(chunk * 128, 128), 128)
        query, key, value = (filtered(p, chunk) for p in range(3))
        for group in range(2):
            compact = pl.ds(pl.multiple_of(chunk * 64, 16), 64)
            for dst, src in ((keys, key), (values, value)):
                pieces = [src[i * 32 + group * 16 : i * 32 + group * 16 + 16] for i in range(4)]
                dst[group, compact, :] = jnp.concatenate(pieces, axis=0)
        out[0, rows, :] = (key.astype(f32) * value.astype(f32)).astype(bf16)
        out[1, rows, :] = (cotangent[rows, :].astype(f32) * query.astype(f32)).astype(bf16)
        for step in steps:
            if step[0] == s:
                start_out(step, 0)
    kept = []
    for group in range(2):
        copy = pltpu.make_async_copy(
            rows_of(out, me, group), positions_of(arr, me, group), load.at[11 + group]
        )
        copy.start()
        kept.append(copy)

    def dot(a, b):
        return jnp.dot(a, b, preferred_element_type=f32)

    def channel(index):
        return pl.ds(index, BLOCKS, stride=32)

    def block(n):
        return slice(n * LANES, (n + 1) * LANES)

    for n in range(BLOCKS):
        held[2, n * 32 : (n + 1) * 32, :] = filters[:, block(n)]

    def filter_spectra(step, carry):
        signals = [held[2, channel(step * 8 + j), :].astype(bf16) for j in range(8)]
        mixed = dot(first[...], jnp.concatenate(signals, axis=1))
        rows = pl.ds(pl.multiple_of(step * 512, 512), 512)
        acc[rows, :] = dot(turned(mixed, 8, turn[0], turn[1]), second[...])
        return carry

    lax.fori_loop(0, 4, filter_spectra, 0)
    for step in steps:
        start_out(step, 1)

    def both_ways(start_at, step, carry):
        index = start_at + step * 4
        signals = [held[s, channel(index + j), :].astype(bf16) for j in range(4) for s in range(2)]
        mixed = dot(first[...], jnp.concatenate(signals, axis=1))
        spectra = dot(turned(mixed, 8, turn[0], turn[1]), second[...])
        rows = pl.ds(pl.multiple_of(index * 64, 256), 256)
        filt = acc[rows, :]
        joined, kept = [], []
        for j in range(4):
            parts = []
            for value in (
                spectra[j * 128 : j * 128 + 64],
                spectra[j * 128 + 64 : j * 128 + 128],
                filt[j * 64 : j * 64 + 64],
            ):
                parts.append((value[:, :LANES], value[:, LANES:]))
            (pr, pi), (wr, wi), (hr, hi) = parts
            joined.append(jnp.concatenate([pr * hr - pi * hi, pr * hi + pi * hr], axis=1))
            joined.append(jnp.concatenate([hr * wr + hi * wi, hr * wi - hi * wr], axis=1))
            kept.append(jnp.concatenate([pr * wr + pi * wi, pr * wi - pi * wr], axis=1))
        fgs[rows, :] = jnp.concatenate(kept, axis=0).astype(bf16)
        back = dot(jnp.concatenate(joined, axis=0).astype(bf16), second_back[...])
        final = dot(first_back[...], unturned(back, 8, turn[0], turn[1]))
        for j in range(4):
            for s in range(2):
                held[s, channel(index + j), :] = final[:, block(2 * j + s)]
        return carry

    def compact_of(group):
        return ret.at[group, :, pl.ds(pl.multiple_of(me * 16, 16), 16), :]

    for group in range(2):
        arrived(*(("out", step, group) for step in steps))
        kept[group].wait()
        own = slice(group * 16, group * 16 + 16)
        for n in range(BLOCKS):
            for s in range(2):
                rows = slice(n * 32 + group * 16, n * 32 + group * 16 + 16)
                held[s, rows, :] = arr[s, own, block(n)].astype(f32)
        lax.fori_loop(0, 4, functools.partial(both_ways, group * 16), 0)
        gain = gains[own, :]
        for n in range(BLOCKS):
            for s in range(2):
                rows = slice(n * 32 + group * 16, n * 32 + group * 16 + 16)
                direct = gain * arr[s, own, block(n)].astype(f32)
                arr[s, own, block(n)] = (held[s, rows, :] + direct).astype(bf16)
        for step in steps:
            src = positions_of(arr, peer_of(*step), group)
            start(("back", step, group), src, compact_of(group), step)
        copy = pltpu.make_async_copy(
            positions_of(arr, me, group), compact_of(group), load.at[13 + group]
        )
        copy.start()
        kept.append(copy)

    def filter_grads(step, carry):
        rows = pl.ds(pl.multiple_of(step * 512, 512), 512)
        back = dot(fgs[rows, :], second_back[...])
        final = dot(first_back[...], unturned(back, 8, turn[0], turn[1]))
        for j in range(8):
            held[2, channel(step * 8 + j), :] = final[:, block(j)]
        return carry

    def stream_grads(group, chunk, carry):
        rows = pl.ds(pl.multiple_of(chunk * 128, 128), 128)
        one, two = ret[group, 0, rows, :].astype(f32), ret[group, 1, rows, :].astype(f32)
        owners = [
            cotangent[pl.ds(pl.multiple_of((chunk * 8 + i) * 32 + group * 16, 16), 16), :]
            for i in range(8)
        ]
        factors = (
            (one, jnp.concatenate(owners, axis=0)),
            (two, values[group, rows, :]),
            (two, keys[group, rows, :]),
        )
        for p, (value, factor) in enumerate(factors):
            grads = (value * factor.astype(f32)).astype(bf16)
            cgx[group * 3 + p, rows, 0:512] = grads
            columns = pl.ds(pl.multiple_of(p * 256 + chunk * 128, 128), 128)
            hout[group, :, columns] = grads[:, 0:128].T[0:16, :]
        return carry

    def tapped(group, p, rows, first, width, kept):
        x = cgx[group * 3 + p, rows, first : first + width].astype(f32)
        total = coltaps[group, rows, p : p + 1] * x
        for j in (1, 2):
            tap = coltaps[group, rows, 3 * j + p : 3 * j + p + 1]
            total = total + tap * pltpu.roll(x, width - j, 1)
        return total[:, :kept].astype(bf16)

    def grad_rows(group, p, chunk):
        return pl.ds(pl.multiple_of(group * 768 + p * 256 + chunk * 128, 128), 128)

    def front(group, chunk, carry):
        rows = pl.ds(pl.multiple_of(chunk * 128, 128), 128)
        for p in range(3):
            pgc[grad_rows(group, p, chunk), 0:384] = tapped(group, p, rows, 0, 512, 384)
        return carry

    def rest(group, chunk, carry):
        rows = pl.ds(pl.multiple_of(chunk * 128, 128), 128)
        for p in range(3):
            columns = pl.ds(pl.multiple_of(p * 256 + chunk * 128, 128), 128)
            edge = hin[group, :, columns].astype(f32)
            edge = jnp.where(me == N_CTX - 1, jnp.zeros_like(edge), edge)
            edge = jnp.concatenate([edge, jnp.zeros((112, 128), f32)], axis=0)
            cgx[group * 3 + p, rows, 512:640] = edge.T.astype(bf16)
            pgc[grad_rows(group, p, chunk), 384:512] = tapped(group, p, rows, 384, 256, 128)
        return carry

    def swap(group, part, first, count):
        places = (pl.ds(group * 768, 768), pl.ds(first, count))
        start(("grads", group, part), pgc.at[places], pgo.at[places], "twin")

    def begin_grads(group):
        arrived(*(("back", step, group) for step in steps))
        kept[2 + group].wait()
        lax.fori_loop(0, 2, functools.partial(stream_grads, group), 0)
        start(("halo", group), hout.at[group], hin.at[group], "last")

    def most_grads(group):
        lax.fori_loop(0, 2, functools.partial(front, group), 0)
        swap(group, 0, 0, 384)

    def last_grads(group):
        arrived(("halo", group))
        lax.fori_loop(0, 2, functools.partial(rest, group), 0)
        swap(group, 1, 384, 128)

    def whole_filter_grads():
        lax.fori_loop(0, 4, filter_grads, 0)
        for n in range(BLOCKS):
            grad[:, block(n)] = held[2, n * 32 : (n + 1) * 32, :]

    def by_position(chunk, carry):
        for p in range(3):
            pieces = []
            for i in range(4):
                for group in range(2):
                    first = group * 768 + p * 256 + chunk * 64 + i * 16
                    pieces.append(pgc[pl.ds(pl.multiple_of(first, 16), 16), :])
            columns = pl.ds(pl.multiple_of(p * 512 + chunk * 128, 128), 128)
            pgt[:, columns] = jnp.concatenate(pieces, axis=0).T
        return carry

    def input_tiles(first):
        def tile(step, carry):
            rows = pl.ds(pl.multiple_of((first + step) * 512, 512), 512)
            ig[:, rows] = lax.dot_general(
                pgt[...],
                wall[pl.ds((first + step) * 2, 2)].reshape(512, 1536),
                (((1,), (1,)), ((), ())),
                preferred_element_type=f32,
            ).astype(bf16)
            return carry

        lax.fori_loop(0, 4, tile, 0)

    def acc_rows(slot, row, count):
        return pl.ds(pl.multiple_of(slot * 768 + row, 16), count)

    def weight_part(slot, group, block, own=True, theirs=True):
        mine = pl.ds(pl.multiple_of((2 * block + core) * 256, 256), 256)
        columns = pl.ds(pl.multiple_of(block * 256, 256), 256)
        rows, kept = slice(group * 768, group * 768 + 768), acc_rows(slot, 0, 768)
        value = dot(pgc[rows, :], tok[16:528, mine]) if own else acc[kept, :]
        if theirs:
            value = value + dot(pgo[rows, :], oth[:, columns])
        acc[kept, :] = value

    def fold(dst, slot, first, last, *terms):
        def chunk(step, carry):
            rows = pl.ds(pl.multiple_of(step * 128, 128), 128)
            total = acc[acc_rows(slot, step * 128, 128), :]
            for term, offset in terms:
                part_rows = pl.ds(pl.multiple_of(step * 128 - offset, 128), 128)
                total = total + term[part_rows, :].astype(f32)
            dst[rows, :] = total.astype(bf16)
            return carry

        lax.fori_loop(first // 128, last // 128, chunk, 0)

    def block_of(y, xh):
        return y * 2 + xh

    y2, yp, ym = lax.rem(y + 2, 4), lax.rem(y + 1, 4), lax.rem(y + 3, 4)
    ztwo, zp, zm = lax.rem(z + 2, 4), lax.rem(z + 1, 4), lax.rem(z + 3, 4)
    xo = 1 - xh
    sides = (1 - xl, xl)
    low, high = pl.ds(0, 384), pl.ds(384, 384)
    parts = (slice(0, 2048), slice(2048, 4096))

    def ig_rows(side, z, first, count):
        return pl.ds(pl.multiple_of((side * 4 + z) * 64 + first, 32), count)

    def ig_add(rows, h, *terms):
        total = ig[rows, parts[h]].astype(f32)
        for term in terms:
            total = total + term[...].astype(f32)
        return total.astype(bf16)

    def z_first(h):
        for k in range(2):
            src = ig.at[ig_rows(sides[k], ztwo, 0, 32), parts[h]]
            start(("z2p", h, k), src, z2.at[h, k, 0], "above")
            src = ig.at[ig_rows(sides[k], ztwo, 32, 32), parts[h]]
            start(("z2m", h, k), src, z2.at[h, k, 1], "below")

    def z_second(h, k):
        arrived(("z2p", h, k))
        rows = ig_rows(sides[k], zp, 0, 32)
        ig[rows, parts[h]] = ig_add(rows, h, z2.at[h, k, 0])
        src = ig.at[ig_rows(sides[k], zp, 0, 64), parts[h]]
        start(("zfp", h, k), src, zf.at[h, k, 0], "above")
        arrived(("z2m", h, k))
        rows = ig_rows(sides[k], zm, 32, 32)
        ig[rows, parts[h]] = ig_add(rows, h, z2.at[h, k, 1])
        src = ig.at[ig_rows(sides[k], zm, 0, 64), parts[h]]
        start(("zfm", h, k), src, zf.at[h, k, 1], "below")

    def z_across(h):
        arrived(("zfp", h, 0), ("zfm", h, 0))
        rows = ig_rows(sides[0], z, 0, 64)
        ig[rows, parts[h]] = ig_add(rows, h, zf.at[h, 0, 0], zf.at[h, 0, 1])
        start(("xz", h), ig.at[rows, parts[h]], xz.at[h], "near")

    def z_last(h):
        arrived(("zfp", h, 1), ("zfm", h, 1), ("xz", h))
        rows = ig_rows(sides[1], z, 0, 64)
        ig_out[:, parts[h]] = ig_add(rows, h, zf.at[h, 1, 0], zf.at[h, 1, 1], xz.at[h])

    early = ((yp, xo), (ym, xo), (y2, xo))

    def own_halves(group):
        for n, place in enumerate(early):
            weight_part(3 * group + n, group, block_of(*place), theirs=False)

    def first_blocks(group):
        arrived(("grads", group, 0), ("grads", group, 1))
        for n, place in enumerate(early):
            slot = 3 * group + n
            weight_part(slot, group, block_of(*place), own=False)
            fold(part.at[group, n], slot, 0, 768)
            dst = (rf.at[group, 0, 0], rf.at[group, 0, 1], xin.at[group])[n]
            peer = ("up", "down", "across")[n]
            start((peer, 0, group), part.at[group, n], dst, peer)

    def second_blocks(group):
        weight_part(0, group, block_of(y2, xh))
        arrived(("across", 0, group))
        fold(part.at[group, 3], 0, 0, 768, (xin.at[group], 0))
        start(("up", 2, group), part.at[group, 3, low], r2.at[group, 0], "up")
        start(("down", 2, group), part.at[group, 3, high], r2.at[group, 1], "down")

    def free_halves(group):
        weight_part(2 * group, group, block_of(yp, xh))
        fold(part.at[group, 4], 2 * group, 384, 768)
        start(("upb", 1, group), part.at[group, 4, high], rf.at[group, 1, 0, high], "up")
        weight_part(2 * group + 1, group, block_of(ym, xh))
        fold(part.at[group, 5], 2 * group + 1, 0, 384)
        start(("downa", 1, group), part.at[group, 5, low], rf.at[group, 1, 1, low], "down")

    def side_blocks(group):
        weight_part(4, group, block_of(y, xo))
        arrived(("up", 0, group), ("down", 0, group))
        sent[("across", 0, group)].wait_send()
        terms = ((rf.at[group, 0, 0], 0), (rf.at[group, 0, 1], 0))
        fold(part.at[group, 2], 4, 0, 768, *terms)
        start(("across", 1, group), part.at[group, 2], xr.at[group], "across")

    def bound_halves(group):
        arrived(("up", 2, group))
        fold(part.at[group, 4], 2 * group, 0, 384, (r2.at[group, 0], 0))
        start(("upa", 1, group), part.at[group, 4, low], rf.at[group, 1, 0, low], "up")
        arrived(("down", 2, group))
        fold(part.at[group, 5], 2 * group + 1, 384, 768, (r2.at[group, 1], 384))
        start(("downb", 1, group), part.at[group, 5, high], rf.at[group, 1, 1, high], "down")

    def own_blocks(group):
        names = (("across", 1), ("upa", 1), ("upb", 1), ("downa", 1), ("downb", 1))
        arrived(*((*name, group) for name in names))

        def chunk(step, carry):
            rows = pl.ds(pl.multiple_of(step * 128, 128), 128)
            place = acc_rows(4 + group, step * 128, 128)
            total = acc[place, :]
            for term in (rf.at[group, 1, 0], rf.at[group, 1, 1], xr.at[group]):
                total = total + term[rows, :].astype(f32)
            acc[place, :] = total
            return carry

        lax.fori_loop(0, 6, chunk, 0)

    def last_fold(step, carry):
        p, chunk = step // 4, lax.rem(step, 4)
        pieces = []
        for i in range(4):
            for group in range(2):
                pieces.append(acc[acc_rows(4 + group, p * 256 + chunk * 64 + i * 16, 16), :])
        columns = pl.ds(pl.multiple_of(chunk * 128, 128), 128)
        wg_out[p, :, columns] = jnp.concatenate(pieces, axis=0).T.astype(bf16)
        return carry

    begin_grads(0)
    most_grads(0)
    whole_filter_grads()
    last_grads(0)
    own_halves(0)
    begin_grads(1)
    first_blocks(0)
    most_grads(1)
    last_grads(1)
    lax.fori_loop(0, 4, by_position, 0)
    input_tiles(0)
    z_first(0)
    own_halves(1)
    first_blocks(1)
    second_blocks(0)
    input_tiles(4)
    z_first(1)
    z_second(0, 0)
    side_blocks(0)
    second_blocks(1)
    z_second(1, 0)
    free_halves(0)
    z_second(0, 1)
    free_halves(1)
    side_blocks(1)
    bound_halves(0)
    z_second(1, 1)
    z_across(0)
    bound_halves(1)
    z_across(1)
    for group in range(2):
        weight_part(4 + group, group, block_of(y, xh))
    own_blocks(0)
    z_last(0)
    z_last(1)
    own_blocks(1)
    lax.fori_loop(0, 12, last_fold, 0)
    for name, copy in sent.items():
        if name[:2] != ("across", 0):
            copy.wait_send()


def mixer(tokens, weight, out_grad, short_taps, long_filter, skip_bias):
    bf16, f32 = jnp.bfloat16, jnp.float32
    vmem = lambda *shape: pltpu.VMEM(shape, bf16)
    wide = lambda *shape: pltpu.VMEM(shape, f32)
    return pl.pallas_call(
        mixer_kernel,
        out_shape=(
            jax.ShapeDtypeStruct((64, 4096), bf16),
            jax.ShapeDtypeStruct((3, 256, 512), bf16),
            jax.ShapeDtypeStruct((32, BLOCKS * LANES), f32),
        ),
        in_specs=[ANY] * 11,
        out_specs=(IN_VMEM,) * 3,
        scratch_shapes=[
            vmem(528, 4096),
            vmem(512, 2048),
            vmem(N_CTX, 256, 1536),
            vmem(512, 512),
            wide(3, 3, 512),
            wide(2, 256, 16),
            wide(32, BLOCKS * LANES),
            wide(1, 32),
            wide(32, LANES),
            vmem(128, 64),
            vmem(256, 256),
            vmem(256, 256),
            vmem(64, 128),
            wide(2, 64, LANES),
            vmem(2, 256, 512),
            vmem(2, 256, 512),
            vmem(2, 512, 512),
            vmem(2, 32, BLOCKS * LANES),
            wide(3, 32 * BLOCKS, LANES),
            vmem(32 * BLOCKS, 2 * LANES),
            vmem(2, 2, 256, 512),
            vmem(6, 256, 640),
            vmem(2, 16, 768),
            vmem(2, 16, 768),
            vmem(1536, 512),
            vmem(512, 1536),
            vmem(1536, 512),
            vmem(512, 4096),
            wide(4608, 256),
            vmem(2, 6, 768, 256),
            vmem(2, 768, 256),
            vmem(2, 2, 384, 256),
            vmem(2, 2, 2, 768, 256),
            vmem(2, 768, 256),
            vmem(2, 2, 2, 32, 2048),
            vmem(2, 2, 2, 64, 2048),
            vmem(2, 64, 2048),
            pltpu.SemaphoreType.DMA((136,)),
            pltpu.SemaphoreType.DMA((136,)),
            pltpu.SemaphoreType.DMA((18,)),
        ],
        compiler_params=pltpu.CompilerParams(
            collective_id=1, has_side_effects=True, vmem_limit_bytes=63 * 1024 * 1024
        ),
    )(
        tokens, weight, out_grad, short_taps, long_filter, skip_bias.reshape(1, 32), *tables()
    )


def hand_out_kernel(*refs):
    count = (len(refs) - 1) // 3
    given, results, held, sem = refs[:count], refs[count : 2 * count], refs[2 * count : -1], refs[-1]
    inward = [pltpu.make_async_copy(given[n], held[n], sem.at[n]) for n in range(count)]
    outward = [pltpu.make_async_copy(held[n], results[n], sem.at[count + n]) for n in range(count)]
    for copy in inward:
        copy.start()
    for first, then in zip(inward, outward):
        first.wait()
        then.start()
    for copy in outward:
        copy.wait()


def hand_out(results):
    count = len(results)
    return pl.pallas_call(
        hand_out_kernel,
        out_shape=[jax.ShapeDtypeStruct(value.shape, value.dtype) for value in results],
        in_specs=[ANY] * count,
        out_specs=[ANY] * count,
        scratch_shapes=[pltpu.VMEM(value.shape, value.dtype) for value in results]
        + [pltpu.SemaphoreType.DMA((2 * count,))],
        compiler_params=pltpu.CompilerParams(vmem_limit_bytes=63 * 1024 * 1024),
    )(*results)


def on_device(tokens, in_weight, short_taps, long_filter, skip_bias, out_grad):
    weight = jnp.transpose(in_weight, (1, 0, 2))
    results = mixer(tokens, weight, out_grad, short_taps, long_filter, skip_bias)
    input_grad, weight_grad, filter_grad = hand_out(results)
    return input_grad, jnp.transpose(weight_grad, (1, 0, 2)), filter_grad


def solution(mesh):
    in_specs = (
        P("ctx", None),
        P("ctx", None, "tp"),
        P(None, None, "tp"),
        P(("tp", "ctx"), None),
        P(("tp", "ctx")),
        P("tp", "ctx"),
    )
    out_specs = (P(("ctx", "tp"), None), P("ctx", None, "tp"), P(("tp", "ctx"), None))
    return jax.shard_map(
        on_device, mesh=mesh, in_specs=in_specs, out_specs=out_specs, check_vma=False
    )
```

```python
import functools
import math

import jax
import jax.numpy as jnp
import numpy as np
from jax import lax
from jax.experimental import pallas as pl
from jax.experimental.pallas import tpu as pltpu
from jax.sharding import PartitionSpec as P

MESH = pl.DeviceIdType.MESH
ANY = pl.BlockSpec(memory_space=pl.ANY)
IN_VMEM = pl.BlockSpec(memory_space=pltpu.VMEM)
N_CTX = 16
LANES = 128
BLOCKS = 64
GROUP = 4


def tables():
    size = 2 * BLOCKS * LANES
    half = np.arange(BLOCKS) + 0.5
    n = np.arange(BLOCKS)
    m = np.arange(LANES)
    theta = 2 * np.pi * half[:, None] * n[None, :] / LANES
    phi = 2 * np.pi * half[:, None] * m[None, :] / size
    psi = 2 * np.pi * (m[:, None] * m[None, :] % LANES) / LANES
    first = np.concatenate([np.cos(theta), -np.sin(theta)], axis=0)
    second = np.block([[np.cos(psi), -np.sin(psi)], [np.sin(psi), np.cos(psi)]])
    second_back = np.block([[np.cos(psi), np.sin(psi)], [-np.sin(psi), np.cos(psi)]])
    first_back = np.concatenate([np.cos(theta).T, -np.sin(theta).T], axis=1)
    low = lambda value: jnp.asarray(value, jnp.bfloat16)
    turn = jnp.asarray(np.stack([np.cos(phi), np.sin(phi)]), jnp.float32)
    return low(first), low(second), low(second_back), low(first_back), turn


def turned(mixed, count, cos, sin):
    result = []
    for index in range(count):
        at = slice(index * LANES, (index + 1) * LANES)
        re, im = mixed[:BLOCKS, at], mixed[BLOCKS:, at]
        both = jnp.concatenate([re * cos + im * sin, im * cos - re * sin], axis=1)
        result.append(both.astype(jnp.bfloat16))
    return jnp.concatenate(result, axis=0)


def unturned(back, count, cos, sin):
    size = 2 * BLOCKS * LANES
    cos, sin = cos * (2.0 / size), sin * (2.0 / size)
    result = []
    for index in range(count):
        rows = slice(index * BLOCKS, (index + 1) * BLOCKS)
        re, im = back[rows, :LANES], back[rows, LANES:]
        both = jnp.concatenate([re * cos - im * sin, im * cos + re * sin], axis=0)
        result.append(both.astype(jnp.bfloat16))
    return jnp.concatenate(result, axis=1)


def places():
    me, b = lax.axis_index("ctx"), lax.axis_index("tp")
    core, xh, y = lax.rem(me, 2), lax.rem(me // 2, 2), me // 4
    z, xl = lax.rem(b, 4), b // 4
    ctx_of = lambda y, xh: (y * 2 + xh) * 2 + core
    return dict(
        core=core,
        xh=xh,
        y=y,
        z=z,
        xl=xl,
        twin={"ctx": me + 1 - 2 * core},
        up={"ctx": ctx_of(lax.rem(y + 1, 4), xh)},
        down={"ctx": ctx_of(lax.rem(y + 3, 4), xh)},
        near={"ctx": me, "tp": (1 - xl) * 4 + z},
        far={"ctx": ctx_of(y, 1 - xh), "tp": (1 - xl) * 4 + z},
        above={"tp": xl * 4 + lax.rem(z + 1, 4)},
        below={"tp": xl * 4 + lax.rem(z + 3, 4)},
    )


def greet(peers):
    barrier = pltpu.get_barrier_semaphore()
    for peer in peers:
        pl.semaphore_signal(barrier, inc=1, device_id=peer, device_id_type=MESH)
    pl.semaphore_wait(barrier, len(peers))


def rows_of(ref, index, group):
    first = pl.multiple_of(index * 32 + group * 16, 16)
    return ref.at[:, pl.ds(first, 16), :]


def positions_of(ref, index, group):
    return ref.at[:, pl.ds(group * 16, 16), pl.ds(pl.multiple_of(index * 512, 512), 512)]


def mixer_kernel(
    tokens, weight, cotangent_in, taps_in, filters_in, bias_in, first_in, second_in,
    second_back_in, first_back_in, turn_in, ig_out, wg_out, grad,
    tok, oth, wall, cotangent, taps, coltaps, filters, bias, gains, first, second, second_back, first_back,
    turn, keys, values, out, arr, held, fgs, ret, cgx, hout, hin, pgc, pgt, pgo, ig, acc, part,
    xin, r2, rf, xr, z2, zf, xz, send, recv, load,
):
    f32, bf16 = jnp.float32, jnp.bfloat16
    at = places()
    core, xh, y, z, xl = at["core"], at["xh"], at["y"], at["z"], at["xl"]
    me = lax.axis_index("ctx")
    at["across"] = {"ctx": (y * 2 + 1 - xh) * 2 + core}
    at["next"] = {"ctx": lax.rem(me + 1, N_CTX)}
    steps = [(s, i) for i in range(4) for s in (1, 3, 2, 0) if (s, i) != (0, 0)]
    fourth = lax.rem(me, 4)

    def peer_of(s, i):
        return lax.rem(y + s, 4) * 4 + lax.rem(fourth + i, 4)

    for step in steps:
        at[step] = {"ctx": peer_of(*step)}
    at["last"] = {"ctx": lax.rem(me + N_CTX - 1, N_CTX)}
    fetched = [
        (tokens, tok.at[pl.ds(16, 512)]),
        (cotangent_in, cotangent),
        (taps_in, taps),
        (filters_in, filters),
        (bias_in, bias),
        (first_in, first),
        (second_in, second),
        (second_back_in, second_back),
        (first_back_in, first_back),
        (turn_in, turn),
    ]
    loads = [
        pltpu.make_async_copy(src, dst, load.at[index]) for index, (src, dst) in enumerate(fetched)
    ]
    own_weight = [
        pltpu.make_async_copy(
            weight.at[p], wall.at[me, :, pl.ds(p * 512, 512)], load.at[15 + p]
        )
        for p in range(3)
    ]
    for one in (*own_weight, *loads):
        one.start()
    greet([at[name] for name in (*steps, "near", "above", "below")])
    sent = {}

    def start(name, src, dst, peer):
        index = len(sent)
        copy = pltpu.make_async_remote_copy(
            src_ref=src,
            dst_ref=dst,
            send_sem=send.at[index],
            recv_sem=recv.at[index],
            device_id=at[peer],
            device_id_type=MESH,
        )
        copy.start()
        sent[name] = copy

    def arrived(*names):
        for name in names:
            sent[name].wait_recv()

    halves = (pl.ds(0, 128), pl.ds(128, 128))

    def half_of(index, half):
        return wall.at[index, halves[half]]

    def pass_on(name, index, half, peer):
        start(name, half_of(index, half), half_of(index, half), peer)

    def hand_over(name, index):
        start(name, wall.at[index], wall.at[index], "twin")

    def multiply(index, fresh=False):
        pair = index // 2
        columns = pl.ds(pl.multiple_of(pair * 512, 512), 512)

        def tile(step, carry):
            place = pl.ds(pl.multiple_of(step * 512, 512), 512)
            value = jnp.dot(
                tok[:, columns],
                wall[pl.ds(pair * 2, 2), :, place].reshape(512, 512),
                preferred_element_type=f32,
            )
            for half in range(2):
                rows = pl.ds(pl.multiple_of(step * 1056 + half * 528, 16), 528)
                piece = value[:, half * 256 : half * 256 + 256]
                acc[rows, :] = piece if fresh else acc[rows, :] + piece
            return carry

        lax.fori_loop(0, 3, tile, 0)

    def ctx_of(y, xh):
        return (lax.rem(y, 4) * 2 + xh) * 2 + core

    below, above, beyond = ctx_of(y + 3, xh), ctx_of(y + 1, xh), ctx_of(y + 2, xh)
    side = ctx_of(y, 1 - xh)
    side_below, side_above = ctx_of(y + 3, 1 - xh), ctx_of(y + 1, 1 - xh)
    side_beyond = ctx_of(y + 2, 1 - xh)

    for one in own_weight:
        one.wait()
    pass_on("w_up0", me, 0, "up")
    pass_on("w_down1", me, 1, "down")
    start("w_across", wall.at[me], wall.at[me], "across")
    hand_over("w_twin", me)
    start("w_halo", tokens.at[pl.ds(496, 16)], tok.at[pl.ds(0, 16)], "next")
    for j in range(8):
        columns = pl.ds(pl.multiple_of((2 * j + 1 - core) * 256, 256), 256)
        start(("swap", j), tokens.at[:, columns], oth.at[:, pl.ds(j * 256, 256)], "twin")
    arrived("w_up0")
    pass_on("w_on0", below, 0, "up")
    arrived("w_down1")
    pass_on("w_on1", above, 1, "down")
    for one in loads:
        one.wait()
    arrived("w_halo", "w_twin")
    multiply(me, fresh=True)
    pass_on("w_up1", me, 1, "up")
    pass_on("w_down0", me, 0, "down")
    arrived("w_across")
    hand_over("w_twin_side", side)
    arrived("w_on0", "w_on1")
    start("w_across_beyond", wall.at[beyond], wall.at[beyond], "across")
    pass_on("w_side_up0", side, 0, "up")
    pass_on("w_side_down1", side, 1, "down")
    hand_over("w_twin_beyond", beyond)
    arrived("w_twin_side")
    multiply(side)
    pass_on("w_side_up1", side, 1, "up")
    pass_on("w_side_down0", side, 0, "down")
    arrived("w_twin_beyond")
    multiply(beyond)
    arrived("w_up1")
    hand_over("w_twin_below", below)
    arrived("w_down0")
    hand_over("w_twin_above", above)
    arrived("w_twin_below")
    multiply(below)
    arrived("w_twin_above")
    multiply(above)
    arrived("w_side_up0")
    pass_on("w_twin_sb0", side_below, 0, "twin")
    arrived("w_side_down1")
    pass_on("w_twin_sa1", side_above, 1, "twin")
    arrived("w_across_beyond")
    hand_over("w_twin_across", side_beyond)
    arrived("w_side_up1")
    pass_on("w_twin_sb1", side_below, 1, "twin")
    arrived("w_side_down0")
    pass_on("w_twin_sa0", side_above, 0, "twin")
    arrived("w_twin_across")
    multiply(side_beyond)
    arrived("w_twin_sb0", "w_twin_sb1")
    multiply(side_below)
    arrived("w_twin_sa0", "w_twin_sa1")
    multiply(side_above)

    for j in range(8):
        arrived(("swap", j))
    columns = jnp.concatenate([taps[0], taps[1], taps[2], jnp.zeros((7, 512), f32)], axis=0).T
    for group in range(2):
        pieces = [columns[i * 32 + group * 16 : i * 32 + group * 16 + 16] for i in range(N_CTX)]
        coltaps[group] = jnp.concatenate(pieces, axis=0)
    diagonal = lax.broadcasted_iota(jnp.int32, (32, 32), 0) == lax.broadcasted_iota(
        jnp.int32, (32, 32), 1
    )
    gain = jnp.where(diagonal, jnp.broadcast_to(bias[...], (32, 32)), 0.0)
    gains[...] = jnp.broadcast_to(jnp.sum(gain, axis=1, keepdims=True), (32, LANES))

    def head(x):
        edge = x[0:16]
        return jnp.concatenate([jnp.where(me == 0, jnp.zeros_like(edge), edge), x[16:]], axis=0)

    def filtered(p, chunk):
        rows = pl.ds(pl.multiple_of((p * 2 + chunk // 2) * 528, 16), 528)
        columns = pl.ds(pl.multiple_of(lax.rem(chunk, 2) * 128, 128), 128)
        own = pl.ds(pl.multiple_of(chunk * 128, 128), 128)
        x = head(acc[rows, columns].astype(bf16).astype(f32))
        total = taps[0, p : p + 1, own] * x
        for j in (1, 2):
            total = total + taps[j, p : p + 1, own] * pltpu.roll(x, j, 0)
        return total[16:].astype(bf16).T

    def start_out(step, group):
        peer = peer_of(*step)
        start(("out", step, group), rows_of(out, peer, group), positions_of(arr, me, group), step)

    for s in (1, 3, 2, 0):
        chunk = lax.rem(y + s, 4)
        rows = pl.ds(pl.multiple_of(chunk * 128, 128), 128)
        query, key, value = (filtered(p, chunk) for p in range(3))
        for group in range(2):
            compact = pl.ds(pl.multiple_of(chunk * 64, 16), 64)
            for dst, src in ((keys, key), (values, value)):
                pieces = [src[i * 32 + group * 16 : i * 32 + group * 16 + 16] for i in range(4)]
                dst[group, compact, :] = jnp.concatenate(pieces, axis=0)
        out[0, rows, :] = (key.astype(f32) * value.astype(f32)).astype(bf16)
        out[1, rows, :] = (cotangent[rows, :].astype(f32) * query.astype(f32)).astype(bf16)
        for step in steps:
            if step[0] == s:
                start_out(step, 0)
    kept = []
    for group in range(2):
        copy = pltpu.make_async_copy(
            rows_of(out, me, group), positions_of(arr, me, group), load.at[11 + group]
        )
        copy.start()
        kept.append(copy)

    def dot(a, b):
        return jnp.dot(a, b, preferred_element_type=f32)

    def channel(index):
        return pl.ds(index, BLOCKS, stride=32)

    def block(n):
        return slice(n * LANES, (n + 1) * LANES)

    for n in range(BLOCKS):
        held[2, n * 32 : (n + 1) * 32, :] = filters[:, block(n)]

    def filter_spectra(step, carry):
        signals = [held[2, channel(step * 8 + j), :].astype(bf16) for j in range(8)]
        mixed = dot(first[...], jnp.concatenate(signals, axis=1))
        rows = pl.ds(pl.multiple_of(step * 512, 512), 512)
        acc[rows, :] = dot(turned(mixed, 8, turn[0], turn[1]), second[...])
        return carry

    lax.fori_loop(0, 4, filter_spectra, 0)
    for step in steps:
        start_out(step, 1)

    def both_ways(start_at, step, carry):
        index = start_at + step * 4
        signals = [held[s, channel(index + j), :].astype(bf16) for j in range(4) for s in range(2)]
        mixed = dot(first[...], jnp.concatenate(signals, axis=1))
        spectra = dot(turned(mixed, 8, turn[0], turn[1]), second[...])
        rows = pl.ds(pl.multiple_of(index * 64, 256), 256)
        filt = acc[rows, :]
        joined, kept = [], []
        for j in range(4):
            parts = []
            for value in (
                spectra[j * 128 : j * 128 + 64],
                spectra[j * 128 + 64 : j * 128 + 128],
                filt[j * 64 : j * 64 + 64],
            ):
                parts.append((value[:, :LANES], value[:, LANES:]))
            (pr, pi), (wr, wi), (hr, hi) = parts
            joined.append(jnp.concatenate([pr * hr - pi * hi, pr * hi + pi * hr], axis=1))
            joined.append(jnp.concatenate([hr * wr + hi * wi, hr * wi - hi * wr], axis=1))
            kept.append(jnp.concatenate([pr * wr + pi * wi, pr * wi - pi * wr], axis=1))
        fgs[rows, :] = jnp.concatenate(kept, axis=0).astype(bf16)
        back = dot(jnp.concatenate(joined, axis=0).astype(bf16), second_back[...])
        final = dot(first_back[...], unturned(back, 8, turn[0], turn[1]))
        for j in range(4):
            for s in range(2):
                held[s, channel(index + j), :] = final[:, block(2 * j + s)]
        return carry

    def compact_of(group):
        return ret.at[group, :, pl.ds(pl.multiple_of(me * 16, 16), 16), :]

    for group in range(2):
        arrived(*(("out", step, group) for step in steps))
        kept[group].wait()
        own = slice(group * 16, group * 16 + 16)
        for n in range(BLOCKS):
            for s in range(2):
                rows = slice(n * 32 + group * 16, n * 32 + group * 16 + 16)
                held[s, rows, :] = arr[s, own, block(n)].astype(f32)
        lax.fori_loop(0, 4, functools.partial(both_ways, group * 16), 0)
        gain = gains[own, :]
        for n in range(BLOCKS):
            for s in range(2):
                rows = slice(n * 32 + group * 16, n * 32 + group * 16 + 16)
                direct = gain * arr[s, own, block(n)].astype(f32)
                arr[s, own, block(n)] = (held[s, rows, :] + direct).astype(bf16)
        for step in steps:
            src = positions_of(arr, peer_of(*step), group)
            start(("back", step, group), src, compact_of(group), step)
        copy = pltpu.make_async_copy(
            positions_of(arr, me, group), compact_of(group), load.at[13 + group]
        )
        copy.start()
        kept.append(copy)

    def filter_grads(step, carry):
        rows = pl.ds(pl.multiple_of(step * 512, 512), 512)
        back = dot(fgs[rows, :], second_back[...])
        final = dot(first_back[...], unturned(back, 8, turn[0], turn[1]))
        for j in range(8):
            held[2, channel(step * 8 + j), :] = final[:, block(j)]
        return carry

    def stream_grads(group, chunk, carry):
        rows = pl.ds(pl.multiple_of(chunk * 128, 128), 128)
        one, two = ret[group, 0, rows, :].astype(f32), ret[group, 1, rows, :].astype(f32)
        owners = [
            cotangent[pl.ds(pl.multiple_of((chunk * 8 + i) * 32 + group * 16, 16), 16), :]
            for i in range(8)
        ]
        factors = (
            (one, jnp.concatenate(owners, axis=0)),
            (two, values[group, rows, :]),
            (two, keys[group, rows, :]),
        )
        for p, (value, factor) in enumerate(factors):
            grads = (value * factor.astype(f32)).astype(bf16)
            cgx[group * 3 + p, rows, 0:512] = grads
            columns = pl.ds(pl.multiple_of(p * 256 + chunk * 128, 128), 128)
            hout[group, :, columns] = grads[:, 0:128].T[0:16, :]
        return carry

    def tapped(group, p, rows, first, width, kept):
        x = cgx[group * 3 + p, rows, first : first + width].astype(f32)
        total = coltaps[group, rows, p : p + 1] * x
        for j in (1, 2):
            tap = coltaps[group, rows, 3 * j + p : 3 * j + p + 1]
            total = total + tap * pltpu.roll(x, width - j, 1)
        return total[:, :kept].astype(bf16)

    def grad_rows(group, p, chunk):
        return pl.ds(pl.multiple_of(group * 768 + p * 256 + chunk * 128, 128), 128)

    def front(group, chunk, carry):
        rows = pl.ds(pl.multiple_of(chunk * 128, 128), 128)
        for p in range(3):
            pgc[grad_rows(group, p, chunk), 0:384] = tapped(group, p, rows, 0, 512, 384)
        return carry

    def rest(group, chunk, carry):
        rows = pl.ds(pl.multiple_of(chunk * 128, 128), 128)
        for p in range(3):
            columns = pl.ds(pl.multiple_of(p * 256 + chunk * 128, 128), 128)
            edge = hin[group, :, columns].astype(f32)
            edge = jnp.where(me == N_CTX - 1, jnp.zeros_like(edge), edge)
            edge = jnp.concatenate([edge, jnp.zeros((112, 128), f32)], axis=0)
            cgx[group * 3 + p, rows, 512:640] = edge.T.astype(bf16)
            pgc[grad_rows(group, p, chunk), 384:512] = tapped(group, p, rows, 384, 256, 128)
        return carry

    def swap(group, part, first, count):
        places = (pl.ds(group * 768, 768), pl.ds(first, count))
        start(("grads", group, part), pgc.at[places], pgo.at[places], "twin")

    def begin_grads(group):
        arrived(*(("back", step, group) for step in steps))
        kept[2 + group].wait()
        lax.fori_loop(0, 2, functools.partial(stream_grads, group), 0)
        start(("halo", group), hout.at[group], hin.at[group], "last")

    def most_grads(group):
        lax.fori_loop(0, 2, functools.partial(front, group), 0)
        swap(group, 0, 0, 384)

    def last_grads(group):
        arrived(("halo", group))
        lax.fori_loop(0, 2, functools.partial(rest, group), 0)
        swap(group, 1, 384, 128)

    def whole_filter_grads():
        lax.fori_loop(0, 4, filter_grads, 0)
        for n in range(BLOCKS):
            grad[:, block(n)] = held[2, n * 32 : (n + 1) * 32, :]

    def by_position(chunk, carry):
        for p in range(3):
            pieces = []
            for i in range(4):
                for group in range(2):
                    first = group * 768 + p * 256 + chunk * 64 + i * 16
                    pieces.append(pgc[pl.ds(pl.multiple_of(first, 16), 16), :])
            columns = pl.ds(pl.multiple_of(p * 512 + chunk * 128, 128), 128)
            pgt[:, columns] = jnp.concatenate(pieces, axis=0).T
        return carry

    def input_tiles(first):
        def tile(step, carry):
            rows = pl.ds(pl.multiple_of((first + step) * 512, 512), 512)
            ig[:, rows] = lax.dot_general(
                pgt[...],
                wall[pl.ds((first + step) * 2, 2)].reshape(512, 1536),
                (((1,), (1,)), ((), ())),
                preferred_element_type=f32,
            ).astype(bf16)
            return carry

        lax.fori_loop(0, 4, tile, 0)

    def acc_rows(slot, row, count):
        return pl.ds(pl.multiple_of(slot * 768 + row, 16), count)

    def weight_part(slot, group, block, own=True, theirs=True):
        mine = pl.ds(pl.multiple_of((2 * block + core) * 256, 256), 256)
        columns = pl.ds(pl.multiple_of(block * 256, 256), 256)
        rows, kept = slice(group * 768, group * 768 + 768), acc_rows(slot, 0, 768)
        value = dot(pgc[rows, :], tok[16:528, mine]) if own else acc[kept, :]
        if theirs:
            value = value + dot(pgo[rows, :], oth[:, columns])
        acc[kept, :] = value

    def fold(dst, slot, first, last, *terms):
        def chunk(step, carry):
            rows = pl.ds(pl.multiple_of(step * 128, 128), 128)
            total = acc[acc_rows(slot, step * 128, 128), :]
            for term, offset in terms:
                part_rows = pl.ds(pl.multiple_of(step * 128 - offset, 128), 128)
                total = total + term[part_rows, :].astype(f32)
            dst[rows, :] = total.astype(bf16)
            return carry

        lax.fori_loop(first // 128, last // 128, chunk, 0)

    def block_of(y, xh):
        return y * 2 + xh

    y2, yp, ym = lax.rem(y + 2, 4), lax.rem(y + 1, 4), lax.rem(y + 3, 4)
    ztwo, zp, zm = lax.rem(z + 2, 4), lax.rem(z + 1, 4), lax.rem(z + 3, 4)
    xo = 1 - xh
    sides = (1 - xl, xl)
    low, high = pl.ds(0, 384), pl.ds(384, 384)
    parts = (slice(0, 2048), slice(2048, 4096))

    def ig_rows(side, z, first, count):
        return pl.ds(pl.multiple_of((side * 4 + z) * 64 + first, 32), count)

    def ig_add(rows, h, *terms):
        total = ig[rows, parts[h]].astype(f32)
        for term in terms:
            total = total + term[...].astype(f32)
        return total.astype(bf16)

    def z_first(h):
        for k in range(2):
            src = ig.at[ig_rows(sides[k], ztwo, 0, 32), parts[h]]
            start(("z2p", h, k), src, z2.at[h, k, 0], "above")
            src = ig.at[ig_rows(sides[k], ztwo, 32, 32), parts[h]]
            start(("z2m", h, k), src, z2.at[h, k, 1], "below")

    def z_second(h, k):
        arrived(("z2p", h, k))
        rows = ig_rows(sides[k], zp, 0, 32)
        ig[rows, parts[h]] = ig_add(rows, h, z2.at[h, k, 0])
        src = ig.at[ig_rows(sides[k], zp, 0, 64), parts[h]]
        start(("zfp", h, k), src, zf.at[h, k, 0], "above")
        arrived(("z2m", h, k))
        rows = ig_rows(sides[k], zm, 32, 32)
        ig[rows, parts[h]] = ig_add(rows, h, z2.at[h, k, 1])
        src = ig.at[ig_rows(sides[k], zm, 0, 64), parts[h]]
        start(("zfm", h, k), src, zf.at[h, k, 1], "below")

    def z_across(h):
        arrived(("zfp", h, 0), ("zfm", h, 0))
        rows = ig_rows(sides[0], z, 0, 64)
        ig[rows, parts[h]] = ig_add(rows, h, zf.at[h, 0, 0], zf.at[h, 0, 1])
        start(("xz", h), ig.at[rows, parts[h]], xz.at[h], "near")

    def z_last(h):
        arrived(("zfp", h, 1), ("zfm", h, 1), ("xz", h))
        rows = ig_rows(sides[1], z, 0, 64)
        ig_out[:, parts[h]] = ig_add(rows, h, zf.at[h, 1, 0], zf.at[h, 1, 1], xz.at[h])

    early = ((yp, xo), (ym, xo), (y2, xo))

    def own_halves(group):
        for n, place in enumerate(early):
            weight_part(3 * group + n, group, block_of(*place), theirs=False)

    def first_blocks(group):
        arrived(("grads", group, 0), ("grads", group, 1))
        for n, place in enumerate(early):
            slot = 3 * group + n
            weight_part(slot, group, block_of(*place), own=False)
            fold(part.at[group, n], slot, 0, 768)
            dst = (rf.at[group, 0, 0], rf.at[group, 0, 1], xin.at[group])[n]
            peer = ("up", "down", "across")[n]
            start((peer, 0, group), part.at[group, n], dst, peer)

    def second_blocks(group):
        weight_part(0, group, block_of(y2, xh))
        arrived(("across", 0, group))
        fold(part.at[group, 3], 0, 0, 768, (xin.at[group], 0))
        start(("up", 2, group), part.at[group, 3, low], r2.at[group, 0], "up")
        start(("down", 2, group), part.at[group, 3, high], r2.at[group, 1], "down")

    def free_halves(group):
        weight_part(2 * group, group, block_of(yp, xh))
        fold(part.at[group, 4], 2 * group, 384, 768)
        start(("upb", 1, group), part.at[group, 4, high], rf.at[group, 1, 0, high], "up")
        weight_part(2 * group + 1, group, block_of(ym, xh))
        fold(part.at[group, 5], 2 * group + 1, 0, 384)
        start(("downa", 1, group), part.at[group, 5, low], rf.at[group, 1, 1, low], "down")

    def side_blocks(group):
        weight_part(4, group, block_of(y, xo))
        arrived(("up", 0, group), ("down", 0, group))
        sent[("across", 0, group)].wait_send()
        terms = ((rf.at[group, 0, 0], 0), (rf.at[group, 0, 1], 0))
        fold(part.at[group, 2], 4, 0, 768, *terms)
        start(("across", 1, group), part.at[group, 2], xr.at[group], "across")

    def bound_halves(group):
        arrived(("up", 2, group))
        fold(part.at[group, 4], 2 * group, 0, 384, (r2.at[group, 0], 0))
        start(("upa", 1, group), part.at[group, 4, low], rf.at[group, 1, 0, low], "up")
        arrived(("down", 2, group))
        fold(part.at[group, 5], 2 * group + 1, 384, 768, (r2.at[group, 1], 384))
        start(("downb", 1, group), part.at[group, 5, high], rf.at[group, 1, 1, high], "down")

    def own_blocks(group):
        names = (("across", 1), ("upa", 1), ("upb", 1), ("downa", 1), ("downb", 1))
        arrived(*((*name, group) for name in names))

        def chunk(step, carry):
            rows = pl.ds(pl.multiple_of(step * 128, 128), 128)
            place = acc_rows(4 + group, step * 128, 128)
            total = acc[place, :]
            for term in (rf.at[group, 1, 0], rf.at[group, 1, 1], xr.at[group]):
                total = total + term[rows, :].astype(f32)
            acc[place, :] = total
            return carry

        lax.fori_loop(0, 6, chunk, 0)

    def last_fold(step, carry):
        p, chunk = step // 4, lax.rem(step, 4)
        pieces = []
        for i in range(4):
            for group in range(2):
                pieces.append(acc[acc_rows(4 + group, p * 256 + chunk * 64 + i * 16, 16), :])
        columns = pl.ds(pl.multiple_of(chunk * 128, 128), 128)
        wg_out[p, :, columns] = jnp.concatenate(pieces, axis=0).T.astype(bf16)
        return carry

    begin_grads(0)
    most_grads(0)
    whole_filter_grads()
    last_grads(0)
    own_halves(0)
    begin_grads(1)
    first_blocks(0)
    most_grads(1)
    last_grads(1)
    lax.fori_loop(0, 4, by_position, 0)
    input_tiles(0)
    z_first(0)
    own_halves(1)
    first_blocks(1)
    second_blocks(0)
    input_tiles(4)
    z_first(1)
    z_second(0, 0)
    side_blocks(0)
    second_blocks(1)
    z_second(1, 0)
    free_halves(0)
    z_second(0, 1)
    free_halves(1)
    side_blocks(1)
    bound_halves(0)
    z_second(1, 1)
    z_across(0)
    bound_halves(1)
    z_across(1)
    for group in range(2):
        weight_part(4 + group, group, block_of(y, xh))
    own_blocks(0)
    z_last(0)
    z_last(1)
    own_blocks(1)
    lax.fori_loop(0, 12, last_fold, 0)
    for name, copy in sent.items():
        if name[:2] != ("across", 0):
            copy.wait_send()


def mixer(tokens, weight, out_grad, short_taps, long_filter, skip_bias):
    bf16, f32 = jnp.bfloat16, jnp.float32
    vmem = lambda *shape: pltpu.VMEM(shape, bf16)
    wide = lambda *shape: pltpu.VMEM(shape, f32)
    return pl.pallas_call(
        mixer_kernel,
        out_shape=(
            jax.ShapeDtypeStruct((64, 4096), bf16),
            jax.ShapeDtypeStruct((3, 256, 512), bf16),
            jax.ShapeDtypeStruct((32, BLOCKS * LANES), f32),
        ),
        in_specs=[ANY] * 11,
        out_specs=(IN_VMEM,) * 3,
        scratch_shapes=[
            vmem(528, 4096),
            vmem(512, 2048),
            vmem(N_CTX, 256, 1536),
            vmem(512, 512),
            wide(3, 3, 512),
            wide(2, 256, 16),
            wide(32, BLOCKS * LANES),
            wide(1, 32),
            wide(32, LANES),
            vmem(128, 64),
            vmem(256, 256),
            vmem(256, 256),
            vmem(64, 128),
            wide(2, 64, LANES),
            vmem(2, 256, 512),
            vmem(2, 256, 512),
            vmem(2, 512, 512),
            vmem(2, 32, BLOCKS * LANES),
            wide(3, 32 * BLOCKS, LANES),
            vmem(32 * BLOCKS, 2 * LANES),
            vmem(2, 2, 256, 512),
            vmem(6, 256, 640),
            vmem(2, 16, 768),
            vmem(2, 16, 768),
            vmem(1536, 512),
            vmem(512, 1536),
            vmem(1536, 512),
            vmem(512, 4096),
            wide(4608, 256),
            vmem(2, 6, 768, 256),
            vmem(2, 768, 256),
            vmem(2, 2, 384, 256),
            vmem(2, 2, 2, 768, 256),
            vmem(2, 768, 256),
            vmem(2, 2, 2, 32, 2048),
            vmem(2, 2, 2, 64, 2048),
            vmem(2, 64, 2048),
            pltpu.SemaphoreType.DMA((136,)),
            pltpu.SemaphoreType.DMA((136,)),
            pltpu.SemaphoreType.DMA((18,)),
        ],
        compiler_params=pltpu.CompilerParams(
            collective_id=1, has_side_effects=True, vmem_limit_bytes=63 * 1024 * 1024
        ),
    )(
        tokens, weight, out_grad, short_taps, long_filter, skip_bias.reshape(1, 32), *tables()
    )


def pieces_of(shapes):
    cuts = []
    for index, shape in enumerate(shapes):
        size = max(1, shape[0] // 4)
        cuts += [(index, pl.ds(first, size)) for first in range(0, shape[0], size)]
    return cuts


def hand_out_kernel(*refs):
    count = (len(refs) - 1) // 3
    given, results, held, sem = refs[:count], refs[count : 2 * count], refs[2 * count : -1], refs[-1]
    inward, outward = [], []
    for place, (n, rows) in enumerate(pieces_of([ref.shape for ref in given])):
        first, second = sem.at[0, place], sem.at[1, place]
        inward.append(pltpu.make_async_copy(given[n].at[rows], held[n].at[rows], first))
        outward.append(pltpu.make_async_copy(held[n].at[rows], results[n].at[rows], second))
    for copy in inward:
        copy.start()
    for first, then in zip(inward, outward):
        first.wait()
        then.start()
    for copy in outward:
        copy.wait()


def hand_out(results):
    count = len(results)
    return pl.pallas_call(
        hand_out_kernel,
        out_shape=[jax.ShapeDtypeStruct(value.shape, value.dtype) for value in results],
        in_specs=[ANY] * count,
        out_specs=[ANY] * count,
        scratch_shapes=[pltpu.VMEM(value.shape, value.dtype) for value in results]
        + [pltpu.SemaphoreType.DMA((2, len(pieces_of([value.shape for value in results]))))],
        compiler_params=pltpu.CompilerParams(vmem_limit_bytes=63 * 1024 * 1024),
    )(*results)


def on_device(tokens, in_weight, short_taps, long_filter, skip_bias, out_grad):
    weight = jnp.transpose(in_weight, (1, 0, 2))
    results = mixer(tokens, weight, out_grad, short_taps, long_filter, skip_bias)
    input_grad, weight_grad, filter_grad = hand_out(results)
    return input_grad, jnp.transpose(weight_grad, (1, 0, 2)), filter_grad


def solution(mesh):
    in_specs = (
        P("ctx", None),
        P("ctx", None, "tp"),
        P(None, None, "tp"),
        P(("tp", "ctx"), None),
        P(("tp", "ctx")),
        P("tp", "ctx"),
    )
    out_specs = (P(("ctx", "tp"), None), P("ctx", None, "tp"), P(("tp", "ctx"), None))
    return jax.shard_map(
        on_device, mesh=mesh, in_specs=in_specs, out_specs=out_specs, check_vma=False
    )
```
